32 devices in a mesh: band: 4 (over y, x), base: 8 (over z, core).
Axes of the slice: x: 2, y: 2, z: 4, core: 2. Of those that a mesh axis runs over, the one named last changes fastest.
Arguments:
- visibilities: bfloat16 [8, 16, 256, 256], P(None, 'base', 'band'), may hold values from -6 to 6
- model: bfloat16 [8, 16, 256, 256], P(None, 'base', 'band'), may hold values from -6 to 6
- start_gains: float32 [8, 128, 512], P(None, 'band', 'base'), may hold values from -1.5 to 2.5
- penalty: float32 [512], P('base'), may hold values from 0.5 to 5
- pairs: int32 [16, 2], P('base'), may hold values from 0 to 31, as said below
- flags: int32 [16, 256], P('base'), may hold values 0 or 1
- chan_band: int32 [256], P('band'), may hold values from 0 to 127, as said below
Outputs:
- gains: float32 [8, 128, 512], P(None, 'band', 'base')
- coefficients: float32 [8, 9, 512], P(None, None, 'base')
The draws below stay inside these ranges and needn't reach their ends.
Inputs may be any that keep to these rules, and one draw needn't show every extreme that they name: `pairs`: each tile joins blocks a <= b, and no two tiles join the same pair of blocks. `chan_band`: the 64 channels of the k-th block of 64 channels map, never falling, onto the intervals k * 32 to k * 32 + 31, each interval holding one channel or more.
All inputs are finite; a program needn't handle non-finite values. No bound on the sum of `flags` on one device may be relied on, other than what follows from the above.
Results may differ from the reference program's by a relative error of at most 0.0003.
Values sent between devices are 32-bit elements; how exact they have to be, the bound alone decides.
No kernel may reach another device: no remote copies, remote signals or barrier semaphores. Data moves between devices by JAX's collectives and lax.ppermute only.
A program may use at most 128 MiB of HBM per device.

```python
import math
import jax
import jax.numpy as jnp
from jax import lax

NST = 512
BLOCK = 16
NBLK = 32
NPOLY = 9
TILES = 16
CH_DEV = 64
NCHAN = 256
SOL_DEV = 32
SOL = 128
ITERS = 3


def draw_start_gains(key, part):
    key = jax.random.fold_in(key, 5)
    noise = 0.3 * jnp.clip(jax.random.normal(key, (8, SOL, NST), jnp.float32), -4.0, 4.0)
    ident = jnp.zeros((8, 1, 1), jnp.float32).at[0].set(1.0).at[3].set(1.0)
    return noise + ident


def draw_pairs(key, part):
    key = jax.random.fold_in(key, 7)
    lower_ids, upper_ids = jnp.triu_indices(NBLK)
    total = lower_ids.shape[0]
    planted = NBLK - 1
    scores = jax.random.permutation(key, total).astype(jnp.int32)
    scores = jnp.where(jnp.arange(total, dtype=jnp.int32) == planted, -1, scores)
    chosen = jnp.argsort(scores, stable=True)[:TILES]
    return jnp.stack([lower_ids[chosen], upper_ids[chosen]], 1).astype(jnp.int32)


def draw_chan_band(key, part):
    key = jax.random.fold_in(key, 11)
    groups = NCHAN // CH_DEV

    def one_group(index):
        cuts = jax.random.permutation(jax.random.fold_in(key, index), CH_DEV - 1)[:SOL_DEV - 1] + 1
        places = jnp.arange(CH_DEV, dtype=jnp.int32)
        local = jnp.sum((places[:, None] >= cuts[None, :]).astype(jnp.int32), 1)
        return local + index * SOL_DEV
    return jax.vmap(one_group)(jnp.arange(groups, dtype=jnp.int32)).reshape(-1).astype(jnp.int32)


def set_ends(entries, stream_key, low, largest):
    longest = entries.shape.index(max(entries.shape))
    spots = []
    for shift in (0, 1):
        where = [jax.random.randint(jax.random.fold_in(stream_key, axis), (), 0, length) for axis, length in enumerate(entries.shape)]
        where[longest] = (where[longest] + shift) % entries.shape[longest]
        spots.append(tuple(where))
    return entries.at[spots[0]].set(low).at[spots[1]].set(largest)


def levels(rng, dims, pieces, low, high):
    def one(axis_at, shards_of):
        draws = jax.random.uniform(jax.random.fold_in(jax.random.fold_in(rng, 6), axis_at), (shards_of,), jnp.float32, low / len(pieces), high / len(pieces))
        return jnp.repeat(jnp.exp(draws), dims[axis_at] // shards_of).reshape((-1,) + (1,) * (len(dims) - axis_at - 1))

    level = one(*pieces[0])
    for cut in pieces[1:]:
        level = level * one(*cut)
    return level


def centred(key, extent, scale, most, pieces=(), held_as=jnp.bfloat16):
    values = jax.random.normal(key, extent, jnp.float32) * scale
    if len(pieces) > 0:
        values = levels(key, extent, pieces, -0.22, 0.18) * values
    return jnp.clip(values, min=-most, max=most).astype(held_as)


def setup_inputs(seed: int = 0) -> dict:
    key_of = jax.random.split(jax.random.key(seed), 8)
    return {
        "visibilities": centred(key_of[0], (8, TILES, NCHAN, BLOCK * BLOCK), 1.0, 6.0, ((1, 8), (2, 4))),
        "model": centred(key_of[1], (8, TILES, NCHAN, BLOCK * BLOCK), 1.0, 6.0, ((1, 8), (2, 4))),
        "start_gains": draw_start_gains(jax.random.fold_in(key_of[7], 71), 0),
        "penalty": jnp.clip(jnp.exp(math.log(5.0) - 2.3025851 * jax.random.uniform(key_of[3], (NST,), jnp.float32) ** levels(key_of[3], (NST,), ((0, 8),), -0.2, 0.2)), 0.5, 5.0),
        "pairs": draw_pairs(jax.random.fold_in(key_of[7], 71), 0),
        "flags": set_ends((jax.random.randint(key_of[5], (TILES, BLOCK * BLOCK), 0, 8) < 7).astype(jnp.int32), jax.random.fold_in(key_of[5], 1), 0, 1),
        "chan_band": draw_chan_band(jax.random.fold_in(key_of[7], 71), 0),
    }


ridge = 0.5

def cmul(left, right):

    def product(upper, lower):
        return jnp.stack([jnp.stack([upper[row_at, 0] * lower[0, col_at] + upper[row_at, 1] * lower[1, col_at] for col_at in range(2)]) for row_at in range(2)])
    return jnp.stack([product(left[0], right[0]) - product(left[1], right[1]), product(left[0], right[1]) + product(left[1], right[0])])

def cherm(matrix):
    return jnp.stack([jnp.swapaxes(matrix[0], 0, 1), -jnp.swapaxes(matrix[1], 0, 1)])

def pack_terms(gain_part, outer_part):
    flat = gain_part.reshape((8,) + gain_part.shape[3:])
    hermit = jnp.stack([outer_part[0, 0, 0], outer_part[0, 1, 1], outer_part[0, 0, 1], outer_part[1, 0, 1]])
    return jnp.concatenate([flat, hermit], 0)

def tile_terms(vis, mdl, first, second, weight):
    along = cmul(mdl, cherm(second))
    gain_first = jnp.sum(weight * cmul(vis, cherm(along)), -1)
    outer_first = jnp.sum(weight * cmul(along, cherm(along)), -1)
    back = cmul(first, mdl)
    gain_second = jnp.sum(weight * cmul(cherm(vis), back), -2)
    outer_second = jnp.sum(weight * cmul(cherm(back), back), -2)
    return (pack_terms(gain_first, outer_first), pack_terms(gain_second, outer_second))

def solve_gains(normal, counts, consensus, dual, penalty):
    scale = 1.0 / jnp.maximum(counts, 1.0)
    rhs = normal[:8] * scale + penalty * (consensus - dual)
    h_first = normal[8] * scale + penalty
    h_second = normal[9] * scale + penalty
    h_real = normal[10] * scale
    h_imag = normal[11] * scale
    determ = h_first * h_second - h_real * h_real - h_imag * h_imag
    zeros = jnp.zeros_like(determ)
    inv_re = jnp.stack([jnp.stack([h_second, -h_real]), jnp.stack([-h_real, h_first])]) / determ
    inv_im = jnp.stack([jnp.stack([zeros, -h_imag]), jnp.stack([h_imag, zeros])]) / determ
    solved = cmul(rhs.reshape((2, 2, 2) + rhs.shape[1:]), jnp.stack([inv_re, inv_im]))
    return solved.reshape(rhs.shape)

def chebyshev(centre):
    terms = [jnp.ones_like(centre), centre]
    for order in range(2, NPOLY):
        terms.append(2.0 * centre * terms[-1] - terms[-2])
    return jnp.stack(terms[:NPOLY], 1)

def reference(visibilities, model, start_gains, penalty, pairs, flags, chan_band):
    high = lax.Precision.HIGHEST
    onehot = (chan_band[:, None] == jnp.arange(SOL, dtype=jnp.int32)[None, :]).astype(jnp.float32)
    chans = jnp.sum(onehot, 0)
    xpos = -1.0 + (2.0 * jnp.arange(NCHAN, dtype=jnp.float32) + 1.0) / NCHAN
    centre = jnp.sum(onehot * xpos[:, None], 0) / chans
    basis = chebyshev(centre)
    gram = jnp.dot(basis.T, basis, precision=high) + ridge * jnp.eye(NPOLY, dtype=jnp.float32)
    factor = jnp.linalg.cholesky(gram)
    same = (pairs[:, 0] == pairs[:, 1]).astype(jnp.float32)
    weights = flags.reshape(TILES, BLOCK, BLOCK).astype(jnp.float32) * (1.0 - same[:, None, None] * jnp.eye(BLOCK, dtype=jnp.float32))
    inside = jnp.arange(BLOCK, dtype=jnp.int32)
    station_w = jnp.zeros((NST,), jnp.float32)
    station_w = station_w.at[(pairs[:, 0:1] * BLOCK + inside[None, :]).reshape(-1)].add(jnp.sum(weights, 2).reshape(-1))
    station_w = station_w.at[(pairs[:, 1:2] * BLOCK + inside[None, :]).reshape(-1)].add(jnp.sum(weights, 1).reshape(-1))
    counts = chans[:, None] * station_w[None, :]
    gains = start_gains
    consensus = start_gains
    dual = jnp.zeros_like(start_gains)
    coeff = jnp.zeros((NPOLY, 8, NST), jnp.float32)
    for step in range(ITERS):

        def per_tile(index, total):
            vis = lax.dynamic_index_in_dim(visibilities, index, 1, keepdims=False).astype(jnp.float32).reshape(2, 2, 2, NCHAN, BLOCK, BLOCK)
            mdl = lax.dynamic_index_in_dim(model, index, 1, keepdims=False).astype(jnp.float32).reshape(2, 2, 2, NCHAN, BLOCK, BLOCK)
            start_a = (pairs[index, 0] * BLOCK).astype(jnp.int32)
            start_b = (pairs[index, 1] * BLOCK).astype(jnp.int32)
            first = jnp.einsum('ksi,cs->kci', lax.dynamic_slice_in_dim(gains, start_a, BLOCK, 2), onehot, precision=high)
            second = jnp.einsum('ksi,cs->kci', lax.dynamic_slice_in_dim(gains, start_b, BLOCK, 2), onehot, precision=high)
            terms_a, terms_b = tile_terms(vis, mdl, first.reshape(2, 2, 2, NCHAN, BLOCK, 1), second.reshape(2, 2, 2, NCHAN, 1, BLOCK), weights[index])
            sum_a = jnp.einsum('kci,cs->ksi', terms_a, onehot, precision=high)
            sum_b = jnp.einsum('kci,cs->ksi', terms_b, onehot, precision=high)
            total = lax.dynamic_update_slice_in_dim(total, lax.dynamic_slice_in_dim(total, start_a, BLOCK, 2) + sum_a, start_a, 2)
            total = lax.dynamic_update_slice_in_dim(total, lax.dynamic_slice_in_dim(total, start_b, BLOCK, 2) + sum_b, start_b, 2)
            return total
        normal = lax.fori_loop(0, TILES, per_tile, jnp.zeros((12, SOL, NST), jnp.float32))
        gains = solve_gains(normal, counts, consensus, dual, penalty)
        total = jnp.einsum('sk,msn->kmn', basis, gains + dual, precision=high)
        coeff = jax.scipy.linalg.cho_solve((factor, True), total.reshape(NPOLY, -1)).reshape(NPOLY, 8, NST)
        consensus = jnp.einsum('sk,kmn->msn', basis, coeff, precision=high)
        dual = dual + gains - consensus
    return (gains, jnp.transpose(coeff, (1, 0, 2)))
```

```python
import functools

import jax
import jax.numpy as jnp
from jax import lax
from jax.experimental import pallas as pl
from jax.experimental.pallas import tpu as pltpu
from jax.sharding import PartitionSpec as P

BLOCK = 16
NPOLY = 9
KPAD = 16
ITERS = 3
LANES = 128
F32 = jnp.float32
BF16 = jnp.bfloat16
HIGH = lax.Precision.HIGHEST

ridge = 0.5

GAIN_ROWS = 8 * BLOCK
TERM_ROWS = 12 * BLOCK


def nt(left, right, **kw):
    return lax.dot_general(
        left, right, (((1,), (1,)), ((), ())), preferred_element_type=F32, **kw
    )


def nn(left, right, **kw):
    return lax.dot_general(
        left, right, (((1,), (0,)), ((), ())), preferred_element_type=F32, **kw
    )


def pick(values, select, dot=nt):
    high = values.astype(BF16)
    low = (values - high.astype(F32)).astype(BF16)
    rows = values.shape[0]
    out = dot(jnp.concatenate([high, low], 0), select)
    return out[:rows] + out[rows:]


def iota(shape, axis):
    return lax.broadcasted_iota(jnp.int32, shape, axis)


def mul(a, b):
    re, im = [], []
    for r in range(2):
        for c in range(2):
            re.append(
                (a[2 * r] * b[c] + a[2 * r + 1] * b[2 + c])
                - (a[4 + 2 * r] * b[4 + c] + a[5 + 2 * r] * b[6 + c])
            )
            im.append(
                (a[2 * r] * b[4 + c] + a[2 * r + 1] * b[6 + c])
                + (a[4 + 2 * r] * b[c] + a[5 + 2 * r] * b[2 + c])
            )
    return re + im


def mul_herm(a, b):
    re, im = [], []
    for r in range(2):
        for c in range(2):
            re.append(
                (a[2 * r] * b[2 * c] + a[2 * r + 1] * b[2 * c + 1])
                + (a[4 + 2 * r] * b[4 + 2 * c] + a[5 + 2 * r] * b[5 + 2 * c])
            )
            im.append(
                (a[4 + 2 * r] * b[2 * c] + a[5 + 2 * r] * b[2 * c + 1])
                - (a[2 * r] * b[4 + 2 * c] + a[2 * r + 1] * b[5 + 2 * c])
            )
    return re + im


def herm_mul(a, b):
    re, im = [], []
    for r in range(2):
        for c in range(2):
            re.append(
                (a[r] * b[c] + a[2 + r] * b[2 + c]) + (a[4 + r] * b[4 + c] + a[6 + r] * b[6 + c])
            )
            im.append(
                (a[r] * b[4 + c] + a[2 + r] * b[6 + c]) - (a[4 + r] * b[c] + a[6 + r] * b[2 + c])
            )
    return re + im


def outer_rows(c):
    return [
        (c[0] * c[0] + c[1] * c[1]) + (c[4] * c[4] + c[5] * c[5]),
        (c[2] * c[2] + c[3] * c[3]) + (c[6] * c[6] + c[7] * c[7]),
        (c[0] * c[2] + c[1] * c[3]) + (c[4] * c[6] + c[5] * c[7]),
        (c[4] * c[2] + c[5] * c[3]) - (c[0] * c[6] + c[1] * c[7]),
    ]


def outer_columns(d):
    return [
        (d[0] * d[0] + d[2] * d[2]) + (d[4] * d[4] + d[6] * d[6]),
        (d[1] * d[1] + d[3] * d[3]) + (d[5] * d[5] + d[7] * d[7]),
        (d[0] * d[1] + d[2] * d[3]) + (d[4] * d[5] + d[6] * d[7]),
        (d[0] * d[5] + d[2] * d[7]) - (d[4] * d[1] + d[6] * d[3]),
    ]


def slot_key(index, pairs, scale, intervals):
    at = index // intervals
    tiles = len(pairs)
    block = jnp.zeros(index.shape, F32)
    for slot in range(2 * tiles):
        value = pairs[slot % tiles][slot // tiles]
        block = jnp.where(at == slot, value.astype(F32), block)
    if scale > 1:
        block = block * scale + (index % intervals).astype(F32)
    return block


def scalar_pairs(pair_ref):
    return [[pair_ref[t, side] for side in range(2)] for t in range(pair_ref.shape[0])]


def owner_key(index, me, blocks, intervals, none, scale=None):
    at = index // intervals
    key = me * blocks + at
    if scale != 1:
        key = key * intervals + index % intervals
    return jnp.where(at < blocks, key, none).astype(F32)


def cell_weights(pairs, flags):
    cells = flags.shape[1]
    cell = iota((1, cells), 1)
    diagonal = (cell // BLOCK == cell % BLOCK).astype(F32)
    rows = []
    for t, pair in enumerate(pairs):
        same = (pair[0] == pair[1]).astype(F32)
        rows.append(flags[t : t + 1, :] * (1.0 - same * diagonal))
    return rows


def greet_kernel(
    blocks, intervals, pair_hbm, start_hbm, penalty_hbm, flag_hbm, out_ref, top_ref, pair_ref, start_ref,
    penalty_ref, flag_ref, sems
):
    copies = [
        pltpu.make_async_copy(source, target, sems.at[n])
        for n, (source, target) in enumerate(
            [
                (start_hbm, start_ref),
                (pair_hbm, pair_ref),
                (flag_hbm, flag_ref),
                (penalty_hbm, penalty_ref),
            ]
        )
    ]
    for copy in copies:
        copy.start()
    for copy in copies[1:]:
        copy.wait()
    owned = blocks * BLOCK
    cells = flag_ref.shape[1]
    me = lax.axis_index("base")
    pairs = scalar_pairs(pair_ref)
    tiles = len(pairs)
    weights = cell_weights(pairs, flag_ref[...].astype(F32))
    lane = iota((cells, LANES), 1)
    cell = iota((cells, LANES), 0)
    at, inside = lane // BLOCK, lane % BLOCK
    member = jnp.where(at < tiles, cell // BLOCK, cell % BLOCK) == inside
    station_w = jnp.zeros((8, LANES), F32)
    for t in range(tiles):
        fold = (member & (at % tiles == t) & (at < 2 * tiles)).astype(BF16)
        station_w = station_w + nn(jnp.broadcast_to(weights[t], (8, cells)).astype(BF16), fold)
    lane = iota((8, LANES), 1)
    row = iota((8, LANES), 0)
    wide = intervals // BLOCK
    slot_at = jnp.where(lane // BLOCK < 2 * tiles, slot_key(lane * wide, pairs, 1, intervals), -2.0)
    owner_at = jnp.where(lane // BLOCK < blocks, (me * blocks + lane // BLOCK).astype(F32), -2.0)
    keys = jnp.where(row == 0, slot_key(lane, pairs, intervals, intervals), 0.0)
    keys = jnp.where(row == 1, owner_key(lane, me, blocks, intervals, -2), keys)
    keys = jnp.where(row == 3, owner_at, keys)
    keys = jnp.where(row == 4, station_w, keys)
    out_ref[GAIN_ROWS:, :] = jnp.where(row == 5, slot_at, keys)
    out_ref[GAIN_ROWS + 2 : GAIN_ROWS + 3, :owned] = penalty_ref[...]
    copies[0].wait()
    place = (iota((BLOCK, owned), 0) == iota((BLOCK, owned), 1) % BLOCK).astype(BF16)
    here = iota((LANES, owned), 0) // intervals == iota((LANES, owned), 1) // BLOCK
    for m in range(8):
        plane = start_ref[m]
        plane = jnp.where(here, jnp.concatenate([plane] * (LANES // intervals), 0), 0.0)
        high = plane.astype(BF16)
        low = (plane - high.astype(F32)).astype(BF16)
        plane = nt(place, high) + nt(place, low)
        out_ref[m * BLOCK : (m + 1) * BLOCK, :] = plane
        if (m + 1) * BLOCK <= top_ref.shape[0]:
            top_ref[m * BLOCK : (m + 1) * BLOCK, :] = plane


def prepare_kernel(
    blocks, intervals, bands, pair_ref, chan_ref, vis_ref, model_ref, flag_ref, vt_ref, mt_ref,
    key_ref, at_ref, basis_ref, chans_ref, expand_ref
):
    planes, width, cells = vis_ref.shape
    pairs = scalar_pairs(pair_ref)
    tiles = len(pairs)
    channels = width // tiles
    me = lax.axis_index("base")
    row = iota((2 * LANES, LANES), 0)
    lane = iota((2 * LANES, LANES), 1)
    for ref, scale in ((key_ref, intervals), (at_ref, 1)):
        ref[...] = jnp.where(
            row < LANES,
            slot_key(row, pairs, scale, intervals),
            owner_key(row - LANES, me, blocks, intervals, -1, scale),
        )
    band_at = lax.axis_index("band")
    local = chan_ref[...] - band_at * intervals
    chan = (band_at * channels + iota((1, channels), 1)).astype(F32)
    xpos = -1.0 + (2.0 * chan + 1.0) / (channels * bands)
    member = (iota((2 * LANES, channels), 0) % intervals == local).astype(F32)
    chans = jnp.sum(member, 1, keepdims=True)
    chans_ref[...] = nt(jnp.ones((8, channels), BF16), member.astype(BF16))
    centre = jnp.sum(member * xpos, 1, keepdims=True) / chans
    terms = [jnp.ones((2 * LANES, LANES), F32), jnp.broadcast_to(centre, (2 * LANES, LANES))]
    for order in range(2, NPOLY):
        terms.append(2.0 * terms[1] * terms[-1] - terms[-2])
    basis = jnp.zeros((2 * LANES, LANES), F32)
    for order in range(NPOLY):
        basis = jnp.where(lane % KPAD == order, terms[order], basis)
    basis_ref[...] = jnp.where(row // intervals == lane // KPAD, basis, 0.0)
    row = iota((LANES, 2 * width), 0)
    lane = iota((LANES, 2 * width), 1)
    wide = jnp.concatenate([local] * (2 * tiles), 1)
    expand = (row // intervals == lane // channels) & (row % intervals == wide)
    expand_ref[...] = expand.astype(BF16)
    ident = (iota((cells, cells), 0) == iota((cells, cells), 1)).astype(BF16)
    rows = cell_weights(pairs, flag_ref[...].astype(F32))
    weight = jnp.concatenate([jnp.broadcast_to(w, (channels, cells)) for w in rows], 0)
    for m in range(planes):
        vt_ref[m] = nt(ident, vis_ref[m]).reshape(BLOCK, BLOCK, width)
        masked = (model_ref[m].astype(F32) * weight).astype(BF16)
        mt_ref[m] = nt(ident, masked).reshape(BLOCK, BLOCK, width)


def tie_kernel(*refs):
    pass


def hand_on_kernel(whole_ref, *refs):
    out_ref = refs[-1]
    out_ref[...] = whole_ref[whole_ref.shape[0] - out_ref.shape[0] :, :]


def hand_on(whole, rows, others):
    vmem = pl.BlockSpec(memory_space=pltpu.VMEM)
    return pl.pallas_call(
        hand_on_kernel,
        out_shape=jax.ShapeDtypeStruct((rows, whole.shape[1]), whole.dtype),
        in_specs=[vmem] + [pl.BlockSpec(memory_space=pl.ANY)] * len(others),
        out_specs=vmem,
        compiler_params=pltpu.CompilerParams(vmem_limit_bytes=1024 * 1024),
    )(whole, *others)


def after(values, others):
    place = pl.BlockSpec(memory_space=pl.ANY)
    return pl.pallas_call(
        tie_kernel,
        out_shape=[jax.ShapeDtypeStruct(x.shape, x.dtype) for x in values],
        in_specs=[place] * (len(values) + len(others)),
        out_specs=[place] * len(values),
        input_output_aliases={n: n for n in range(len(values))},
        compiler_params=pltpu.CompilerParams(vmem_limit_bytes=1024 * 1024),
    )(*values, *others)


def normal_terms(gains, vt_ref, mt_ref, expand, first_s, second_s, a_s, b_s):
    wide = pick(gains, expand, nn)
    width = wide.shape[1] // 2
    first_s[...] = wide[:, :width].reshape(8, BLOCK, width)
    second_s[...] = wide[:, width:].reshape(8, BLOCK, width)
    half = BLOCK // 2

    def step(i, totals):
        partial = None
        new = []
        first = [first_s[m, pl.ds(i, 1), :] for m in range(8)]
        vis_all = [vt_ref[m, i].astype(F32) for m in range(8)]
        mdl_all = [mt_ref[m, i].astype(F32) for m in range(8)]
        for h in range(2):
            at = slice(h * half, (h + 1) * half)
            vis = [x[at] for x in vis_all]
            mdl = [x[at] for x in mdl_all]
            second = [second_s[m, at, :] for m in range(8)]
            along = mul_herm(mdl, second)
            terms = mul_herm(vis, along) + outer_rows(along)
            partial = terms if partial is None else [x + y for x, y in zip(partial, terms)]
            back = mul(first, mdl)
            terms = herm_mul(vis, back) + outer_columns(back)
            new += [x + y for x, y in zip(totals[12 * h : 12 * (h + 1)], terms)]
        for k in range(12):
            a_s[k, pl.ds(i, 1), :] = jnp.sum(partial[k], 0, keepdims=True)
        return tuple(new)

    zero = jnp.zeros((half, width), F32)
    totals = lax.fori_loop(0, BLOCK, step, (zero,) * 24)
    for h in range(2):
        for k in range(12):
            b_s[k, h * half : (h + 1) * half, :] = totals[12 * h + k]
    return jnp.concatenate(
        [a_s[...].reshape(TERM_ROWS, width), b_s[...].reshape(TERM_ROWS, width)], 1
    )


def key_match(rows, lanes):
    count = lanes.shape[1] // LANES
    return (jnp.concatenate([rows] * count, 1) == lanes).astype(BF16)


def beside(refs, form):
    refs = list(refs)
    pieces = []
    for parts in form:
        part = [refs.pop(0)[...] for _ in range(parts)]
        pieces.append(part[0] if parts == 1 else jnp.concatenate(part, 0))
    return jnp.concatenate(pieces, 1), refs


def first_kernel(form, *refs):
    every, refs = beside(refs, form)
    key_ref, expand_ref, vt_ref, mt_ref, gains_ref, out_ref, top_ref = refs[:7]
    scratch = refs[7:]
    select = key_match(key_ref[:LANES, :], every[GAIN_ROWS + 1 : GAIN_ROWS + 2])
    gains = pick(every[:GAIN_ROWS], select)
    gains_ref[...] = gains
    expand = expand_ref[...]
    terms = pick(normal_terms(gains, vt_ref, mt_ref, expand, *scratch), expand)
    out_ref[...] = terms
    top_ref[...] = terms[: top_ref.shape[0]]


def state_kernel(form, blocks, intervals, *refs):
    every, refs = beside(refs, form)
    key_ref, at_ref, gains_ref, chans_ref, z_ref, pen_ref, scale_ref, select_ref = refs
    rows = every[GAIN_ROWS:]
    z_ref[:, :LANES] = gains_ref[...]
    z_ref[:, LANES:] = every[:GAIN_ROWS, :LANES]
    select_ref[...] = key_match(key_ref[...], rows[0:1])
    lanes = rows.shape[1]
    diagonal = iota((BLOCK, lanes), 0) == iota((BLOCK, lanes), 1) % BLOCK
    at = at_ref[...]
    pen = pick(jnp.where(diagonal, rows[2:3], 0.0), key_match(at, rows[3:4]))
    unused = iota(pen.shape, 1) >= LANES + blocks * intervals
    pen_ref[...] = jnp.where(unused, 1.0, pen)
    weights = pick(jnp.where(diagonal, rows[4:5], 0.0), key_match(at, rows[5:6]))
    scale_ref[...] = 1.0 / jnp.maximum(weights * chans_ref[0:1, :], 1.0)


def solve(normal, scale, pen, consensus):
    part = [normal[BLOCK * k : BLOCK * (k + 1)] * scale for k in range(12)]
    rhs = [part[m] + pen * consensus[BLOCK * m : BLOCK * (m + 1)] for m in range(8)]
    h_first = part[8] + pen
    h_second = part[9] + pen
    h_real, h_imag = part[10], part[11]
    determ = h_first * h_second - h_real * h_real - h_imag * h_imag
    over = 1.0 / determ
    d_first, d_second = h_first * over, h_second * over
    d_real, d_imag = h_real * over, h_imag * over
    out = [None] * 8
    for r in range(2):
        x_re, y_re = rhs[2 * r], rhs[2 * r + 1]
        x_im, y_im = rhs[4 + 2 * r], rhs[5 + 2 * r]
        out[2 * r] = x_re * d_second - (y_re * d_real + y_im * d_imag)
        out[4 + 2 * r] = x_im * d_second - (y_im * d_real - y_re * d_imag)
        out[2 * r + 1] = y_re * d_first - (x_re * d_real - x_im * d_imag)
        out[5 + 2 * r] = y_im * d_first - (x_im * d_real + x_re * d_imag)
    return jnp.concatenate(out, 0)


def step_kernel(form, *refs):
    every, refs = beside(refs, form)
    select_ref, z_ref, pen_ref, scale_ref, expand_ref, vt_ref, mt_ref = refs[:7]
    gains_ref, out_ref, top_ref = refs[7:10]
    scratch = refs[10:]
    normal = pick(every, select_ref[...])
    gains = solve(normal, scale_ref[...], pen_ref[...], z_ref[...])
    gains_ref[...] = gains
    expand = expand_ref[...]
    terms = pick(normal_terms(gains[:, :LANES], vt_ref, mt_ref, expand, *scratch), expand)
    out_ref[...] = terms
    top_ref[...] = terms[: top_ref.shape[0]]


def first_total_kernel(gains_ref, basis_ref, out_ref):
    basis = basis_ref[...]
    total = nn(gains_ref[...], basis, precision=HIGH)
    part = basis[: basis.shape[0] // 8]
    gram = lax.dot_general(
        part, part, (((0,), (0,)), ((), ())), preferred_element_type=F32, precision=HIGH
    )
    out_ref[:GAIN_ROWS, :] = total
    out_ref[GAIN_ROWS:, :] = gram[:KPAD]


def total_kernel(gains_ref, dual_ref, basis_ref, out_ref):
    out_ref[...] = nn(gains_ref[...] + dual_ref[...], basis_ref[...], precision=HIGH)


def invert(gram):
    row, lane = iota(gram.shape, 0), iota(gram.shape, 1)
    inner = (row < NPOLY) & (lane < NPOLY)
    work = jnp.where(inner, gram + jnp.where(row == lane, ridge, 0.0), 0.0)
    for p in range(NPOLY):
        here = lane == p
        column = jnp.sum(jnp.where(here, work, 0.0), 1, keepdims=True)
        over = 1.0 / column[p : p + 1]
        pivot = jnp.where(here[:1], over, work[p : p + 1] * over)
        work = jnp.where(row == p, pivot, jnp.where(here, 0.0, work) - column * pivot)
    return work


def settle(total, inverse, basis_ref, gains, z_ref, dual_ref):
    coeff = nn(total, inverse, precision=HIGH)
    consensus = nt(coeff, basis_ref[...], precision=HIGH)
    z_ref[...] = 2.0 * consensus - gains
    dual_ref[...] = gains - consensus


def band_total(refs):
    totals = [ref[...] for ref in refs]
    while len(totals) > 1:
        totals = [totals[n] + totals[n + 1] for n in range(0, len(totals), 2)]
    return totals[0]


def first_consensus_kernel(
    one_ref, two_ref, gains_ref, basis_ref, z_ref, dual_ref, inverse_ref
):
    total = one_ref[...] + two_ref[...]
    small = invert(total[GAIN_ROWS:])
    row, lane = iota((LANES, LANES), 0), iota((LANES, LANES), 1)
    spread = ((row == lane % KPAD) & (row < KPAD)).astype(F32)
    wide = nn(jnp.concatenate([small] * (LANES // KPAD), 0), spread, precision=HIGH)
    inverse = jnp.where(row // KPAD == lane // KPAD, wide, 0.0)
    inverse_ref[...] = inverse
    settle(total[:GAIN_ROWS], inverse, basis_ref, gains_ref[...], z_ref, dual_ref)


def consensus_kernel(
    one_ref, two_ref, gains_ref, old_ref, basis_ref, inverse_ref, z_ref, dual_ref
):
    total = one_ref[...] + two_ref[...]
    gains = gains_ref[...] + old_ref[...]
    settle(total, inverse_ref[...], basis_ref, gains, z_ref, dual_ref)


def last_kernel(form, *refs):
    every, refs = beside(refs, form)
    select_ref, z_ref, pen_ref, scale_ref, dual_ref, basis_ref, gains_ref, out_ref = refs
    own = slice(LANES, 2 * LANES)
    normal = pick(every, select_ref[own, :])
    gains = solve(normal, scale_ref[:, own], pen_ref[:, own], z_ref[:, own])
    gains_ref[...] = gains
    total = nn(gains + dual_ref[:, own], basis_ref[own, :], precision=HIGH)
    half = GAIN_ROWS // 2
    low = iota((half, LANES), 1) < LANES // 2
    out_ref[...] = jnp.where(low, pltpu.roll(total[:half], LANES // 2, 1), total[half:])


def gains_kernel(blocks, intervals, gains_ref, out_ref):
    owned = blocks * BLOCK
    place = (iota((intervals, LANES), 0) == iota((intervals, LANES), 1) % intervals).astype(BF16)
    here = iota((owned, LANES), 0) // BLOCK == iota((owned, LANES), 1) // intervals
    for m in range(8):
        part = gains_ref[m * BLOCK : (m + 1) * BLOCK, :]
        out_ref[m] = turn(place, jnp.where(here, jnp.concatenate([part] * blocks, 0), 0.0))


def turn(place, values):
    high = values.astype(BF16)
    rest = values - high.astype(F32)
    mid = rest.astype(BF16)
    low = (rest - mid.astype(F32)).astype(BF16)
    return (nt(place, high) + nt(place, mid)) + nt(place, low)


def coefficient_kernel(bands, blocks, *refs):
    inverse_ref, out_ref = refs[bands:]
    coeff = nn(band_total(refs[:bands]), inverse_ref[...], precision=HIGH)
    owned = blocks * BLOCK
    place = (iota((KPAD, LANES), 0) == iota((KPAD, LANES), 1) % KPAD).astype(BF16)
    for m in range(8):
        first = (m // 4) * (LANES // 2 // KPAD)
        here = iota((owned, LANES), 0) // BLOCK == iota((owned, LANES), 1) // KPAD - first
        part = coeff[(m % 4) * BLOCK : (m % 4 + 1) * BLOCK]
        part = jnp.where(here, jnp.concatenate([part] * blocks, 0), 0.0)
        out_ref[:, m, :] = turn(place, part)[:NPOLY]


def call(kernel, operands, shapes, scratch=(), smem=0, held=False, flops=20_000_000, moved=None):
    vmem = pl.BlockSpec(memory_space=pltpu.VMEM)
    in_specs = [pl.BlockSpec(memory_space=pltpu.SMEM)] * smem + [vmem] * (len(operands) - smem)
    params = pltpu.CompilerParams(vmem_limit_bytes=12 * 1024 * 1024)
    if held:
        in_specs = [pl.BlockSpec(memory_space=pl.ANY)] * len(operands)
        params = pltpu.CompilerParams()
    if moved is None:
        moved = sum(x.size * x.dtype.itemsize for x in (*operands, *shapes))
    return pl.pallas_call(
        kernel,
        out_shape=shapes,
        in_specs=in_specs,
        out_specs=[vmem] * len(shapes),
        scratch_shapes=list(scratch),
        compiler_params=params,
        cost_estimate=pl.CostEstimate(flops=flops, bytes_accessed=moved, transcendentals=0),
    )(*operands)


def share_base(x, top, early=(), late=(), first=False):
    devices = lax.axis_size("base")
    chips = devices // 2

    def along(y, k):
        return lax.ppermute(y, "base", [(d, d ^ (2 * k)) for d in range(devices)])

    if chips == 4:
        two = along(x, 2)
        far = along(top, 3)
        one = along(x, 1)
        rest = along(hand_on(two, x.shape[0] - top.shape[0], early), 1)
        if first:
            (one,) = after([one], (far,))
        if late:
            (rest,) = after([rest], late)
        mine, form = [x, one, two, far, rest], [1, 1, 1, 2]
    else:
        mine = {0: x}
        step = chips // 2
        while step:
            for k in sorted(mine):
                mine[k + step] = along(mine[k], step)
            if early:
                (mine[step],) = after([mine[step]], early)
                early = ()
            step //= 2
        if late:
            (mine[chips - 1],) = after([mine[chips - 1]], late)
        mine, form = [mine[k] for k in sorted(mine)], [1] * chips
    other = [lax.ppermute(y, "base", [(d, d ^ 1) for d in range(devices)]) for y in mine]
    return mine + other, form + form


def share_band(x):
    devices = lax.axis_size("band")
    return [x] + [
        lax.ppermute(x, "band", [(d, d ^ k) for d in range(devices)]) for k in range(1, devices)
    ]


def sum_band(x):
    devices = lax.axis_size("band")
    step, came = 1, []
    while 2 * step < devices:
        came.append(lax.ppermute(x, "band", [(d, d ^ step) for d in range(devices)]))
        x = x + came[-1]
        step = 2 * step
    return (x, lax.ppermute(x, "band", [(d, d ^ step) for d in range(devices)])), came[:1]


def on_device(visibilities, model, start_gains, penalty, pairs, flags, chan_band):
    tiles, channels, cells = visibilities.shape[1:]
    intervals = start_gains.shape[1]
    owned = start_gains.shape[2]
    blocks = owned // BLOCK
    count = lax.axis_size("base")
    bands = lax.axis_size("band")
    width = tiles * channels

    def shape(*extent, dtype=F32):
        return jax.ShapeDtypeStruct(extent, dtype)

    wide = shape(GAIN_ROWS, 2 * LANES)
    narrow = shape(GAIN_ROWS, LANES)
    single = shape(BLOCK, 2 * LANES)
    messages = [shape(TERM_ROWS, LANES), shape(TERM_ROWS // 2, LANES)]
    square = shape(2 * LANES, LANES)
    planes = shape(8, BLOCK, BLOCK, width)

    greeting, top = call(
        functools.partial(greet_kernel, blocks, intervals),
        (pairs, start_gains, penalty.reshape(1, owned), flags),
        [shape(GAIN_ROWS + 8, LANES), shape(GAIN_ROWS // 2, LANES)],
        [
            pltpu.SMEM(pairs.shape, jnp.int32),
            pltpu.VMEM(start_gains.shape, F32),
            pltpu.VMEM((1, owned), F32),
            pltpu.VMEM(flags.shape, jnp.int32),
            pltpu.SemaphoreType.DMA((4,)),
        ],
        held=True,
    )
    vt, mt, keys, at, basis, chans, expand = call(
        functools.partial(prepare_kernel, blocks, intervals, bands),
        (
            pairs,
            chan_band.reshape(1, channels),
            visibilities.reshape(8, width, cells),
            model.reshape(8, width, cells),
            flags,
        ),
        [
            planes,
            planes,
            square,
            square,
            square,
            shape(8, 2 * LANES),
            shape(LANES, 2 * width, dtype=BF16),
        ],
        smem=1,
        moved=100_000,
    )
    greetings, form = share_base(greeting, top, early=(chans,), first=True)
    scratch = [pltpu.VMEM((8, BLOCK, width), F32)] * 2 + [pltpu.VMEM((12, BLOCK, width), F32)] * 2

    gains, *message = call(
        functools.partial(first_kernel, form),
        (*greetings, keys, expand, vt, mt),
        [narrow, *messages],
        scratch,
    )
    z, pen, scale, select = call(
        functools.partial(state_kernel, form, blocks, intervals),
        (*greetings, keys, at, gains, chans),
        [wide, single, single, shape(2 * LANES, count * LANES, dtype=BF16)],
    )
    pieces, form = share_base(*message, early=(scale,))
    gains, *message = call(
        functools.partial(step_kernel, form),
        (*pieces, select, z, pen, scale, expand, vt, mt),
        [wide, *messages],
        scratch,
    )
    (part,) = call(first_total_kernel, (gains, basis), [shape(GAIN_ROWS + KPAD, LANES)])
    parts, came = sum_band(part)
    z, dual, inverse = call(first_consensus_kernel, (*parts, gains, basis), [wide, wide, narrow])
    pieces, form = share_base(*message, early=came, late=(z,))
    gains, *message = call(
        functools.partial(step_kernel, form),
        (*pieces, select, z, pen, scale, expand, vt, mt),
        [wide, *messages],
        scratch,
    )
    (part,) = call(total_kernel, (gains, dual, basis), [narrow])
    parts, came = sum_band(part)
    z, dual = call(consensus_kernel, (*parts, gains, dual, basis, inverse), [wide, wide])
    pieces, form = share_base(*message, early=came, late=(z,))
    gains, part = call(
        functools.partial(last_kernel, form),
        (*pieces, select, z, pen, scale, dual, basis),
        [narrow, shape(GAIN_ROWS // 2, LANES)],
    )
    parts = share_band(part)
    (out,) = call(
        functools.partial(gains_kernel, blocks, intervals),
        (gains,),
        [shape(8, intervals, owned)],
    )
    (coefficients,) = call(
        functools.partial(coefficient_kernel, bands, blocks),
        (*parts, inverse),
        [shape(NPOLY, 8, owned)],
    )
    return (out, jnp.transpose(coefficients, (1, 0, 2)))


def solution(mesh):
    in_specs = (
        P(None, "base", "band", None),
        P(None, "base", "band", None),
        P(None, "band", "base"),
        P("base"),
        P("base", None),
        P("base", None),
        P("band"),
    )
    out_specs = (P(None, "band", "base"), P(None, None, "base"))
    return jax.shard_map(
        on_device, mesh=mesh, in_specs=in_specs, out_specs=out_specs, check_vma=False
    )
```

```python
import functools

import jax
import jax.numpy as jnp
from jax import lax
from jax.experimental import pallas as pl
from jax.experimental.pallas import tpu as pltpu
from jax.sharding import PartitionSpec as P

BLOCK = 16
NPOLY = 9
KPAD = 16
ITERS = 3
LANES = 128
F32 = jnp.float32
BF16 = jnp.bfloat16
HIGH = lax.Precision.HIGHEST

ridge = 0.5

GAIN_ROWS = 8 * BLOCK
TERM_ROWS = 12 * BLOCK
PRODUCTS = 48
CROSS = ((0, 1), (0, 2), (0, 3), (1, 2), (1, 3), (2, 3))


def nt(left, right, **kw):
    return lax.dot_general(
        left, right, (((1,), (1,)), ((), ())), preferred_element_type=F32, **kw
    )


def nn(left, right, **kw):
    return lax.dot_general(
        left, right, (((1,), (0,)), ((), ())), preferred_element_type=F32, **kw
    )


def pick(values, select, dot=nt):
    high = values.astype(BF16)
    low = (values - high.astype(F32)).astype(BF16)
    rows = values.shape[0]
    out = dot(jnp.concatenate([high, low], 0), select)
    return out[:rows] + out[rows:]


def iota(shape, axis):
    return lax.broadcasted_iota(jnp.int32, shape, axis)


def add(terms):
    total = None
    for sign, x, y in terms:
        if total is None:
            total = x * y if sign > 0 else -(x * y)
        else:
            total = total + x * y if sign > 0 else total - x * y
    return total


def apply_gains(pairs, gains, turned):
    re, im = [], []
    for r in range(2):
        for c in range(2):
            to_re, to_im = [], []
            for k in range(2):
                for n in range(2):
                    x_re, x_im = pairs(k, r, n, c) if turned else pairs(r, k, c, n)
                    g_re, g_im = gains[2 * k + n], gains[4 + 2 * k + n]
                    sign = -1 if turned else 1
                    to_re += [(1, x_re, g_re), (-sign, x_im, g_im)]
                    to_im += [(1, x_re, g_im), (sign, x_im, g_re)]
            re.append(add(to_re))
            im.append(add(to_im))
    return re + im


def square(gains):
    return [
        add([(1, gains[n], gains[n]) for n in (0, 2, 4, 6)]),
        add([(1, gains[n], gains[n]) for n in (1, 3, 5, 7)]),
        add([(1, gains[n], gains[n + 1]) for n in (0, 2, 4, 6)]),
        add([(1, gains[0], gains[5]), (-1, gains[4], gains[1])])
        + add([(1, gains[2], gains[7]), (-1, gains[6], gains[3])]),
    ]


def outer_first(own, cross, q):
    out = []
    for r in range(2):
        x_re, x_im = cross(r, 0, r, 1)
        twice = add([(1, x_re, q[2]), (-1, x_im, q[3])])
        out.append(add([(1, own[r][0], q[0]), (1, own[r][1], q[1])]) + (twice + twice))
    (a_re, a_im), (b_re, b_im) = cross(0, 0, 1, 0), cross(0, 1, 1, 1)
    (c_re, c_im), (d_re, d_im) = cross(0, 0, 1, 1), cross(0, 1, 1, 0)
    out.append(
        add([(1, a_re, q[0]), (1, b_re, q[1]), (1, c_re + d_re, q[2]), (-1, c_im - d_im, q[3])])
    )
    out.append(
        add([(1, a_im, q[0]), (1, b_im, q[1]), (1, c_im + d_im, q[2]), (1, c_re - d_re, q[3])])
    )
    return out


def outer_second(own, cross, q):
    out = []
    for c in range(2):
        x_re, x_im = cross(0, c, 1, c)
        twice = add([(1, x_re, q[2]), (1, x_im, q[3])])
        out.append(add([(1, own[0][c], q[0]), (1, own[1][c], q[1])]) + (twice + twice))
    (a_re, a_im), (b_re, b_im) = cross(0, 0, 0, 1), cross(1, 0, 1, 1)
    (c_re, c_im), (d_re, d_im) = cross(0, 0, 1, 1), cross(0, 1, 1, 0)
    out.append(
        add([(1, a_re, q[0]), (1, b_re, q[1]), (1, c_re + d_re, q[2]), (1, c_im + d_im, q[3])])
    )
    out.append(
        add([(-1, a_im, q[0]), (-1, b_im, q[1]), (1, c_re - d_re, q[3]), (-1, c_im - d_im, q[2])])
    )
    return out


def slot_key(index, pairs, scale, intervals):
    at = index // intervals
    tiles = len(pairs)
    block = jnp.zeros(index.shape, F32)
    for slot in range(2 * tiles):
        value = pairs[slot % tiles][slot // tiles]
        block = jnp.where(at == slot, value.astype(F32), block)
    if scale > 1:
        block = block * scale + (index % intervals).astype(F32)
    return block


def scalar_pairs(pair_ref):
    return [[pair_ref[t, side] for side in range(2)] for t in range(pair_ref.shape[0])]


def owner_key(index, me, blocks, intervals, none, scale=None):
    at = index // intervals
    key = me * blocks + at
    if scale != 1:
        key = key * intervals + index % intervals
    return jnp.where(at < blocks, key, none).astype(F32)


def cell_weights(pairs, flags):
    cells = flags.shape[1]
    cell = iota((1, cells), 1)
    diagonal = (cell // BLOCK == cell % BLOCK).astype(F32)
    rows = []
    for t, pair in enumerate(pairs):
        same = (pair[0] == pair[1]).astype(F32)
        rows.append(flags[t : t + 1, :] * (1.0 - same * diagonal))
    return rows


def greet_kernel(
    blocks, intervals, pair_hbm, start_hbm, penalty_hbm, flag_hbm, out_ref, pair_ref, start_ref,
    penalty_ref, flag_ref, sems
):
    copies = [
        pltpu.make_async_copy(source, target, sems.at[n])
        for n, (source, target) in enumerate(
            [
                (start_hbm, start_ref),
                (pair_hbm, pair_ref),
                (flag_hbm, flag_ref),
                (penalty_hbm, penalty_ref),
            ]
        )
    ]
    for copy in copies:
        copy.start()
    for copy in copies[1:]:
        copy.wait()
    owned = blocks * BLOCK
    cells = flag_ref.shape[1]
    me = lax.axis_index("base")
    pairs = scalar_pairs(pair_ref)
    tiles = len(pairs)
    weights = cell_weights(pairs, flag_ref[...].astype(F32))
    lane = iota((cells, LANES), 1)
    cell = iota((cells, LANES), 0)
    at, inside = lane // BLOCK, lane % BLOCK
    member = jnp.where(at < tiles, cell // BLOCK, cell % BLOCK) == inside
    station_w = jnp.zeros((8, LANES), F32)
    for t in range(tiles):
        fold = (member & (at % tiles == t) & (at < 2 * tiles)).astype(BF16)
        station_w = station_w + nn(jnp.broadcast_to(weights[t], (8, cells)).astype(BF16), fold)
    lane = iota((8, LANES), 1)
    row = iota((8, LANES), 0)
    wide = intervals // BLOCK
    slot_at = jnp.where(lane // BLOCK < 2 * tiles, slot_key(lane * wide, pairs, 1, intervals), -2.0)
    owner_at = jnp.where(lane // BLOCK < blocks, (me * blocks + lane // BLOCK).astype(F32), -2.0)
    keys = jnp.where(row == 0, slot_key(lane, pairs, intervals, intervals), 0.0)
    keys = jnp.where(row == 1, owner_key(lane, me, blocks, intervals, -2), keys)
    keys = jnp.where(row == 3, owner_at, keys)
    keys = jnp.where(row == 4, station_w, keys)
    out_ref[GAIN_ROWS:, :] = jnp.where(row == 5, slot_at, keys)
    out_ref[GAIN_ROWS + 2 : GAIN_ROWS + 3, :owned] = penalty_ref[...]
    copies[0].wait()
    place = (iota((BLOCK, owned), 0) == iota((BLOCK, owned), 1) % BLOCK).astype(BF16)
    here = iota((LANES, owned), 0) // intervals == iota((LANES, owned), 1) // BLOCK
    for m in range(8):
        plane = start_ref[m]
        plane = jnp.where(here, jnp.concatenate([plane] * (LANES // intervals), 0), 0.0)
        high = plane.astype(BF16)
        low = (plane - high.astype(F32)).astype(BF16)
        out_ref[m * BLOCK : (m + 1) * BLOCK, :] = nt(place, high) + nt(place, low)


def prepare_kernel(
    blocks, intervals, bands, pair_hbm, chan_hbm, flag_hbm, vis_hbm, model_hbm, prod_ref, key_ref,
    at_ref, basis_ref, chans_ref, pair_ref, chan_ref, flag_ref, vis_ref, model_ref, mt_ref, sems
):
    planes, width, cells = vis_ref.shape
    moves = [(pair_hbm, pair_ref), (chan_hbm, chan_ref), (flag_hbm, flag_ref)]
    for source, target in ((model_hbm, model_ref), (vis_hbm, vis_ref)):
        moves += [(source.at[m], target.at[m]) for m in range(planes)]
    copies = [
        pltpu.make_async_copy(source, target, sems.at[n])
        for n, (source, target) in enumerate(moves)
    ]
    for copy in copies[: 3 + planes]:
        copy.start()
    for copy in copies[:3]:
        copy.wait()
    pairs = scalar_pairs(pair_ref)
    tiles = len(pairs)
    channels = width // tiles
    me = lax.axis_index("base")
    row = iota((2 * LANES, LANES), 0)
    lane = iota((2 * LANES, LANES), 1)
    for ref, scale in ((key_ref, intervals), (at_ref, 1)):
        ref[...] = jnp.where(
            row < LANES,
            slot_key(row, pairs, scale, intervals),
            owner_key(row - LANES, me, blocks, intervals, -1, scale),
        )
    band_at = lax.axis_index("band")
    local = chan_ref[...] - band_at * intervals
    chan = (band_at * channels + iota((1, channels), 1)).astype(F32)
    xpos = -1.0 + (2.0 * chan + 1.0) / (channels * bands)
    member = (iota((2 * LANES, channels), 0) % intervals == local).astype(F32)
    chans = jnp.sum(member, 1, keepdims=True)
    chans_ref[...] = nt(jnp.ones((8, channels), BF16), member.astype(BF16))
    centre = jnp.sum(member * xpos, 1, keepdims=True) / chans
    terms = [jnp.ones((2 * LANES, LANES), F32), jnp.broadcast_to(centre, (2 * LANES, LANES))]
    for order in range(2, NPOLY):
        terms.append(2.0 * terms[1] * terms[-1] - terms[-2])
    basis = jnp.zeros((2 * LANES, LANES), F32)
    for order in range(NPOLY):
        basis = jnp.where(lane % KPAD == order, terms[order], basis)
    basis_ref[...] = jnp.where(row // intervals == lane // KPAD, basis, 0.0)
    lanes = 2 * tiles * intervals
    row = iota((lanes, 2 * width), 0)
    lane = iota((lanes, 2 * width), 1)
    at = jnp.concatenate([local] * (2 * tiles), 1)
    fold = ((row // intervals == lane // channels) & (row % intervals == at)).astype(BF16)
    ident = (iota((cells, cells), 0) == iota((cells, cells), 1)).astype(BF16)
    rows = cell_weights(pairs, flag_ref[...].astype(F32))
    weight = jnp.concatenate([jnp.broadcast_to(w, (channels, cells)) for w in rows], 0)
    half = cells // 2

    def put(at, product):
        beside = jnp.concatenate([product[:half], product[half:]], 1)
        prod_ref[at] = pick(beside, fold).reshape(prod_ref.shape[1:])

    order = [4 * (m % 2) + m // 2 for m in range(planes)]
    for m in range(planes):
        copies[3 + m].wait()
        copies[3 + planes + order[m]].start()
        masked = (model_ref[m].astype(F32) * weight).astype(BF16)
        mt_ref[m] = nt(ident, masked)
    for x in range(4):
        put(32 + x, mt_ref[x] * mt_ref[x] + mt_ref[4 + x] * mt_ref[4 + x])
    for n, (x, y) in enumerate(CROSS):
        x_re, x_im, y_re, y_im = mt_ref[x], mt_ref[4 + x], mt_ref[y], mt_ref[4 + y]
        put(36 + n, x_re * y_re + x_im * y_im)
        put(42 + n, x_im * y_re - x_re * y_im)
    for x in range(4):
        copies[3 + planes + x].wait()
        copies[3 + planes + 4 + x].wait()
        v_re, v_im = nt(ident, vis_ref[x]), nt(ident, vis_ref[4 + x])
        for y in range(4):
            m_re, m_im = mt_ref[y], mt_ref[4 + y]
            put(4 * x + y, v_re * m_re + v_im * m_im)
            put(16 + 4 * x + y, v_im * m_re - v_re * m_im)


def tie_kernel(*refs):
    pass


def after(values, others):
    place = pl.BlockSpec(memory_space=pl.ANY)
    return pl.pallas_call(
        tie_kernel,
        out_shape=[jax.ShapeDtypeStruct(x.shape, x.dtype) for x in values],
        in_specs=[place] * (len(values) + len(others)),
        out_specs=[place] * len(values),
        input_output_aliases={n: n for n in range(len(values))},
        compiler_params=pltpu.CompilerParams(vmem_limit_bytes=1024 * 1024),
    )(*values, *others)


def normal_terms(gains, prod_ref, first_s, second_s, a_s, out_ref):
    half = BLOCK // 2
    low = iota((half, LANES), 1) < LANES // 2

    def swap(x):
        return pltpu.roll(x, LANES // 2, 1)

    first, second = [], [[], []]
    for m in range(8):
        part = [gains[m * BLOCK + h * half : m * BLOCK + (h + 1) * half] for h in range(2)]
        first.append(jnp.where(low, part[0], swap(part[1])))
        for h in range(2):
            second[h].append(jnp.where(low, swap(part[h]), part[h]))
    for n, x in enumerate(first + square(first)):
        first_s[n] = x
    for h in range(2):
        for n, x in enumerate(second[h] + square(second[h])):
            second_s[h, n] = x

    def step(i, totals):
        partial = None
        new = []
        one = [first_s[n, pl.ds(i, 1), :] for n in range(12)]
        for h in range(2):
            two = [second_s[h, n] for n in range(12)]

            def load(n):
                return prod_ref[n, i, h * half : (h + 1) * half, :]

            def pairs(r, k, c, n):
                at = (2 * r + k) * 4 + 2 * c + n
                return load(at), load(16 + at)

            def cross(r, k, c, n):
                at = CROSS.index((2 * r + k, 2 * c + n))
                return load(36 + at), load(42 + at)

            own = [[load(32 + 2 * r + k) for k in range(2)] for r in range(2)]
            terms = apply_gains(pairs, two[:8], False) + outer_first(own, cross, two[8:])
            partial = terms if partial is None else [x + y for x, y in zip(partial, terms)]
            terms = apply_gains(pairs, one[:8], True) + outer_second(own, cross, one[8:])
            new += [x + y for x, y in zip(totals[12 * h : 12 * (h + 1)], terms)]
        for k in range(12):
            a_s[k, pl.ds(i, 1), :] = jnp.sum(partial[k], 0, keepdims=True)
        return tuple(new)

    zero = jnp.zeros((half, LANES), F32)
    totals = lax.fori_loop(0, half, step, (zero,) * 24)
    for k in range(12):
        mine = a_s[k]
        for h in range(2):
            other = totals[12 * h + k]
            other = other + swap(other)
            at = k * BLOCK + h * half
            out_ref[at : at + half, :] = jnp.where(low, swap(mine) if h else mine, other)


def key_match(rows, lanes):
    count = lanes.shape[1] // LANES
    return (jnp.concatenate([rows] * count, 1) == lanes).astype(BF16)


def beside(refs, count):
    return jnp.concatenate([p[...] for p in refs[:count]], 1), refs[count:]


def first_kernel(count, *refs):
    every, refs = beside(refs, count)
    key_ref, prod_ref, gains_ref, out_ref = refs[:4]
    scratch = refs[4:]
    select = key_match(key_ref[:LANES, :], every[GAIN_ROWS + 1 : GAIN_ROWS + 2])
    gains = pick(every[:GAIN_ROWS], select)
    gains_ref[...] = gains
    normal_terms(gains, prod_ref, *scratch, out_ref)


def state_kernel(count, blocks, intervals, *refs):
    every, refs = beside(refs, count)
    key_ref, at_ref, gains_ref, chans_ref, z_ref, pen_ref, scale_ref, select_ref = refs
    rows = every[GAIN_ROWS:]
    z_ref[:, :LANES] = gains_ref[...]
    z_ref[:, LANES:] = every[:GAIN_ROWS, :LANES]
    select_ref[...] = key_match(key_ref[...], rows[0:1])
    lanes = rows.shape[1]
    diagonal = iota((BLOCK, lanes), 0) == iota((BLOCK, lanes), 1) % BLOCK
    at = at_ref[...]
    pen = pick(jnp.where(diagonal, rows[2:3], 0.0), key_match(at, rows[3:4]))
    unused = iota(pen.shape, 1) >= LANES + blocks * intervals
    pen_ref[...] = jnp.where(unused, 1.0, pen)
    weights = pick(jnp.where(diagonal, rows[4:5], 0.0), key_match(at, rows[5:6]))
    scale_ref[...] = 1.0 / jnp.maximum(weights * chans_ref[0:1, :], 1.0)


def solve(normal, scale, pen, consensus):
    part = [normal[BLOCK * k : BLOCK * (k + 1)] * scale for k in range(12)]
    rhs = [part[m] + pen * consensus[BLOCK * m : BLOCK * (m + 1)] for m in range(8)]
    h_first = part[8] + pen
    h_second = part[9] + pen
    h_real, h_imag = part[10], part[11]
    determ = h_first * h_second - h_real * h_real - h_imag * h_imag
    over = 1.0 / determ
    d_first, d_second = h_first * over, h_second * over
    d_real, d_imag = h_real * over, h_imag * over
    out = [None] * 8
    for r in range(2):
        x_re, y_re = rhs[2 * r], rhs[2 * r + 1]
        x_im, y_im = rhs[4 + 2 * r], rhs[5 + 2 * r]
        out[2 * r] = x_re * d_second - (y_re * d_real + y_im * d_imag)
        out[4 + 2 * r] = x_im * d_second - (y_im * d_real - y_re * d_imag)
        out[2 * r + 1] = y_re * d_first - (x_re * d_real - x_im * d_imag)
        out[5 + 2 * r] = y_im * d_first - (x_im * d_real + x_re * d_imag)
    return jnp.concatenate(out, 0)


def step_kernel(count, *refs):
    every, refs = beside(refs, count)
    select_ref, z_ref, pen_ref, scale_ref, prod_ref, gains_ref, out_ref = refs[:7]
    scratch = refs[7:]
    normal = pick(every, select_ref[...])
    gains = solve(normal, scale_ref[...], pen_ref[...], z_ref[...])
    gains_ref[...] = gains
    normal_terms(gains[:, :LANES], prod_ref, *scratch, out_ref)


def first_total_kernel(gains_ref, basis_ref, out_ref):
    basis = basis_ref[...]
    total = nn(gains_ref[...], basis, precision=HIGH)
    part = basis[: basis.shape[0] // 8]
    gram = lax.dot_general(
        part, part, (((0,), (0,)), ((), ())), preferred_element_type=F32, precision=HIGH
    )
    out_ref[:GAIN_ROWS, :] = total
    out_ref[GAIN_ROWS:, :] = gram[:KPAD]


def total_kernel(gains_ref, dual_ref, basis_ref, out_ref):
    out_ref[...] = nn(gains_ref[...] + dual_ref[...], basis_ref[...], precision=HIGH)


def invert(gram):
    row, lane = iota(gram.shape, 0), iota(gram.shape, 1)
    inner = (row < NPOLY) & (lane < NPOLY)
    work = jnp.where(inner, gram + jnp.where(row == lane, ridge, 0.0), 0.0)
    for p in range(NPOLY):
        here = lane == p
        column = jnp.sum(jnp.where(here, work, 0.0), 1, keepdims=True)
        over = 1.0 / column[p : p + 1]
        pivot = jnp.where(here[:1], over, work[p : p + 1] * over)
        work = jnp.where(row == p, pivot, jnp.where(here, 0.0, work) - column * pivot)
    return work


def settle(total, inverse, basis_ref, gains, z_ref, dual_ref):
    coeff = nn(total, inverse, precision=HIGH)
    consensus = nt(coeff, basis_ref[...], precision=HIGH)
    z_ref[...] = 2.0 * consensus - gains
    dual_ref[...] = gains - consensus


def band_total(refs):
    totals = [ref[...] for ref in refs]
    while len(totals) > 1:
        totals = [totals[n] + totals[n + 1] for n in range(0, len(totals), 2)]
    return totals[0]


def first_consensus_kernel(
    one_ref, two_ref, gains_ref, basis_ref, z_ref, dual_ref, inverse_ref
):
    total = one_ref[...] + two_ref[...]
    small = invert(total[GAIN_ROWS:])
    row, lane = iota((LANES, LANES), 0), iota((LANES, LANES), 1)
    spread = ((row == lane % KPAD) & (row < KPAD)).astype(F32)
    wide = nn(jnp.concatenate([small] * (LANES // KPAD), 0), spread, precision=HIGH)
    inverse = jnp.where(row // KPAD == lane // KPAD, wide, 0.0)
    inverse_ref[...] = inverse
    settle(total[:GAIN_ROWS], inverse, basis_ref, gains_ref[...], z_ref, dual_ref)


def consensus_kernel(
    one_ref, two_ref, gains_ref, old_ref, basis_ref, inverse_ref, z_ref, dual_ref
):
    total = one_ref[...] + two_ref[...]
    gains = gains_ref[...] + old_ref[...]
    settle(total, inverse_ref[...], basis_ref, gains, z_ref, dual_ref)


def last_kernel(count, *refs):
    every, refs = beside(refs, count)
    select_ref, z_ref, pen_ref, scale_ref, dual_ref, basis_ref, gains_ref, out_ref = refs
    own = slice(LANES, 2 * LANES)
    normal = pick(every, select_ref[own, :])
    gains = solve(normal, scale_ref[:, own], pen_ref[:, own], z_ref[:, own])
    gains_ref[...] = gains
    total = nn(gains + dual_ref[:, own], basis_ref[own, :], precision=HIGH)
    half = GAIN_ROWS // 2
    low = iota((half, LANES), 1) < LANES // 2
    out_ref[...] = jnp.where(low, pltpu.roll(total[:half], LANES // 2, 1), total[half:])


def gains_kernel(blocks, intervals, gains_ref, out_ref):
    owned = blocks * BLOCK
    place = (iota((intervals, LANES), 0) == iota((intervals, LANES), 1) % intervals).astype(BF16)
    here = iota((owned, LANES), 0) // BLOCK == iota((owned, LANES), 1) // intervals
    for m in range(8):
        part = gains_ref[m * BLOCK : (m + 1) * BLOCK, :]
        out_ref[m] = turn(place, jnp.where(here, jnp.concatenate([part] * blocks, 0), 0.0))


def turn(place, values):
    high = values.astype(BF16)
    rest = values - high.astype(F32)
    mid = rest.astype(BF16)
    low = (rest - mid.astype(F32)).astype(BF16)
    return (nt(place, high) + nt(place, mid)) + nt(place, low)


def coefficient_kernel(bands, blocks, *refs):
    inverse_ref, out_ref = refs[bands:]
    coeff = nn(band_total(refs[:bands]), inverse_ref[...], precision=HIGH)
    owned = blocks * BLOCK
    place = (iota((KPAD, LANES), 0) == iota((KPAD, LANES), 1) % KPAD).astype(BF16)
    parts = []
    for m in range(8):
        first = (m // 4) * (LANES // 2 // KPAD)
        here = iota((owned, LANES), 0) // BLOCK == iota((owned, LANES), 1) // KPAD - first
        part = coeff[(m % 4) * BLOCK : (m % 4 + 1) * BLOCK]
        parts.append(jnp.where(here, jnp.concatenate([part] * blocks, 0), 0.0))
    turned = turn(place, jnp.concatenate(parts, 0))
    for m in range(8):
        out_ref[:, m, :] = turned[:NPOLY, m * owned : (m + 1) * owned]


def call(kernel, operands, shapes, scratch=(), hbm=False, flops=20_000_000):
    vmem = pl.BlockSpec(memory_space=pltpu.VMEM)
    in_specs = [vmem] * len(operands)
    moved = sum(x.size * x.dtype.itemsize for x in (*operands, *shapes))
    if hbm:
        in_specs = [pl.BlockSpec(memory_space=pltpu.HBM)] * len(operands)
        operands = [pltpu.with_memory_space_constraint(x, pltpu.HBM) for x in operands]
    return pl.pallas_call(
        kernel,
        out_shape=shapes,
        in_specs=in_specs,
        out_specs=[vmem] * len(shapes),
        scratch_shapes=list(scratch),
        compiler_params=pltpu.CompilerParams(vmem_limit_bytes=14 * 1024 * 1024),
        cost_estimate=pl.CostEstimate(flops=flops, bytes_accessed=moved, transcendentals=0),
    )(*operands)


def share_base(x, last=(), ties=(2,)):
    devices = lax.axis_size("base")
    mine = [x] + [
        lax.ppermute(x, "base", [(d, d ^ (2 * k)) for d in range(devices)])
        for k in range(1, devices // 2)
    ]
    if last:
        for k, y in zip(ties, after([mine[k] for k in ties], last)):
            mine[k] = y
    other = [lax.ppermute(y, "base", [(d, d ^ 1) for d in range(devices)]) for y in mine]
    return mine + other


def share_band(x):
    devices = lax.axis_size("band")
    return [x] + [
        lax.ppermute(x, "band", [(d, d ^ k) for d in range(devices)]) for k in range(1, devices)
    ]


def sum_band(x):
    devices = lax.axis_size("band")
    step = 1
    while 2 * step < devices:
        x = x + lax.ppermute(x, "band", [(d, d ^ step) for d in range(devices)])
        step = 2 * step
    return x, lax.ppermute(x, "band", [(d, d ^ step) for d in range(devices)])


def on_device(visibilities, model, start_gains, penalty, pairs, flags, chan_band):
    tiles, channels, cells = visibilities.shape[1:]
    intervals = start_gains.shape[1]
    owned = start_gains.shape[2]
    blocks = owned // BLOCK
    count = lax.axis_size("base")
    bands = lax.axis_size("band")
    width = tiles * channels

    def shape(*extent, dtype=F32):
        return jax.ShapeDtypeStruct(extent, dtype)

    wide = shape(GAIN_ROWS, 2 * LANES)
    narrow = shape(GAIN_ROWS, LANES)
    single = shape(BLOCK, 2 * LANES)
    terms = shape(TERM_ROWS, LANES)
    square = shape(2 * LANES, LANES)

    (greeting,) = call(
        functools.partial(greet_kernel, blocks, intervals),
        (pairs, start_gains, penalty.reshape(1, owned), flags),
        [shape(GAIN_ROWS + 8, LANES)],
        [
            pltpu.SMEM(pairs.shape, jnp.int32),
            pltpu.VMEM(start_gains.shape, F32),
            pltpu.VMEM((1, owned), F32),
            pltpu.VMEM(flags.shape, jnp.int32),
            pltpu.SemaphoreType.DMA((4,)),
        ],
        hbm=True,
    )
    products, keys, at, basis, chans = call(
        functools.partial(prepare_kernel, blocks, intervals, bands),
        (
            pairs,
            chan_band.reshape(1, channels),
            flags,
            visibilities.reshape(8, width, cells),
            model.reshape(8, width, cells),
        ),
        [
            shape(PRODUCTS, BLOCK // 2, BLOCK, 2 * tiles * intervals),
            square,
            square,
            square,
            shape(8, 2 * LANES),
        ],
        [
            pltpu.SMEM(pairs.shape, jnp.int32),
            pltpu.VMEM((1, channels), jnp.int32),
            pltpu.VMEM(flags.shape, jnp.int32),
            *[pltpu.VMEM((8, width, cells), BF16)] * 2,
            pltpu.VMEM((8, cells, width), F32),
            pltpu.SemaphoreType.DMA((19,)),
        ],
        hbm=True,
        flops=2_000_000_000,
    )
    greetings = share_base(greeting, last=(chans,))
    scratch = [
        pltpu.VMEM((12, BLOCK // 2, LANES), F32),
        pltpu.VMEM((2, 12, BLOCK // 2, LANES), F32),
        pltpu.VMEM((12, BLOCK // 2, LANES), F32),
    ]

    gains, message = call(
        functools.partial(first_kernel, count),
        (*greetings, keys, products),
        [narrow, terms],
        scratch,
    )
    z, pen, scale, select = call(
        functools.partial(state_kernel, count, blocks, intervals),
        (*greetings, keys, at, gains, chans),
        [wide, single, single, shape(2 * LANES, count * LANES, dtype=BF16)],
    )
    pieces = share_base(message, last=(scale,))
    gains, message = call(
        functools.partial(step_kernel, count),
        (*pieces, select, z, pen, scale, products),
        [wide, terms],
        scratch,
    )
    (part,) = call(first_total_kernel, (gains, basis), [shape(GAIN_ROWS + KPAD, LANES)])
    z, dual, inverse = call(
        first_consensus_kernel, (*sum_band(part), gains, basis), [wide, wide, narrow]
    )
    pieces = share_base(message, last=(z,), ties=(1, 2))
    gains, message = call(
        functools.partial(step_kernel, count),
        (*pieces, select, z, pen, scale, products),
        [wide, terms],
        scratch,
    )
    (part,) = call(total_kernel, (gains, dual, basis), [narrow])
    z, dual = call(consensus_kernel, (*sum_band(part), gains, dual, basis, inverse), [wide, wide])
    pieces = share_base(message, last=(z,), ties=(1, 2))
    gains, part = call(
        functools.partial(last_kernel, count),
        (*pieces, select, z, pen, scale, dual, basis),
        [narrow, shape(GAIN_ROWS // 2, LANES)],
    )
    parts = share_band(part)
    (out,) = call(
        functools.partial(gains_kernel, blocks, intervals),
        (gains,),
        [shape(8, intervals, owned)],
    )
    (coefficients,) = call(
        functools.partial(coefficient_kernel, bands, blocks),
        (*parts, inverse),
        [shape(NPOLY, 8, owned)],
    )
    return (out, jnp.transpose(coefficients, (1, 0, 2)))


def solution(mesh):
    in_specs = (
        P(None, "base", "band", None),
        P(None, "base", "band", None),
        P(None, "band", "base"),
        P("base"),
        P("base", None),
        P("base", None),
        P("band"),
    )
    out_specs = (P(None, "band", "base"), P(None, None, "base"))
    return jax.shard_map(
        on_device, mesh=mesh, in_specs=in_specs, out_specs=out_specs, check_vma=False
    )
```

```python
import functools

import jax
import jax.numpy as jnp
from jax import lax
from jax.experimental import pallas as pl
from jax.experimental.pallas import tpu as pltpu
from jax.sharding import PartitionSpec as P

BLOCK = 16
NPOLY = 9
KPAD = 16
ITERS = 3
LANES = 128
F32 = jnp.float32
BF16 = jnp.bfloat16
HIGH = lax.Precision.HIGHEST

ridge = 0.5

GAIN_ROWS = 8 * BLOCK
TERM_ROWS = 12 * BLOCK
PRODUCTS = 48
CROSS = ((0, 1), (0, 2), (0, 3), (1, 2), (1, 3), (2, 3))


def nt(left, right, **kw):
    return lax.dot_general(
        left, right, (((1,), (1,)), ((), ())), preferred_element_type=F32, **kw
    )


def nn(left, right, **kw):
    return lax.dot_general(
        left, right, (((1,), (0,)), ((), ())), preferred_element_type=F32, **kw
    )


def pick(values, select, dot=nt):
    high = values.astype(BF16)
    low = (values - high.astype(F32)).astype(BF16)
    rows = values.shape[0]
    out = dot(jnp.concatenate([high, low], 0), select)
    return out[:rows] + out[rows:]


def iota(shape, axis):
    return lax.broadcasted_iota(jnp.int32, shape, axis)


def add(terms):
    total = None
    for sign, x, y in terms:
        if total is None:
            total = x * y if sign > 0 else -(x * y)
        else:
            total = total + x * y if sign > 0 else total - x * y
    return total


def apply_gains(pairs, gains, turned):
    re, im = [], []
    for r in range(2):
        for c in range(2):
            to_re, to_im = [], []
            for k in range(2):
                for n in range(2):
                    x_re, x_im = pairs(k, r, n, c) if turned else pairs(r, k, c, n)
                    g_re, g_im = gains[2 * k + n], gains[4 + 2 * k + n]
                    sign = -1 if turned else 1
                    to_re += [(1, x_re, g_re), (-sign, x_im, g_im)]
                    to_im += [(1, x_re, g_im), (sign, x_im, g_re)]
            re.append(add(to_re))
            im.append(add(to_im))
    return re + im


def square(gains):
    return [
        add([(1, gains[n], gains[n]) for n in (0, 2, 4, 6)]),
        add([(1, gains[n], gains[n]) for n in (1, 3, 5, 7)]),
        add([(1, gains[n], gains[n + 1]) for n in (0, 2, 4, 6)]),
        add([(1, gains[0], gains[5]), (-1, gains[4], gains[1])])
        + add([(1, gains[2], gains[7]), (-1, gains[6], gains[3])]),
    ]


def outer_first(own, cross, q):
    out = []
    for r in range(2):
        x_re, x_im = cross(r, 0, r, 1)
        twice = add([(1, x_re, q[2]), (-1, x_im, q[3])])
        out.append(add([(1, own[r][0], q[0]), (1, own[r][1], q[1])]) + (twice + twice))
    (a_re, a_im), (b_re, b_im) = cross(0, 0, 1, 0), cross(0, 1, 1, 1)
    (c_re, c_im), (d_re, d_im) = cross(0, 0, 1, 1), cross(0, 1, 1, 0)
    out.append(
        add([(1, a_re, q[0]), (1, b_re, q[1]), (1, c_re + d_re, q[2]), (-1, c_im - d_im, q[3])])
    )
    out.append(
        add([(1, a_im, q[0]), (1, b_im, q[1]), (1, c_im + d_im, q[2]), (1, c_re - d_re, q[3])])
    )
    return out


def outer_second(own, cross, q):
    out = []
    for c in range(2):
        x_re, x_im = cross(0, c, 1, c)
        twice = add([(1, x_re, q[2]), (1, x_im, q[3])])
        out.append(add([(1, own[0][c], q[0]), (1, own[1][c], q[1])]) + (twice + twice))
    (a_re, a_im), (b_re, b_im) = cross(0, 0, 0, 1), cross(1, 0, 1, 1)
    (c_re, c_im), (d_re, d_im) = cross(0, 0, 1, 1), cross(0, 1, 1, 0)
    out.append(
        add([(1, a_re, q[0]), (1, b_re, q[1]), (1, c_re + d_re, q[2]), (1, c_im + d_im, q[3])])
    )
    out.append(
        add([(-1, a_im, q[0]), (-1, b_im, q[1]), (1, c_re - d_re, q[3]), (-1, c_im - d_im, q[2])])
    )
    return out


def slot_key(index, pairs, scale, intervals):
    at = index // intervals
    tiles = len(pairs)
    block = jnp.zeros(index.shape, F32)
    for slot in range(2 * tiles):
        value = pairs[slot % tiles][slot // tiles]
        block = jnp.where(at == slot, value.astype(F32), block)
    if scale > 1:
        block = block * scale + (index % intervals).astype(F32)
    return block


def scalar_pairs(pair_ref):
    return [[pair_ref[t, side] for side in range(2)] for t in range(pair_ref.shape[0])]


def owner_key(index, me, blocks, intervals, none, scale=None):
    at = index // intervals
    key = me * blocks + at
    if scale != 1:
        key = key * intervals + index % intervals
    return jnp.where(at < blocks, key, none).astype(F32)


def cell_weights(pairs, flags):
    cells = flags.shape[1]
    cell = iota((1, cells), 1)
    diagonal = (cell // BLOCK == cell % BLOCK).astype(F32)
    rows = []
    for t, pair in enumerate(pairs):
        same = (pair[0] == pair[1]).astype(F32)
        rows.append(flags[t : t + 1, :] * (1.0 - same * diagonal))
    return rows


def greet_kernel(
    blocks, intervals, pair_hbm, start_hbm, penalty_hbm, flag_hbm, out_ref, pair_ref, start_ref,
    penalty_ref, flag_ref, sems
):
    copies = [
        pltpu.make_async_copy(source, target, sems.at[n])
        for n, (source, target) in enumerate(
            [
                (start_hbm, start_ref),
                (pair_hbm, pair_ref),
                (flag_hbm, flag_ref),
                (penalty_hbm, penalty_ref),
            ]
        )
    ]
    for copy in copies:
        copy.start()
    for copy in copies[1:]:
        copy.wait()
    owned = blocks * BLOCK
    cells = flag_ref.shape[1]
    me = lax.axis_index("base")
    pairs = scalar_pairs(pair_ref)
    tiles = len(pairs)
    weights = cell_weights(pairs, flag_ref[...].astype(F32))
    lane = iota((cells, LANES), 1)
    cell = iota((cells, LANES), 0)
    at, inside = lane // BLOCK, lane % BLOCK
    member = jnp.where(at < tiles, cell // BLOCK, cell % BLOCK) == inside
    station_w = jnp.zeros((8, LANES), F32)
    for t in range(tiles):
        fold = (member & (at % tiles == t) & (at < 2 * tiles)).astype(BF16)
        station_w = station_w + nn(jnp.broadcast_to(weights[t], (8, cells)).astype(BF16), fold)
    lane = iota((8, LANES), 1)
    row = iota((8, LANES), 0)
    wide = intervals // BLOCK
    slot_at = jnp.where(lane // BLOCK < 2 * tiles, slot_key(lane * wide, pairs, 1, intervals), -2.0)
    owner_at = jnp.where(lane // BLOCK < blocks, (me * blocks + lane // BLOCK).astype(F32), -2.0)
    keys = jnp.where(row == 0, slot_key(lane, pairs, intervals, intervals), 0.0)
    keys = jnp.where(row == 1, owner_key(lane, me, blocks, intervals, -2), keys)
    keys = jnp.where(row == 3, owner_at, keys)
    keys = jnp.where(row == 4, station_w, keys)
    out_ref[GAIN_ROWS:, :] = jnp.where(row == 5, slot_at, keys)
    out_ref[GAIN_ROWS + 2 : GAIN_ROWS + 3, :owned] = penalty_ref[...]
    copies[0].wait()
    place = (iota((BLOCK, owned), 0) == iota((BLOCK, owned), 1) % BLOCK).astype(BF16)
    here = iota((LANES, owned), 0) // intervals == iota((LANES, owned), 1) // BLOCK
    for m in range(8):
        plane = start_ref[m]
        plane = jnp.where(here, jnp.concatenate([plane] * (LANES // intervals), 0), 0.0)
        high = plane.astype(BF16)
        low = (plane - high.astype(F32)).astype(BF16)
        out_ref[m * BLOCK : (m + 1) * BLOCK, :] = nt(place, high) + nt(place, low)


def prepare_kernel(
    blocks, intervals, bands, pair_hbm, chan_hbm, flag_hbm, vis_hbm, model_hbm, prod_ref, key_ref,
    at_ref, basis_ref, chans_ref, pair_ref, chan_ref, flag_ref, vis_ref, model_ref, mt_ref, sems
):
    planes, width, cells = vis_ref.shape
    moves = [
        (model_hbm, model_ref),
        (vis_hbm, vis_ref),
        (pair_hbm, pair_ref),
        (chan_hbm, chan_ref),
        (flag_hbm, flag_ref),
    ]
    copies = [
        pltpu.make_async_copy(source, target, sems.at[n])
        for n, (source, target) in enumerate(moves)
    ]
    for copy in copies:
        copy.start()
    for copy in copies[2:]:
        copy.wait()
    pairs = scalar_pairs(pair_ref)
    tiles = len(pairs)
    channels = width // tiles
    me = lax.axis_index("base")
    row = iota((2 * LANES, LANES), 0)
    lane = iota((2 * LANES, LANES), 1)
    for ref, scale in ((key_ref, intervals), (at_ref, 1)):
        ref[...] = jnp.where(
            row < LANES,
            slot_key(row, pairs, scale, intervals),
            owner_key(row - LANES, me, blocks, intervals, -1, scale),
        )
    band_at = lax.axis_index("band")
    local = chan_ref[...] - band_at * intervals
    chan = (band_at * channels + iota((1, channels), 1)).astype(F32)
    xpos = -1.0 + (2.0 * chan + 1.0) / (channels * bands)
    member = (iota((2 * LANES, channels), 0) % intervals == local).astype(F32)
    chans = jnp.sum(member, 1, keepdims=True)
    chans_ref[...] = nt(jnp.ones((8, channels), BF16), member.astype(BF16))
    centre = jnp.sum(member * xpos, 1, keepdims=True) / chans
    terms = [jnp.ones((2 * LANES, LANES), F32), jnp.broadcast_to(centre, (2 * LANES, LANES))]
    for order in range(2, NPOLY):
        terms.append(2.0 * terms[1] * terms[-1] - terms[-2])
    basis = jnp.zeros((2 * LANES, LANES), F32)
    for order in range(NPOLY):
        basis = jnp.where(lane % KPAD == order, terms[order], basis)
    basis_ref[...] = jnp.where(row // intervals == lane // KPAD, basis, 0.0)
    lanes = 2 * tiles * intervals
    row = iota((lanes, 2 * width), 0)
    lane = iota((lanes, 2 * width), 1)
    at = jnp.concatenate([local] * (2 * tiles), 1)
    fold = ((row // intervals == lane // channels) & (row % intervals == at)).astype(BF16)
    ident = (iota((cells, cells), 0) == iota((cells, cells), 1)).astype(BF16)
    rows = cell_weights(pairs, flag_ref[...].astype(F32))
    weight = jnp.concatenate([jnp.broadcast_to(w, (channels, cells)) for w in rows], 0)
    half = cells // 2

    def put(at, product):
        beside = jnp.concatenate([product[:half], product[half:]], 1)
        prod_ref[at] = pick(beside, fold).reshape(prod_ref.shape[1:])

    copies[0].wait()
    for m in range(planes):
        masked = (model_ref[m].astype(F32) * weight).astype(BF16)
        mt_ref[m] = nt(ident, masked)
    for x in range(4):
        put(32 + x, mt_ref[x] * mt_ref[x] + mt_ref[4 + x] * mt_ref[4 + x])
    for n, (x, y) in enumerate(CROSS):
        x_re, x_im, y_re, y_im = mt_ref[x], mt_ref[4 + x], mt_ref[y], mt_ref[4 + y]
        put(36 + n, x_re * y_re + x_im * y_im)
        put(42 + n, x_im * y_re - x_re * y_im)
    copies[1].wait()
    for x in range(4):
        v_re, v_im = nt(ident, vis_ref[x]), nt(ident, vis_ref[4 + x])
        for y in range(4):
            m_re, m_im = mt_ref[y], mt_ref[4 + y]
            put(4 * x + y, v_re * m_re + v_im * m_im)
            put(16 + 4 * x + y, v_im * m_re - v_re * m_im)


def tie_kernel(*refs):
    pass


def after(values, others, flops=0):
    place = pl.BlockSpec(memory_space=pl.ANY)
    return pl.pallas_call(
        tie_kernel,
        out_shape=[jax.ShapeDtypeStruct(x.shape, x.dtype) for x in values],
        in_specs=[place] * (len(values) + len(others)),
        out_specs=[place] * len(values),
        input_output_aliases={n: n for n in range(len(values))},
        compiler_params=pltpu.CompilerParams(vmem_limit_bytes=1024 * 1024),
        cost_estimate=pl.CostEstimate(flops=flops, bytes_accessed=0, transcendentals=0),
    )(*values, *others)


def normal_terms(gains, prod_ref, first_s, second_s, a_s, out_ref):
    half = BLOCK // 2
    low = iota((half, LANES), 1) < LANES // 2

    def swap(x):
        return pltpu.roll(x, LANES // 2, 1)

    first, second = [], [[], []]
    for m in range(8):
        part = [gains[m * BLOCK + h * half : m * BLOCK + (h + 1) * half] for h in range(2)]
        first.append(jnp.where(low, part[0], swap(part[1])))
        for h in range(2):
            second[h].append(jnp.where(low, swap(part[h]), part[h]))
    for n, x in enumerate(first + square(first)):
        first_s[n] = x
    for h in range(2):
        for n, x in enumerate(second[h] + square(second[h])):
            second_s[h, n] = x

    def step(i, totals):
        partial = None
        new = []
        one = [first_s[n, pl.ds(i, 1), :] for n in range(12)]
        for h in range(2):
            two = [second_s[h, n] for n in range(12)]

            def load(n):
                return prod_ref[n, i, h * half : (h + 1) * half, :]

            def pairs(r, k, c, n):
                at = (2 * r + k) * 4 + 2 * c + n
                return load(at), load(16 + at)

            def cross(r, k, c, n):
                at = CROSS.index((2 * r + k, 2 * c + n))
                return load(36 + at), load(42 + at)

            own = [[load(32 + 2 * r + k) for k in range(2)] for r in range(2)]
            terms = apply_gains(pairs, two[:8], False) + outer_first(own, cross, two[8:])
            partial = terms if partial is None else [x + y for x, y in zip(partial, terms)]
            terms = apply_gains(pairs, one[:8], True) + outer_second(own, cross, one[8:])
            new += [x + y for x, y in zip(totals[12 * h : 12 * (h + 1)], terms)]
        for k in range(12):
            a_s[k, pl.ds(i, 1), :] = jnp.sum(partial[k], 0, keepdims=True)
        return tuple(new)

    zero = jnp.zeros((half, LANES), F32)
    totals = lax.fori_loop(0, half, step, (zero,) * 24, unroll=2)
    for k in range(12):
        mine = a_s[k]
        for h in range(2):
            other = totals[12 * h + k]
            other = other + swap(other)
            at = k * BLOCK + h * half
            out_ref[at : at + half, :] = jnp.where(low, swap(mine) if h else mine, other)


def key_match(rows, lanes):
    count = lanes.shape[1] // LANES
    return (jnp.concatenate([rows] * count, 1) == lanes).astype(BF16)


def beside(refs, count):
    return jnp.concatenate([p[...] for p in refs[:count]], 1), refs[count:]


def first_kernel(count, *refs):
    every, refs = beside(refs, count)
    key_ref, prod_ref, gains_ref, out_ref = refs[:4]
    scratch = refs[4:]
    select = key_match(key_ref[:LANES, :], every[GAIN_ROWS + 1 : GAIN_ROWS + 2])
    gains = pick(every[:GAIN_ROWS], select)
    gains_ref[...] = gains
    normal_terms(gains, prod_ref, *scratch, out_ref)


def state_kernel(count, blocks, intervals, *refs):
    every, refs = beside(refs, count)
    key_ref, at_ref, gains_ref, chans_ref, z_ref, pen_ref, scale_ref, select_ref = refs
    rows = every[GAIN_ROWS:]
    z_ref[:, :LANES] = gains_ref[...]
    z_ref[:, LANES:] = every[:GAIN_ROWS, :LANES]
    select_ref[...] = key_match(key_ref[...], rows[0:1])
    lanes = rows.shape[1]
    diagonal = iota((BLOCK, lanes), 0) == iota((BLOCK, lanes), 1) % BLOCK
    at = at_ref[...]
    pen = pick(jnp.where(diagonal, rows[2:3], 0.0), key_match(at, rows[3:4]))
    unused = iota(pen.shape, 1) >= LANES + blocks * intervals
    pen_ref[...] = jnp.where(unused, 1.0, pen)
    weights = pick(jnp.where(diagonal, rows[4:5], 0.0), key_match(at, rows[5:6]))
    scale_ref[...] = 1.0 / jnp.maximum(weights * chans_ref[0:1, :], 1.0)


def solve(normal, scale, pen, consensus):
    part = [normal[BLOCK * k : BLOCK * (k + 1)] * scale for k in range(12)]
    rhs = [part[m] + pen * consensus[BLOCK * m : BLOCK * (m + 1)] for m in range(8)]
    h_first = part[8] + pen
    h_second = part[9] + pen
    h_real, h_imag = part[10], part[11]
    determ = h_first * h_second - h_real * h_real - h_imag * h_imag
    over = 1.0 / determ
    d_first, d_second = h_first * over, h_second * over
    d_real, d_imag = h_real * over, h_imag * over
    out = [None] * 8
    for r in range(2):
        x_re, y_re = rhs[2 * r], rhs[2 * r + 1]
        x_im, y_im = rhs[4 + 2 * r], rhs[5 + 2 * r]
        out[2 * r] = x_re * d_second - (y_re * d_real + y_im * d_imag)
        out[4 + 2 * r] = x_im * d_second - (y_im * d_real - y_re * d_imag)
        out[2 * r + 1] = y_re * d_first - (x_re * d_real - x_im * d_imag)
        out[5 + 2 * r] = y_im * d_first - (x_im * d_real + x_re * d_imag)
    return jnp.concatenate(out, 0)


def step_kernel(count, *refs):
    every, refs = beside(refs, count)
    select_ref, z_ref, pen_ref, scale_ref, prod_ref, gains_ref, out_ref = refs[:7]
    scratch = refs[7:]
    normal = pick(every, select_ref[...])
    gains = solve(normal, scale_ref[...], pen_ref[...], z_ref[...])
    gains_ref[...] = gains
    normal_terms(gains[:, :LANES], prod_ref, *scratch, out_ref)


def first_total_kernel(gains_ref, basis_ref, out_ref):
    basis = basis_ref[...]
    total = nn(gains_ref[...], basis, precision=HIGH)
    part = basis[: basis.shape[0] // 8]
    gram = lax.dot_general(
        part, part, (((0,), (0,)), ((), ())), preferred_element_type=F32, precision=HIGH
    )
    out_ref[:GAIN_ROWS, :] = total
    out_ref[GAIN_ROWS:, :] = gram[:KPAD]


def total_kernel(gains_ref, dual_ref, basis_ref, out_ref):
    out_ref[...] = nn(gains_ref[...] + dual_ref[...], basis_ref[...], precision=HIGH)


def invert(gram):
    row, lane = iota(gram.shape, 0), iota(gram.shape, 1)
    inner = (row < NPOLY) & (lane < NPOLY)
    work = jnp.where(inner, gram + jnp.where(row == lane, ridge, 0.0), 0.0)
    for p in range(NPOLY):
        here = lane == p
        column = jnp.sum(jnp.where(here, work, 0.0), 1, keepdims=True)
        over = 1.0 / column[p : p + 1]
        pivot = jnp.where(here[:1], over, work[p : p + 1] * over)
        work = jnp.where(row == p, pivot, jnp.where(here, 0.0, work) - column * pivot)
    return work


def settle(total, inverse, basis_ref, gains, z_ref, dual_ref):
    coeff = nn(total, inverse, precision=HIGH)
    consensus = nt(coeff, basis_ref[...], precision=HIGH)
    z_ref[...] = 2.0 * consensus - gains
    dual_ref[...] = gains - consensus


def band_total(refs):
    totals = [ref[...] for ref in refs]
    while len(totals) > 1:
        totals = [totals[n] + totals[n + 1] for n in range(0, len(totals), 2)]
    return totals[0]


def first_consensus_kernel(
    one_ref, two_ref, gains_ref, basis_ref, z_ref, dual_ref, inverse_ref
):
    total = one_ref[...] + two_ref[...]
    small = invert(total[GAIN_ROWS:])
    row, lane = iota((LANES, LANES), 0), iota((LANES, LANES), 1)
    spread = ((row == lane % KPAD) & (row < KPAD)).astype(F32)
    wide = nn(jnp.concatenate([small] * (LANES // KPAD), 0), spread, precision=HIGH)
    inverse = jnp.where(row // KPAD == lane // KPAD, wide, 0.0)
    inverse_ref[...] = inverse
    settle(total[:GAIN_ROWS], inverse, basis_ref, gains_ref[...], z_ref, dual_ref)


def consensus_kernel(
    one_ref, two_ref, gains_ref, old_ref, basis_ref, inverse_ref, z_ref, dual_ref
):
    total = one_ref[...] + two_ref[...]
    gains = gains_ref[...] + old_ref[...]
    settle(total, inverse_ref[...], basis_ref, gains, z_ref, dual_ref)


def last_kernel(count, *refs):
    every, refs = beside(refs, count)
    select_ref, z_ref, pen_ref, scale_ref, dual_ref, basis_ref, gains_ref, out_ref = refs
    own = slice(LANES, 2 * LANES)
    normal = pick(every, select_ref[own, :])
    gains = solve(normal, scale_ref[:, own], pen_ref[:, own], z_ref[:, own])
    gains_ref[...] = gains
    total = nn(gains + dual_ref[:, own], basis_ref[own, :], precision=HIGH)
    half = GAIN_ROWS // 2
    low = iota((half, LANES), 1) < LANES // 2
    out_ref[...] = jnp.where(low, pltpu.roll(total[:half], LANES // 2, 1), total[half:])


def gains_kernel(blocks, intervals, gains_ref, out_ref):
    owned = blocks * BLOCK
    place = (iota((intervals, LANES), 0) == iota((intervals, LANES), 1) % intervals).astype(BF16)
    here = iota((owned, LANES), 0) // BLOCK == iota((owned, LANES), 1) // intervals
    for m in range(8):
        part = gains_ref[m * BLOCK : (m + 1) * BLOCK, :]
        out_ref[m] = turn(place, jnp.where(here, jnp.concatenate([part] * blocks, 0), 0.0))


def turn(place, values):
    high = values.astype(BF16)
    rest = values - high.astype(F32)
    mid = rest.astype(BF16)
    low = (rest - mid.astype(F32)).astype(BF16)
    return (nt(place, high) + nt(place, mid)) + nt(place, low)


def coefficient_kernel(bands, blocks, *refs):
    inverse_ref, out_ref = refs[bands:]
    coeff = nn(band_total(refs[:bands]), inverse_ref[...], precision=HIGH)
    owned = blocks * BLOCK
    place = (iota((KPAD, LANES), 0) == iota((KPAD, LANES), 1) % KPAD).astype(BF16)
    parts = []
    for m in range(8):
        first = (m // 4) * (LANES // 2 // KPAD)
        here = iota((owned, LANES), 0) // BLOCK == iota((owned, LANES), 1) // KPAD - first
        part = coeff[(m % 4) * BLOCK : (m % 4 + 1) * BLOCK]
        parts.append(jnp.where(here, jnp.concatenate([part] * blocks, 0), 0.0))
    turned = turn(place, jnp.concatenate(parts, 0))
    for m in range(8):
        out_ref[:, m, :] = turned[:NPOLY, m * owned : (m + 1) * owned]


def call(kernel, operands, shapes, scratch=(), hbm=False, flops=20_000_000):
    vmem = pl.BlockSpec(memory_space=pltpu.VMEM)
    in_specs = [vmem] * len(operands)
    moved = sum(x.size * x.dtype.itemsize for x in (*operands, *shapes))
    if hbm:
        in_specs = [pl.BlockSpec(memory_space=pltpu.HBM)] * len(operands)
        operands = [pltpu.with_memory_space_constraint(x, pltpu.HBM) for x in operands]
    return pl.pallas_call(
        kernel,
        out_shape=shapes,
        in_specs=in_specs,
        out_specs=[vmem] * len(shapes),
        scratch_shapes=list(scratch),
        compiler_params=pltpu.CompilerParams(vmem_limit_bytes=14 * 1024 * 1024),
        cost_estimate=pl.CostEstimate(flops=flops, bytes_accessed=moved, transcendentals=0),
    )(*operands)


def share_base(x, last=(), ties=(2,), ahead=False):
    devices = lax.axis_size("base")
    mine = [x] + [
        lax.ppermute(x, "base", [(d, d ^ (2 * k)) for d in range(devices)])
        for k in range(1, devices // 2)
    ]
    if ahead:
        mine[3:] = after(mine[3:], (), flops=5_000_000_000)
    if last:
        for k, y in zip(ties, after([mine[k] for k in ties], last)):
            mine[k] = y
    other = [lax.ppermute(y, "base", [(d, d ^ 1) for d in range(devices)]) for y in mine]
    return mine + other


def share_band(x):
    devices = lax.axis_size("band")
    return [x] + [
        lax.ppermute(x, "band", [(d, d ^ k) for d in range(devices)]) for k in range(1, devices)
    ]


def sum_band(x):
    devices = lax.axis_size("band")
    step = 1
    while 2 * step < devices:
        x = x + lax.ppermute(x, "band", [(d, d ^ step) for d in range(devices)])
        step = 2 * step
    return x, lax.ppermute(x, "band", [(d, d ^ step) for d in range(devices)])


def on_device(visibilities, model, start_gains, penalty, pairs, flags, chan_band):
    tiles, channels, cells = visibilities.shape[1:]
    intervals = start_gains.shape[1]
    owned = start_gains.shape[2]
    blocks = owned // BLOCK
    count = lax.axis_size("base")
    bands = lax.axis_size("band")
    width = tiles * channels

    def shape(*extent, dtype=F32):
        return jax.ShapeDtypeStruct(extent, dtype)

    wide = shape(GAIN_ROWS, 2 * LANES)
    narrow = shape(GAIN_ROWS, LANES)
    single = shape(BLOCK, 2 * LANES)
    terms = shape(TERM_ROWS, LANES)
    square = shape(2 * LANES, LANES)

    (greeting,) = call(
        functools.partial(greet_kernel, blocks, intervals),
        (pairs, start_gains, penalty.reshape(1, owned), flags),
        [shape(GAIN_ROWS + 8, LANES)],
        [
            pltpu.SMEM(pairs.shape, jnp.int32),
            pltpu.VMEM(start_gains.shape, F32),
            pltpu.VMEM((1, owned), F32),
            pltpu.VMEM(flags.shape, jnp.int32),
            pltpu.SemaphoreType.DMA((4,)),
        ],
        hbm=True,
    )
    products, keys, at, basis, chans = call(
        functools.partial(prepare_kernel, blocks, intervals, bands),
        (
            pairs,
            chan_band.reshape(1, channels),
            flags,
            visibilities.reshape(8, width, cells),
            model.reshape(8, width, cells),
        ),
        [
            shape(PRODUCTS, BLOCK // 2, BLOCK, 2 * tiles * intervals),
            square,
            square,
            square,
            shape(8, 2 * LANES),
        ],
        [
            pltpu.SMEM(pairs.shape, jnp.int32),
            pltpu.VMEM((1, channels), jnp.int32),
            pltpu.VMEM(flags.shape, jnp.int32),
            *[pltpu.VMEM((8, width, cells), BF16)] * 2,
            pltpu.VMEM((8, cells, width), F32),
            pltpu.SemaphoreType.DMA((5,)),
        ],
        hbm=True,
        flops=2_000_000_000,
    )
    greetings = share_base(greeting, last=(chans,))
    scratch = [
        pltpu.VMEM((12, BLOCK // 2, LANES), F32),
        pltpu.VMEM((2, 12, BLOCK // 2, LANES), F32),
        pltpu.VMEM((12, BLOCK // 2, LANES), F32),
    ]

    gains, message = call(
        functools.partial(first_kernel, count),
        (*greetings, keys, products),
        [narrow, terms],
        scratch,
    )
    z, pen, scale, select = call(
        functools.partial(state_kernel, count, blocks, intervals),
        (*greetings, keys, at, gains, chans),
        [wide, single, single, shape(2 * LANES, count * LANES, dtype=BF16)],
    )
    pieces = share_base(message, last=(scale,))
    gains, message = call(
        functools.partial(step_kernel, count),
        (*pieces, select, z, pen, scale, products),
        [wide, terms],
        scratch,
    )
    (part,) = call(first_total_kernel, (gains, basis), [shape(GAIN_ROWS + KPAD, LANES)])
    z, dual, inverse = call(
        first_consensus_kernel, (*sum_band(part), gains, basis), [wide, wide, narrow]
    )
    pieces = share_base(message, last=(z,), ties=(1, 2), ahead=True)
    gains, message = call(
        functools.partial(step_kernel, count),
        (*pieces, select, z, pen, scale, products),
        [wide, terms],
        scratch,
    )
    (part,) = call(total_kernel, (gains, dual, basis), [narrow])
    z, dual = call(consensus_kernel, (*sum_band(part), gains, dual, basis, inverse), [wide, wide])
    pieces = share_base(message, last=(z,), ties=(1, 2), ahead=True)
    gains, part = call(
        functools.partial(last_kernel, count),
        (*pieces, select, z, pen, scale, dual, basis),
        [narrow, shape(GAIN_ROWS // 2, LANES)],
    )
    parts = share_band(part)
    (out,) = call(
        functools.partial(gains_kernel, blocks, intervals),
        (gains,),
        [shape(8, intervals, owned)],
    )
    (coefficients,) = call(
        functools.partial(coefficient_kernel, bands, blocks),
        (*parts, inverse),
        [shape(NPOLY, 8, owned)],
    )
    return (out, jnp.transpose(coefficients, (1, 0, 2)))


def solution(mesh):
    in_specs = (
        P(None, "base", "band", None),
        P(None, "base", "band", None),
        P(None, "band", "base"),
        P("base"),
        P("base", None),
        P("base", None),
        P("band"),
    )
    out_specs = (P(None, "band", "base"), P(None, None, "base"))
    return jax.shard_map(
        on_device, mesh=mesh, in_specs=in_specs, out_specs=out_specs, check_vma=False
    )
```

```python
import functools

import jax
import jax.numpy as jnp
from jax import lax
from jax.experimental import pallas as pl
from jax.experimental.pallas import tpu as pltpu
from jax.sharding import PartitionSpec as P

BLOCK = 16
NPOLY = 9
KPAD = 16
ITERS = 3
LANES = 128
F32 = jnp.float32
BF16 = jnp.bfloat16
HIGH = lax.Precision.HIGHEST

ridge = 0.5

GAIN_ROWS = 8 * BLOCK
TERM_ROWS = 12 * BLOCK
PRODUCTS = 48
CROSS = ((0, 1), (0, 2), (0, 3), (1, 2), (1, 3), (2, 3))


def nt(left, right, **kw):
    return lax.dot_general(
        left, right, (((1,), (1,)), ((), ())), preferred_element_type=F32, **kw
    )


def nn(left, right, **kw):
    return lax.dot_general(
        left, right, (((1,), (0,)), ((), ())), preferred_element_type=F32, **kw
    )


def pick(values, select, dot=nt):
    high = values.astype(BF16)
    low = (values - high.astype(F32)).astype(BF16)
    rows = values.shape[0]
    out = dot(jnp.concatenate([high, low], 0), select)
    return out[:rows] + out[rows:]


def iota(shape, axis):
    return lax.broadcasted_iota(jnp.int32, shape, axis)


def add(terms):
    total = None
    for sign, x, y in terms:
        if total is None:
            total = x * y if sign > 0 else -(x * y)
        else:
            total = total + x * y if sign > 0 else total - x * y
    return total


def apply_gains(pairs, gains, turned):
    re, im = [], []
    for r in range(2):
        for c in range(2):
            to_re, to_im = [], []
            for k in range(2):
                for n in range(2):
                    x_re, x_im = pairs(k, r, n, c) if turned else pairs(r, k, c, n)
                    g_re, g_im = gains[2 * k + n], gains[4 + 2 * k + n]
                    sign = -1 if turned else 1
                    to_re += [(1, x_re, g_re), (-sign, x_im, g_im)]
                    to_im += [(1, x_re, g_im), (sign, x_im, g_re)]
            re.append(add(to_re))
            im.append(add(to_im))
    return re + im


def square(gains):
    return [
        add([(1, gains[n], gains[n]) for n in (0, 2, 4, 6)]),
        add([(1, gains[n], gains[n]) for n in (1, 3, 5, 7)]),
        add([(1, gains[n], gains[n + 1]) for n in (0, 2, 4, 6)]),
        add([(1, gains[0], gains[5]), (-1, gains[4], gains[1])])
        + add([(1, gains[2], gains[7]), (-1, gains[6], gains[3])]),
    ]


def outer_first(own, cross, q):
    out = []
    for r in range(2):
        x_re, x_im = cross(r, 0, r, 1)
        twice = add([(1, x_re, q[2]), (-1, x_im, q[3])])
        out.append(add([(1, own[r][0], q[0]), (1, own[r][1], q[1])]) + (twice + twice))
    (a_re, a_im), (b_re, b_im) = cross(0, 0, 1, 0), cross(0, 1, 1, 1)
    (c_re, c_im), (d_re, d_im) = cross(0, 0, 1, 1), cross(0, 1, 1, 0)
    out.append(
        add([(1, a_re, q[0]), (1, b_re, q[1]), (1, c_re + d_re, q[2]), (-1, c_im - d_im, q[3])])
    )
    out.append(
        add([(1, a_im, q[0]), (1, b_im, q[1]), (1, c_im + d_im, q[2]), (1, c_re - d_re, q[3])])
    )
    return out


def outer_second(own, cross, q):
    out = []
    for c in range(2):
        x_re, x_im = cross(0, c, 1, c)
        twice = add([(1, x_re, q[2]), (1, x_im, q[3])])
        out.append(add([(1, own[0][c], q[0]), (1, own[1][c], q[1])]) + (twice + twice))
    (a_re, a_im), (b_re, b_im) = cross(0, 0, 0, 1), cross(1, 0, 1, 1)
    (c_re, c_im), (d_re, d_im) = cross(0, 0, 1, 1), cross(0, 1, 1, 0)
    out.append(
        add([(1, a_re, q[0]), (1, b_re, q[1]), (1, c_re + d_re, q[2]), (1, c_im + d_im, q[3])])
    )
    out.append(
        add([(-1, a_im, q[0]), (-1, b_im, q[1]), (1, c_re - d_re, q[3]), (-1, c_im - d_im, q[2])])
    )
    return out


def slot_key(index, pairs, scale, intervals):
    at = index // intervals
    tiles = len(pairs)
    block = jnp.zeros(index.shape, F32)
    for slot in range(2 * tiles):
        value = pairs[slot % tiles][slot // tiles]
        block = jnp.where(at == slot, value.astype(F32), block)
    if scale > 1:
        block = block * scale + (index % intervals).astype(F32)
    return block


def scalar_pairs(pair_ref):
    return [[pair_ref[t, side] for side in range(2)] for t in range(pair_ref.shape[0])]


def owner_key(index, me, blocks, intervals, none, scale=None):
    at = index // intervals
    key = me * blocks + at
    if scale != 1:
        key = key * intervals + index % intervals
    return jnp.where(at < blocks, key, none).astype(F32)


def cell_weights(pairs, flags):
    cells = flags.shape[1]
    cell = iota((1, cells), 1)
    diagonal = (cell // BLOCK == cell % BLOCK).astype(F32)
    rows = []
    for t, pair in enumerate(pairs):
        same = (pair[0] == pair[1]).astype(F32)
        rows.append(flags[t : t + 1, :] * (1.0 - same * diagonal))
    return rows


def greet_kernel(
    blocks, intervals, pair_hbm, start_hbm, penalty_hbm, flag_hbm, out_ref, pair_ref, start_ref,
    penalty_ref, flag_ref, sems
):
    copies = [
        pltpu.make_async_copy(source, target, sems.at[n])
        for n, (source, target) in enumerate(
            [
                (start_hbm, start_ref),
                (pair_hbm, pair_ref),
                (flag_hbm, flag_ref),
                (penalty_hbm, penalty_ref),
            ]
        )
    ]
    for copy in copies:
        copy.start()
    for copy in copies[1:]:
        copy.wait()
    owned = blocks * BLOCK
    cells = flag_ref.shape[1]
    me = lax.axis_index("base")
    pairs = scalar_pairs(pair_ref)
    tiles = len(pairs)
    weights = cell_weights(pairs, flag_ref[...].astype(F32))
    lane = iota((cells, LANES), 1)
    cell = iota((cells, LANES), 0)
    at, inside = lane // BLOCK, lane % BLOCK
    member = jnp.where(at < tiles, cell // BLOCK, cell % BLOCK) == inside
    station_w = jnp.zeros((8, LANES), F32)
    for t in range(tiles):
        fold = (member & (at % tiles == t) & (at < 2 * tiles)).astype(BF16)
        station_w = station_w + nn(jnp.broadcast_to(weights[t], (8, cells)).astype(BF16), fold)
    lane = iota((8, LANES), 1)
    row = iota((8, LANES), 0)
    wide = intervals // BLOCK
    slot_at = jnp.where(lane // BLOCK < 2 * tiles, slot_key(lane * wide, pairs, 1, intervals), -2.0)
    owner_at = jnp.where(lane // BLOCK < blocks, (me * blocks + lane // BLOCK).astype(F32), -2.0)
    keys = jnp.where(row == 0, slot_key(lane, pairs, intervals, intervals), 0.0)
    keys = jnp.where(row == 1, owner_key(lane, me, blocks, intervals, -2), keys)
    keys = jnp.where(row == 3, owner_at, keys)
    keys = jnp.where(row == 4, station_w, keys)
    out_ref[GAIN_ROWS:, :] = jnp.where(row == 5, slot_at, keys)
    out_ref[GAIN_ROWS + 2 : GAIN_ROWS + 3, :owned] = penalty_ref[...]
    copies[0].wait()
    place = (iota((BLOCK, owned), 0) == iota((BLOCK, owned), 1) % BLOCK).astype(BF16)
    here = iota((LANES, owned), 0) // intervals == iota((LANES, owned), 1) // BLOCK
    for m in range(8):
        plane = start_ref[m]
        plane = jnp.where(here, jnp.concatenate([plane] * (LANES // intervals), 0), 0.0)
        high = plane.astype(BF16)
        low = (plane - high.astype(F32)).astype(BF16)
        out_ref[m * BLOCK : (m + 1) * BLOCK, :] = nt(place, high) + nt(place, low)


def prepare_kernel(
    blocks, intervals, bands, pair_hbm, chan_hbm, flag_hbm, vis_hbm, model_hbm, prod_ref, key_ref,
    at_ref, basis_ref, chans_ref, pair_ref, chan_ref, flag_ref, vis_ref, model_ref, mt_ref, sems
):
    planes, width, cells = vis_ref.shape
    moves = [
        (model_hbm, model_ref),
        (vis_hbm, vis_ref),
        (pair_hbm, pair_ref),
        (chan_hbm, chan_ref),
        (flag_hbm, flag_ref),
    ]
    copies = [
        pltpu.make_async_copy(source, target, sems.at[n])
        for n, (source, target) in enumerate(moves)
    ]
    for copy in copies:
        copy.start()
    for copy in copies[2:]:
        copy.wait()
    pairs = scalar_pairs(pair_ref)
    tiles = len(pairs)
    channels = width // tiles
    me = lax.axis_index("base")
    row = iota((2 * LANES, LANES), 0)
    lane = iota((2 * LANES, LANES), 1)
    for ref, scale in ((key_ref, intervals), (at_ref, 1)):
        ref[...] = jnp.where(
            row < LANES,
            slot_key(row, pairs, scale, intervals),
            owner_key(row - LANES, me, blocks, intervals, -1, scale),
        )
    band_at = lax.axis_index("band")
    local = chan_ref[...] - band_at * intervals
    chan = (band_at * channels + iota((1, channels), 1)).astype(F32)
    xpos = -1.0 + (2.0 * chan + 1.0) / (channels * bands)
    member = (iota((2 * LANES, channels), 0) % intervals == local).astype(F32)
    chans = jnp.sum(member, 1, keepdims=True)
    chans_ref[...] = nt(jnp.ones((8, channels), BF16), member.astype(BF16))
    centre = jnp.sum(member * xpos, 1, keepdims=True) / chans
    terms = [jnp.ones((2 * LANES, LANES), F32), jnp.broadcast_to(centre, (2 * LANES, LANES))]
    for order in range(2, NPOLY):
        terms.append(2.0 * terms[1] * terms[-1] - terms[-2])
    basis = jnp.zeros((2 * LANES, LANES), F32)
    for order in range(NPOLY):
        basis = jnp.where(lane % KPAD == order, terms[order], basis)
    basis_ref[...] = jnp.where(row // intervals == lane // KPAD, basis, 0.0)
    lanes = 2 * tiles * intervals
    row = iota((lanes, 2 * width), 0)
    lane = iota((lanes, 2 * width), 1)
    at = jnp.concatenate([local] * (2 * tiles), 1)
    fold = ((row // intervals == lane // channels) & (row % intervals == at)).astype(BF16)
    ident = (iota((cells, cells), 0) == iota((cells, cells), 1)).astype(BF16)
    rows = cell_weights(pairs, flag_ref[...].astype(F32))
    weight = jnp.concatenate([jnp.broadcast_to(w, (channels, cells)) for w in rows], 0)
    half = cells // 2

    def put(at, product):
        beside = jnp.concatenate([product[:half], product[half:]], 1)
        prod_ref[at] = pick(beside, fold).reshape(prod_ref.shape[1:])

    copies[0].wait()
    for m in range(planes):
        masked = (model_ref[m].astype(F32) * weight).astype(BF16)
        mt_ref[m] = nt(ident, masked)
    for x in range(4):
        put(32 + x, mt_ref[x] * mt_ref[x] + mt_ref[4 + x] * mt_ref[4 + x])
    for n, (x, y) in enumerate(CROSS):
        x_re, x_im, y_re, y_im = mt_ref[x], mt_ref[4 + x], mt_ref[y], mt_ref[4 + y]
        put(36 + n, x_re * y_re + x_im * y_im)
        put(42 + n, x_im * y_re - x_re * y_im)
    copies[1].wait()
    for x in range(4):
        v_re, v_im = nt(ident, vis_ref[x]), nt(ident, vis_ref[4 + x])
        for y in range(4):
            m_re, m_im = mt_ref[y], mt_ref[4 + y]
            put(4 * x + y, v_re * m_re + v_im * m_im)
            put(16 + 4 * x + y, v_im * m_re - v_re * m_im)


def tie_kernel(*refs):
    pass


def after(values, others, flops=0):
    place = pl.BlockSpec(memory_space=pl.ANY)
    return pl.pallas_call(
        tie_kernel,
        out_shape=[jax.ShapeDtypeStruct(x.shape, x.dtype) for x in values],
        in_specs=[place] * (len(values) + len(others)),
        out_specs=[place] * len(values),
        input_output_aliases={n: n for n in range(len(values))},
        compiler_params=pltpu.CompilerParams(vmem_limit_bytes=1024 * 1024),
        cost_estimate=pl.CostEstimate(flops=flops, bytes_accessed=0, transcendentals=0),
    )(*values, *others)


def normal_terms(gains, prod_ref, first_s, second_s, a_s, out_ref):
    half = BLOCK // 2
    low = iota((half, LANES), 1) < LANES // 2

    def swap(x):
        return pltpu.roll(x, LANES // 2, 1)

    first, second = [], [[], []]
    for m in range(8):
        part = [gains[m * BLOCK + h * half : m * BLOCK + (h + 1) * half] for h in range(2)]
        first.append(jnp.where(low, part[0], swap(part[1])))
        for h in range(2):
            second[h].append(jnp.where(low, swap(part[h]), part[h]))
    for n, x in enumerate(first + square(first)):
        first_s[n] = x
    for h in range(2):
        for n, x in enumerate(second[h] + square(second[h])):
            second_s[h, n] = x

    def step(i, totals):
        partial = None
        new = []
        one = [first_s[n, pl.ds(i, 1), :] for n in range(12)]
        for h in range(2):
            two = [second_s[h, n] for n in range(12)]

            def load(n):
                return prod_ref[n, i, h * half : (h + 1) * half, :]

            def pairs(r, k, c, n):
                at = (2 * r + k) * 4 + 2 * c + n
                return load(at), load(16 + at)

            def cross(r, k, c, n):
                at = CROSS.index((2 * r + k, 2 * c + n))
                return load(36 + at), load(42 + at)

            own = [[load(32 + 2 * r + k) for k in range(2)] for r in range(2)]
            terms = apply_gains(pairs, two[:8], False) + outer_first(own, cross, two[8:])
            partial = terms if partial is None else [x + y for x, y in zip(partial, terms)]
            terms = apply_gains(pairs, one[:8], True) + outer_second(own, cross, one[8:])
            new += [x + y for x, y in zip(totals[12 * h : 12 * (h + 1)], terms)]
        for k in range(12):
            a_s[k, pl.ds(i, 1), :] = jnp.sum(partial[k], 0, keepdims=True)
        return tuple(new)

    zero = jnp.zeros((half, LANES), F32)
    totals = lax.fori_loop(0, half, step, (zero,) * 24, unroll=4)
    for k in range(12):
        mine = a_s[k]
        for h in range(2):
            other = totals[12 * h + k]
            other = other + swap(other)
            at = k * BLOCK + h * half
            out_ref[at : at + half, :] = jnp.where(low, swap(mine) if h else mine, other)


def key_match(rows, lanes):
    count = lanes.shape[1] // LANES
    return (jnp.concatenate([rows] * count, 1) == lanes).astype(BF16)


def beside(refs, count):
    return jnp.concatenate([p[...] for p in refs[:count]], 1), refs[count:]


def first_kernel(count, *refs):
    every, refs = beside(refs, count)
    key_ref, prod_ref, gains_ref, out_ref = refs[:4]
    scratch = refs[4:]
    select = key_match(key_ref[:LANES, :], every[GAIN_ROWS + 1 : GAIN_ROWS + 2])
    gains = pick(every[:GAIN_ROWS], select)
    gains_ref[...] = gains
    normal_terms(gains, prod_ref, *scratch, out_ref)


def state_kernel(count, blocks, intervals, *refs):
    every, refs = beside(refs, count)
    key_ref, at_ref, gains_ref, chans_ref, basis_ref = refs[:5]
    z_ref, pen_ref, scale_ref, select_ref, turned_ref = refs[5:]
    place = (iota((KPAD, LANES), 0) == iota((KPAD, LANES), 1) % KPAD).astype(BF16)
    for n, piece in enumerate(split(turn(place, basis_ref[LANES:, :]))):
        turned_ref[n * KPAD : (n + 1) * KPAD, :] = piece
    rows = every[GAIN_ROWS:]
    z_ref[:, :LANES] = gains_ref[...]
    z_ref[:, LANES:] = every[:GAIN_ROWS, :LANES]
    select_ref[...] = key_match(key_ref[...], rows[0:1])
    lanes = rows.shape[1]
    diagonal = iota((BLOCK, lanes), 0) == iota((BLOCK, lanes), 1) % BLOCK
    at = at_ref[...]
    pen = pick(jnp.where(diagonal, rows[2:3], 0.0), key_match(at, rows[3:4]))
    unused = iota(pen.shape, 1) >= LANES + blocks * intervals
    pen_ref[...] = jnp.where(unused, 1.0, pen)
    weights = pick(jnp.where(diagonal, rows[4:5], 0.0), key_match(at, rows[5:6]))
    scale_ref[...] = 1.0 / jnp.maximum(weights * chans_ref[0:1, :], 1.0)


def solve(normal, scale, pen, consensus):
    part = [normal[BLOCK * k : BLOCK * (k + 1)] * scale for k in range(12)]
    rhs = [part[m] + pen * consensus[BLOCK * m : BLOCK * (m + 1)] for m in range(8)]
    h_first = part[8] + pen
    h_second = part[9] + pen
    h_real, h_imag = part[10], part[11]
    determ = h_first * h_second - h_real * h_real - h_imag * h_imag
    over = 1.0 / determ
    d_first, d_second = h_first * over, h_second * over
    d_real, d_imag = h_real * over, h_imag * over
    out = [None] * 8
    for r in range(2):
        x_re, y_re = rhs[2 * r], rhs[2 * r + 1]
        x_im, y_im = rhs[4 + 2 * r], rhs[5 + 2 * r]
        out[2 * r] = x_re * d_second - (y_re * d_real + y_im * d_imag)
        out[4 + 2 * r] = x_im * d_second - (y_im * d_real - y_re * d_imag)
        out[2 * r + 1] = y_re * d_first - (x_re * d_real - x_im * d_imag)
        out[5 + 2 * r] = y_im * d_first - (x_im * d_real + x_re * d_imag)
    return jnp.concatenate(out, 0)


def step_kernel(count, *refs):
    every, refs = beside(refs, count)
    select_ref, z_ref, pen_ref, scale_ref, prod_ref, gains_ref, out_ref = refs[:7]
    scratch = refs[7:]
    normal = pick(every, select_ref[...])
    gains = solve(normal, scale_ref[...], pen_ref[...], z_ref[...])
    gains_ref[...] = gains
    normal_terms(gains[:, :LANES], prod_ref, *scratch, out_ref)


def first_total_kernel(gains_ref, basis_ref, out_ref):
    basis = basis_ref[...]
    total = nn(gains_ref[...], basis, precision=HIGH)
    part = basis[: basis.shape[0] // 8]
    gram = lax.dot_general(
        part, part, (((0,), (0,)), ((), ())), preferred_element_type=F32, precision=HIGH
    )
    out_ref[:GAIN_ROWS, :] = total
    out_ref[GAIN_ROWS:, :] = gram[:KPAD]


def total_kernel(gains_ref, dual_ref, basis_ref, out_ref):
    out_ref[...] = nn(gains_ref[...] + dual_ref[...], basis_ref[...], precision=HIGH)


def inverse_of_three(d):
    def minor(r, c):
        (r0, r1), (c0, c1) = [[k for k in range(3) if k != n] for n in (r, c)]
        value = d[r0][c0] * d[r1][c1] - d[r0][c1] * d[r1][c0]
        return value if (r + c) % 2 == 0 else -value

    minors = [[minor(r, c) for c in range(3)] for r in range(3)]
    over = 1.0 / (d[0][0] * minors[0][0] + d[0][1] * minors[0][1] + d[0][2] * minors[0][2])
    return [[minors[c][r] * over for c in range(3)] for r in range(3)]


def invert(gram):
    row, lane = iota(gram.shape, 0), iota(gram.shape, 1)
    inner = (row < NPOLY) & (lane < NPOLY)
    work = jnp.where(inner, gram + jnp.where(row == lane, ridge, 0.0), 0.0)
    lanes = iota((1, gram.shape[1]), 1)
    for p in range(0, NPOLY, 3):
        rows = [work[p + a : p + a + 1] for a in range(3)]
        block = inverse_of_three(
            [
                [jnp.broadcast_to(rows[a][:, p + b : p + b + 1], lanes.shape) for b in range(3)]
                for a in range(3)
            ]
        )
        columns = [work[:, p + b : p + b + 1] for b in range(3)]
        here = (lane >= p) & (lane < p + 3)
        rows = [jnp.where(here[:1], 0.0, x) for x in rows]
        pivots = []
        for a in range(3):
            pivot = block[a][0] * rows[0] + block[a][1] * rows[1] + block[a][2] * rows[2]
            for b in range(3):
                pivot = jnp.where(lanes == p + b, block[a][b], pivot)
            pivots.append(pivot)
        work = jnp.where(here, 0.0, work)
        for b in range(3):
            work = work - columns[b] * pivots[b]
        for a in range(3):
            work = jnp.where(row == p + a, pivots[a], work)
    return work


def settle(total, inverse, basis_ref, gains, z_ref, dual_ref):
    coeff = nn(total, inverse, precision=HIGH)
    consensus = nt(coeff, basis_ref[...], precision=HIGH)
    z_ref[...] = 2.0 * consensus - gains
    dual_ref[...] = gains - consensus


def band_total(refs):
    totals = [ref[...] for ref in refs]
    while len(totals) > 1:
        totals = [totals[n] + totals[n + 1] for n in range(0, len(totals), 2)]
    return totals[0]


def first_consensus_kernel(
    one_ref, two_ref, gains_ref, basis_ref, z_ref, dual_ref, inverse_ref
):
    total = one_ref[...] + two_ref[...]
    small = invert(total[GAIN_ROWS:])
    row, lane = iota((LANES, LANES), 0), iota((LANES, LANES), 1)
    spread = ((row == lane % KPAD) & (row < KPAD)).astype(F32)
    wide = nn(jnp.concatenate([small] * (LANES // KPAD), 0), spread, precision=HIGH)
    inverse = jnp.where(row // KPAD == lane // KPAD, wide, 0.0)
    inverse_ref[...] = inverse
    settle(total[:GAIN_ROWS], inverse, basis_ref, gains_ref[...], z_ref, dual_ref)


def consensus_kernel(
    one_ref, two_ref, gains_ref, old_ref, basis_ref, inverse_ref, z_ref, dual_ref
):
    total = one_ref[...] + two_ref[...]
    gains = gains_ref[...] + old_ref[...]
    settle(total, inverse_ref[...], basis_ref, gains, z_ref, dual_ref)


def last_kernel(count, blocks, intervals, *refs):
    every, refs = beside(refs, count)
    select_ref, z_ref, pen_ref, scale_ref, dual_ref, turned_ref, gains_ref, out_ref = refs
    own = slice(LANES, 2 * LANES)
    normal = pick(every, select_ref[own, :])
    gains = solve(normal, scale_ref[:, own], pen_ref[:, own], z_ref[:, own])
    gains_ref[...] = gains
    owned = blocks * BLOCK
    here = iota((owned, LANES), 0) // BLOCK == iota((owned, LANES), 1) // intervals
    summed = gains + dual_ref[:, own]
    parts = [summed[m * BLOCK : (m + 1) * BLOCK] for m in range(8)]
    parts = [jnp.where(here, jnp.concatenate([x] * blocks, 0), 0.0) for x in parts]
    high, mid, low = split(jnp.concatenate(parts, 0))
    turned = turned_ref[...]
    first, second = nt(turned, high), nt(turned[: 2 * KPAD], mid)
    small = first[2 * KPAD :] + second[KPAD:] + nt(turned[:KPAD], low)
    total = first[:KPAD] + ((first[KPAD : 2 * KPAD] + second[:KPAD]) + small)
    chunks = total.shape[1] // LANES
    for c in range(chunks):
        lanes = slice(c * LANES, (c + 1) * LANES)
        out_ref[8 * c : 8 * c + 8, :] = total[:8, lanes]
        out_ref[8 * chunks + c : 8 * chunks + c + 1, :] = total[8:9, lanes]
    rest = 9 * chunks
    out_ref[rest:, :] = jnp.zeros((out_ref.shape[0] - rest, LANES), F32)


def gains_kernel(blocks, intervals, gains_ref, out_ref):
    owned = blocks * BLOCK
    place = (iota((intervals, LANES), 0) == iota((intervals, LANES), 1) % intervals).astype(BF16)
    here = iota((owned, LANES), 0) // BLOCK == iota((owned, LANES), 1) // intervals
    for m in range(8):
        part = gains_ref[m * BLOCK : (m + 1) * BLOCK, :]
        out_ref[m] = turn(place, jnp.where(here, jnp.concatenate([part] * blocks, 0), 0.0))


def split(values):
    high = values.astype(BF16)
    rest = values - high.astype(F32)
    mid = rest.astype(BF16)
    return high, mid, (rest - mid.astype(F32)).astype(BF16)


def turn(place, values):
    high, mid, low = split(values)
    return (nt(place, high) + nt(place, mid)) + nt(place, low)


def coefficient_kernel(bands, *refs):
    inverse_ref, out_ref = refs[bands:]
    total = band_total(refs[:bands])
    owned = out_ref.shape[2]
    chunks = 8 * owned // LANES
    inverse = inverse_ref[:KPAD, :KPAD]
    eight = jnp.concatenate([total[8 * c : 8 * c + 8] for c in range(chunks)], 1)
    ninth = jnp.concatenate([total[8 * chunks + c : 8 * chunks + c + 1] for c in range(chunks)], 1)
    coeff = nn(inverse[:, :8], eight, precision=HIGH) + inverse[:, 8:9] * ninth
    for m in range(8):
        out_ref[:, m, :] = coeff[:NPOLY, m * owned : (m + 1) * owned]


def call(kernel, operands, shapes, scratch=(), hbm=False, flops=20_000_000):
    vmem = pl.BlockSpec(memory_space=pltpu.VMEM)
    in_specs = [vmem] * len(operands)
    moved = sum(x.size * x.dtype.itemsize for x in (*operands, *shapes))
    if hbm:
        in_specs = [pl.BlockSpec(memory_space=pltpu.HBM)] * len(operands)
        operands = [pltpu.with_memory_space_constraint(x, pltpu.HBM) for x in operands]
    return pl.pallas_call(
        kernel,
        out_shape=shapes,
        in_specs=in_specs,
        out_specs=[vmem] * len(shapes),
        scratch_shapes=list(scratch),
        compiler_params=pltpu.CompilerParams(vmem_limit_bytes=14 * 1024 * 1024),
        cost_estimate=pl.CostEstimate(flops=flops, bytes_accessed=moved, transcendentals=0),
    )(*operands)


def share_base(x, last=(), ties=(2,), ahead=False):
    devices = lax.axis_size("base")
    mine = [x] + [
        lax.ppermute(x, "base", [(d, d ^ (2 * k)) for d in range(devices)])
        for k in range(1, devices // 2)
    ]
    if ahead:
        mine[3:] = after(mine[3:], (), flops=5_000_000_000)
    if last:
        for k, y in zip(ties, after([mine[k] for k in ties], last)):
            mine[k] = y
    other = [lax.ppermute(y, "base", [(d, d ^ 1) for d in range(devices)]) for y in mine]
    return mine + other


def share_band(x):
    devices = lax.axis_size("band")
    return [x] + [
        lax.ppermute(x, "band", [(d, d ^ k) for d in range(devices)]) for k in range(1, devices)
    ]


def sum_band(x):
    devices = lax.axis_size("band")
    step = 1
    while 2 * step < devices:
        x = x + lax.ppermute(x, "band", [(d, d ^ step) for d in range(devices)])
        step = 2 * step
    return x, lax.ppermute(x, "band", [(d, d ^ step) for d in range(devices)])


def on_device(visibilities, model, start_gains, penalty, pairs, flags, chan_band):
    tiles, channels, cells = visibilities.shape[1:]
    intervals = start_gains.shape[1]
    owned = start_gains.shape[2]
    blocks = owned // BLOCK
    count = lax.axis_size("base")
    bands = lax.axis_size("band")
    width = tiles * channels

    def shape(*extent, dtype=F32):
        return jax.ShapeDtypeStruct(extent, dtype)

    wide = shape(GAIN_ROWS, 2 * LANES)
    narrow = shape(GAIN_ROWS, LANES)
    single = shape(BLOCK, 2 * LANES)
    terms = shape(TERM_ROWS, LANES)
    square = shape(2 * LANES, LANES)

    (greeting,) = call(
        functools.partial(greet_kernel, blocks, intervals),
        (pairs, start_gains, penalty.reshape(1, owned), flags),
        [shape(GAIN_ROWS + 8, LANES)],
        [
            pltpu.SMEM(pairs.shape, jnp.int32),
            pltpu.VMEM(start_gains.shape, F32),
            pltpu.VMEM((1, owned), F32),
            pltpu.VMEM(flags.shape, jnp.int32),
            pltpu.SemaphoreType.DMA((4,)),
        ],
        hbm=True,
    )
    products, keys, at, basis, chans = call(
        functools.partial(prepare_kernel, blocks, intervals, bands),
        (
            pairs,
            chan_band.reshape(1, channels),
            flags,
            visibilities.reshape(8, width, cells),
            model.reshape(8, width, cells),
        ),
        [
            shape(PRODUCTS, BLOCK // 2, BLOCK, 2 * tiles * intervals),
            square,
            square,
            square,
            shape(8, 2 * LANES),
        ],
        [
            pltpu.SMEM(pairs.shape, jnp.int32),
            pltpu.VMEM((1, channels), jnp.int32),
            pltpu.VMEM(flags.shape, jnp.int32),
            *[pltpu.VMEM((8, width, cells), BF16)] * 2,
            pltpu.VMEM((8, cells, width), F32),
            pltpu.SemaphoreType.DMA((5,)),
        ],
        hbm=True,
        flops=2_000_000_000,
    )
    greetings = share_base(greeting, last=(chans,))
    scratch = [
        pltpu.VMEM((12, BLOCK // 2, LANES), F32),
        pltpu.VMEM((2, 12, BLOCK // 2, LANES), F32),
        pltpu.VMEM((12, BLOCK // 2, LANES), F32),
    ]

    gains, message = call(
        functools.partial(first_kernel, count),
        (*greetings, keys, products),
        [narrow, terms],
        scratch,
    )
    z, pen, scale, select, turned = call(
        functools.partial(state_kernel, count, blocks, intervals),
        (*greetings, keys, at, gains, chans, basis),
        [
            wide,
            single,
            single,
            shape(2 * LANES, count * LANES, dtype=BF16),
            shape(3 * KPAD, LANES, dtype=BF16),
        ],
    )
    pieces = share_base(message, last=(scale,), ahead=True)
    gains, message = call(
        functools.partial(step_kernel, count),
        (*pieces, select, z, pen, scale, products),
        [wide, terms],
        scratch,
    )
    (part,) = call(first_total_kernel, (gains, basis), [shape(GAIN_ROWS + KPAD, LANES)])
    z, dual, inverse = call(
        first_consensus_kernel, (*sum_band(part), gains, basis), [wide, wide, narrow]
    )
    pieces = share_base(message, last=(z,), ties=(1, 2), ahead=True)
    gains, message = call(
        functools.partial(step_kernel, count),
        (*pieces, select, z, pen, scale, products),
        [wide, terms],
        scratch,
    )
    (part,) = call(total_kernel, (gains, dual, basis), [narrow])
    z, dual = call(consensus_kernel, (*sum_band(part), gains, dual, basis, inverse), [wide, wide])
    pieces = share_base(message, last=(z,), ties=(1, 2), ahead=True)
    chunks = 8 * owned // LANES
    gains, part = call(
        functools.partial(last_kernel, count, blocks, intervals),
        (*pieces, select, z, pen, scale, dual, turned),
        [narrow, shape(8 * chunks + -(-chunks // 8) * 8, LANES)],
    )
    parts = share_band(part)
    (out,) = call(
        functools.partial(gains_kernel, blocks, intervals),
        (gains,),
        [shape(8, intervals, owned)],
    )
    (coefficients,) = call(
        functools.partial(coefficient_kernel, bands),
        (*parts, inverse),
        [shape(NPOLY, 8, owned)],
    )
    return (out, jnp.transpose(coefficients, (1, 0, 2)))


def solution(mesh):
    in_specs = (
        P(None, "base", "band", None),
        P(None, "base", "band", None),
        P(None, "band", "base"),
        P("base"),
        P("base", None),
        P("base", None),
        P("band"),
    )
    out_specs = (P(None, "band", "base"), P(None, None, "base"))
    return jax.shard_map(
        on_device, mesh=mesh, in_specs=in_specs, out_specs=out_specs, check_vma=False
    )
```

```python
import functools

import jax
import jax.numpy as jnp
from jax import lax
from jax.experimental import pallas as pl
from jax.experimental.pallas import tpu as pltpu
from jax.sharding import PartitionSpec as P

BLOCK = 16
NPOLY = 9
KPAD = 16
ITERS = 3
LANES = 128
F32 = jnp.float32
BF16 = jnp.bfloat16
HIGH = lax.Precision.HIGHEST

ridge = 0.5

GAIN_ROWS = 8 * BLOCK
TERM_ROWS = 12 * BLOCK
PRODUCTS = 48
CROSS = ((0, 1), (0, 2), (0, 3), (1, 2), (1, 3), (2, 3))


def nt(left, right, **kw):
    return lax.dot_general(
        left, right, (((1,), (1,)), ((), ())), preferred_element_type=F32, **kw
    )


def nn(left, right, **kw):
    return lax.dot_general(
        left, right, (((1,), (0,)), ((), ())), preferred_element_type=F32, **kw
    )


def pick(values, select, dot=nt):
    high = values.astype(BF16)
    low = (values - high.astype(F32)).astype(BF16)
    rows = values.shape[0]
    out = dot(jnp.concatenate([high, low], 0), select)
    return out[:rows] + out[rows:]


def iota(shape, axis):
    return lax.broadcasted_iota(jnp.int32, shape, axis)


def add(terms):
    total = None
    for sign, x, y in terms:
        if total is None:
            total = x * y if sign > 0 else -(x * y)
        else:
            total = total + x * y if sign > 0 else total - x * y
    return total


def apply_gains(pairs, gains, turned):
    re, im = [], []
    for r in range(2):
        for c in range(2):
            to_re, to_im = [], []
            for k in range(2):
                for n in range(2):
                    x_re, x_im = pairs(k, r, n, c) if turned else pairs(r, k, c, n)
                    g_re, g_im = gains[2 * k + n], gains[4 + 2 * k + n]
                    sign = -1 if turned else 1
                    to_re += [(1, x_re, g_re), (-sign, x_im, g_im)]
                    to_im += [(1, x_re, g_im), (sign, x_im, g_re)]
            re.append(add(to_re))
            im.append(add(to_im))
    return re + im


def square(gains):
    return [
        add([(1, gains[n], gains[n]) for n in (0, 2, 4, 6)]),
        add([(1, gains[n], gains[n]) for n in (1, 3, 5, 7)]),
        add([(1, gains[n], gains[n + 1]) for n in (0, 2, 4, 6)]),
        add([(1, gains[0], gains[5]), (-1, gains[4], gains[1])])
        + add([(1, gains[2], gains[7]), (-1, gains[6], gains[3])]),
    ]


def outer_first(own, cross, q):
    out = []
    for r in range(2):
        x_re, x_im = cross(r, 0, r, 1)
        twice = add([(1, x_re, q[2]), (-1, x_im, q[3])])
        out.append(add([(1, own[r][0], q[0]), (1, own[r][1], q[1])]) + (twice + twice))
    (a_re, a_im), (b_re, b_im) = cross(0, 0, 1, 0), cross(0, 1, 1, 1)
    (c_re, c_im), (d_re, d_im) = cross(0, 0, 1, 1), cross(0, 1, 1, 0)
    out.append(
        add([(1, a_re, q[0]), (1, b_re, q[1]), (1, c_re + d_re, q[2]), (-1, c_im - d_im, q[3])])
    )
    out.append(
        add([(1, a_im, q[0]), (1, b_im, q[1]), (1, c_im + d_im, q[2]), (1, c_re - d_re, q[3])])
    )
    return out


def outer_second(own, cross, q):
    out = []
    for c in range(2):
        x_re, x_im = cross(0, c, 1, c)
        twice = add([(1, x_re, q[2]), (1, x_im, q[3])])
        out.append(add([(1, own[0][c], q[0]), (1, own[1][c], q[1])]) + (twice + twice))
    (a_re, a_im), (b_re, b_im) = cross(0, 0, 0, 1), cross(1, 0, 1, 1)
    (c_re, c_im), (d_re, d_im) = cross(0, 0, 1, 1), cross(0, 1, 1, 0)
    out.append(
        add([(1, a_re, q[0]), (1, b_re, q[1]), (1, c_re + d_re, q[2]), (1, c_im + d_im, q[3])])
    )
    out.append(
        add([(-1, a_im, q[0]), (-1, b_im, q[1]), (1, c_re - d_re, q[3]), (-1, c_im - d_im, q[2])])
    )
    return out


def slot_key(index, pairs, scale, intervals):
    at = index // intervals
    tiles = len(pairs)
    block = jnp.zeros(index.shape, F32)
    for slot in range(2 * tiles):
        value = pairs[slot % tiles][slot // tiles]
        block = jnp.where(at == slot, value.astype(F32), block)
    if scale > 1:
        block = block * scale + (index % intervals).astype(F32)
    return block


def scalar_pairs(pair_ref):
    return [[pair_ref[t, side] for side in range(2)] for t in range(pair_ref.shape[0])]


def owner_key(index, me, blocks, intervals, none, scale=None):
    at = index // intervals
    key = me * blocks + at
    if scale != 1:
        key = key * intervals + index % intervals
    return jnp.where(at < blocks, key, none).astype(F32)


def cell_weights(pairs, flags):
    cells = flags.shape[1]
    cell = iota((1, cells), 1)
    diagonal = (cell // BLOCK == cell % BLOCK).astype(F32)
    rows = []
    for t, pair in enumerate(pairs):
        same = (pair[0] == pair[1]).astype(F32)
        rows.append(flags[t : t + 1, :] * (1.0 - same * diagonal))
    return rows


def greet_kernel(
    blocks, intervals, pair_hbm, start_hbm, penalty_hbm, flag_hbm, out_ref, pair_ref, start_ref,
    penalty_ref, flag_ref, sems
):
    copies = [
        pltpu.make_async_copy(source, target, sems.at[n])
        for n, (source, target) in enumerate(
            [
                (start_hbm, start_ref),
                (pair_hbm, pair_ref),
                (flag_hbm, flag_ref),
                (penalty_hbm, penalty_ref),
            ]
        )
    ]
    for copy in copies:
        copy.start()
    for copy in copies[1:]:
        copy.wait()
    owned = blocks * BLOCK
    cells = flag_ref.shape[1]
    me = lax.axis_index("base")
    pairs = scalar_pairs(pair_ref)
    tiles = len(pairs)
    weights = cell_weights(pairs, flag_ref[...].astype(F32))
    lane = iota((cells, LANES), 1)
    cell = iota((cells, LANES), 0)
    at, inside = lane // BLOCK, lane % BLOCK
    member = jnp.where(at < tiles, cell // BLOCK, cell % BLOCK) == inside
    station_w = jnp.zeros((8, LANES), F32)
    for t in range(tiles):
        fold = (member & (at % tiles == t) & (at < 2 * tiles)).astype(BF16)
        station_w = station_w + nn(jnp.broadcast_to(weights[t], (8, cells)).astype(BF16), fold)
    lane = iota((8, LANES), 1)
    row = iota((8, LANES), 0)
    wide = intervals // BLOCK
    slot_at = jnp.where(lane // BLOCK < 2 * tiles, slot_key(lane * wide, pairs, 1, intervals), -2.0)
    owner_at = jnp.where(lane // BLOCK < blocks, (me * blocks + lane // BLOCK).astype(F32), -2.0)
    keys = jnp.where(row == 0, slot_key(lane, pairs, intervals, intervals), 0.0)
    keys = jnp.where(row == 1, owner_key(lane, me, blocks, intervals, -2), keys)
    keys = jnp.where(row == 3, owner_at, keys)
    keys = jnp.where(row == 4, station_w, keys)
    out_ref[GAIN_ROWS:, :] = jnp.where(row == 5, slot_at, keys)
    out_ref[GAIN_ROWS + 2 : GAIN_ROWS + 3, :owned] = penalty_ref[...]
    copies[0].wait()
    place = (iota((BLOCK, owned), 0) == iota((BLOCK, owned), 1) % BLOCK).astype(BF16)
    here = iota((LANES, owned), 0) // intervals == iota((LANES, owned), 1) // BLOCK
    for m in range(8):
        plane = start_ref[m]
        plane = jnp.where(here, jnp.concatenate([plane] * (LANES // intervals), 0), 0.0)
        high = plane.astype(BF16)
        low = (plane - high.astype(F32)).astype(BF16)
        out_ref[m * BLOCK : (m + 1) * BLOCK, :] = nt(place, high) + nt(place, low)


def prepare_kernel(
    blocks, intervals, bands, pair_hbm, chan_hbm, flag_hbm, vis_hbm, model_hbm, prod_ref, key_ref,
    at_ref, basis_ref, chans_ref, pair_ref, chan_ref, flag_ref, vis_ref, model_ref, mt_ref, sems
):
    planes, width, cells = vis_ref.shape
    moves = [
        (model_hbm, model_ref),
        (vis_hbm, vis_ref),
        (pair_hbm, pair_ref),
        (chan_hbm, chan_ref),
        (flag_hbm, flag_ref),
    ]
    copies = [
        pltpu.make_async_copy(source, target, sems.at[n])
        for n, (source, target) in enumerate(moves)
    ]
    for copy in copies:
        copy.start()
    for copy in copies[2:]:
        copy.wait()
    pairs = scalar_pairs(pair_ref)
    tiles = len(pairs)
    channels = width // tiles
    me = lax.axis_index("base")
    row = iota((2 * LANES, LANES), 0)
    lane = iota((2 * LANES, LANES), 1)
    for ref, scale in ((key_ref, intervals), (at_ref, 1)):
        ref[...] = jnp.where(
            row < LANES,
            slot_key(row, pairs, scale, intervals),
            owner_key(row - LANES, me, blocks, intervals, -1, scale),
        )
    band_at = lax.axis_index("band")
    local = chan_ref[...] - band_at * intervals
    chan = (band_at * channels + iota((1, channels), 1)).astype(F32)
    xpos = -1.0 + (2.0 * chan + 1.0) / (channels * bands)
    member = (iota((2 * LANES, channels), 0) % intervals == local).astype(F32)
    chans = jnp.sum(member, 1, keepdims=True)
    chans_ref[...] = nt(jnp.ones((8, channels), BF16), member.astype(BF16))
    centre = jnp.sum(member * xpos, 1, keepdims=True) / chans
    terms = [jnp.ones((2 * LANES, LANES), F32), jnp.broadcast_to(centre, (2 * LANES, LANES))]
    for order in range(2, NPOLY):
        terms.append(2.0 * terms[1] * terms[-1] - terms[-2])
    basis = jnp.zeros((2 * LANES, LANES), F32)
    for order in range(NPOLY):
        basis = jnp.where(lane % KPAD == order, terms[order], basis)
    basis_ref[...] = jnp.where(row // intervals == lane // KPAD, basis, 0.0)
    lanes = 2 * tiles * intervals
    row = iota((lanes, 2 * width), 0)
    lane = iota((lanes, 2 * width), 1)
    at = jnp.concatenate([local] * (2 * tiles), 1)
    fold = ((row // intervals == lane // channels) & (row % intervals == at)).astype(BF16)
    ident = (iota((cells, cells), 0) == iota((cells, cells), 1)).astype(BF16)
    rows = cell_weights(pairs, flag_ref[...].astype(F32))
    weight = jnp.concatenate([jnp.broadcast_to(w, (channels, cells)) for w in rows], 0)
    half = cells // 2

    def put(at, product):
        beside = jnp.concatenate([product[:half], product[half:]], 1)
        prod_ref[at] = pick(beside, fold).reshape(prod_ref.shape[1:])

    copies[0].wait()
    for m in range(planes):
        masked = (model_ref[m].astype(F32) * weight).astype(BF16)
        mt_ref[m] = nt(ident, masked)
    for x in range(4):
        put(32 + x, mt_ref[x] * mt_ref[x] + mt_ref[4 + x] * mt_ref[4 + x])
    for n, (x, y) in enumerate(CROSS):
        x_re, x_im, y_re, y_im = mt_ref[x], mt_ref[4 + x], mt_ref[y], mt_ref[4 + y]
        put(36 + n, x_re * y_re + x_im * y_im)
        put(42 + n, x_im * y_re - x_re * y_im)
    copies[1].wait()
    for x in range(4):
        v_re, v_im = nt(ident, vis_ref[x]), nt(ident, vis_ref[4 + x])
        for y in range(4):
            m_re, m_im = mt_ref[y], mt_ref[4 + y]
            put(4 * x + y, v_re * m_re + v_im * m_im)
            put(16 + 4 * x + y, v_im * m_re - v_re * m_im)


def tie_kernel(*refs):
    pass


def after(values, others, flops=0):
    place = pl.BlockSpec(memory_space=pl.ANY)
    return pl.pallas_call(
        tie_kernel,
        out_shape=[jax.ShapeDtypeStruct(x.shape, x.dtype) for x in values],
        in_specs=[place] * (len(values) + len(others)),
        out_specs=[place] * len(values),
        input_output_aliases={n: n for n in range(len(values))},
        compiler_params=pltpu.CompilerParams(vmem_limit_bytes=1024 * 1024),
        cost_estimate=pl.CostEstimate(flops=flops, bytes_accessed=0, transcendentals=0),
    )(*values, *others)


def normal_terms(gains, prod_ref, first_s, second_s, a_s, out_ref):
    half = BLOCK // 2
    low = iota((half, LANES), 1) < LANES // 2

    def swap(x):
        return pltpu.roll(x, LANES // 2, 1)

    first, second = [], [[], []]
    for m in range(8):
        part = [gains[m * BLOCK + h * half : m * BLOCK + (h + 1) * half] for h in range(2)]
        first.append(jnp.where(low, part[0], swap(part[1])))
        for h in range(2):
            second[h].append(jnp.where(low, swap(part[h]), part[h]))
    for n, x in enumerate(first + square(first)):
        first_s[n] = x
    for h in range(2):
        for n, x in enumerate(second[h] + square(second[h])):
            second_s[h, n] = x

    def step(i, totals):
        partial = None
        new = []
        one = [first_s[n, pl.ds(i, 1), :] for n in range(12)]
        for h in range(2):
            two = [second_s[h, n] for n in range(12)]

            def load(n):
                return prod_ref[n, i, h * half : (h + 1) * half, :]

            def pairs(r, k, c, n):
                at = (2 * r + k) * 4 + 2 * c + n
                return load(at), load(16 + at)

            def cross(r, k, c, n):
                at = CROSS.index((2 * r + k, 2 * c + n))
                return load(36 + at), load(42 + at)

            own = [[load(32 + 2 * r + k) for k in range(2)] for r in range(2)]
            terms = apply_gains(pairs, two[:8], False) + outer_first(own, cross, two[8:])
            partial = terms if partial is None else [x + y for x, y in zip(partial, terms)]
            terms = apply_gains(pairs, one[:8], True) + outer_second(own, cross, one[8:])
            new += [x + y for x, y in zip(totals[12 * h : 12 * (h + 1)], terms)]
        for k in range(12):
            a_s[k, pl.ds(i, 1), :] = jnp.sum(partial[k], 0, keepdims=True)
        return tuple(new)

    zero = jnp.zeros((half, LANES), F32)
    totals = lax.fori_loop(0, half, step, (zero,) * 24, unroll=4)
    for k in range(12):
        mine = a_s[k]
        for h in range(2):
            other = totals[12 * h + k]
            other = other + swap(other)
            at = k * BLOCK + h * half
            out_ref[at : at + half, :] = jnp.where(low, swap(mine) if h else mine, other)


def key_match(rows, lanes):
    count = lanes.shape[1] // LANES
    return (jnp.concatenate([rows] * count, 1) == lanes).astype(BF16)


def beside(refs, count):
    return jnp.concatenate([p[...] for p in refs[:count]], 1), refs[count:]


def first_kernel(count, *refs):
    every, refs = beside(refs, count)
    key_ref, prod_ref, gains_ref, out_ref = refs[:4]
    scratch = refs[4:]
    select = key_match(key_ref[:LANES, :], every[GAIN_ROWS + 1 : GAIN_ROWS + 2])
    gains = pick(every[:GAIN_ROWS], select)
    gains_ref[...] = gains
    normal_terms(gains, prod_ref, *scratch, out_ref)


def state_kernel(count, blocks, intervals, *refs):
    every, refs = beside(refs, count)
    key_ref, at_ref, gains_ref, chans_ref, basis_ref = refs[:5]
    z_ref, pen_ref, scale_ref, select_ref, turned_ref = refs[5:]
    place = (iota((KPAD, LANES), 0) == iota((KPAD, LANES), 1) % KPAD).astype(BF16)
    for n, piece in enumerate(split(turn(place, basis_ref[LANES:, :]))):
        turned_ref[n * KPAD : (n + 1) * KPAD, :] = piece
    rows = every[GAIN_ROWS:]
    z_ref[:, :LANES] = gains_ref[...]
    z_ref[:, LANES:] = every[:GAIN_ROWS, :LANES]
    select_ref[...] = key_match(key_ref[...], rows[0:1])
    lanes = rows.shape[1]
    diagonal = iota((BLOCK, lanes), 0) == iota((BLOCK, lanes), 1) % BLOCK
    at = at_ref[...]
    pen = pick(jnp.where(diagonal, rows[2:3], 0.0), key_match(at, rows[3:4]))
    unused = iota(pen.shape, 1) >= LANES + blocks * intervals
    pen_ref[...] = jnp.where(unused, 1.0, pen)
    weights = pick(jnp.where(diagonal, rows[4:5], 0.0), key_match(at, rows[5:6]))
    scale_ref[...] = 1.0 / jnp.maximum(weights * chans_ref[0:1, :], 1.0)


def solve(normal, scale, pen, consensus):
    part = [normal[BLOCK * k : BLOCK * (k + 1)] * scale for k in range(12)]
    rhs = [part[m] + pen * consensus[BLOCK * m : BLOCK * (m + 1)] for m in range(8)]
    h_first = part[8] + pen
    h_second = part[9] + pen
    h_real, h_imag = part[10], part[11]
    determ = h_first * h_second - h_real * h_real - h_imag * h_imag
    over = 1.0 / determ
    d_first, d_second = h_first * over, h_second * over
    d_real, d_imag = h_real * over, h_imag * over
    out = [None] * 8
    for r in range(2):
        x_re, y_re = rhs[2 * r], rhs[2 * r + 1]
        x_im, y_im = rhs[4 + 2 * r], rhs[5 + 2 * r]
        out[2 * r] = x_re * d_second - (y_re * d_real + y_im * d_imag)
        out[4 + 2 * r] = x_im * d_second - (y_im * d_real - y_re * d_imag)
        out[2 * r + 1] = y_re * d_first - (x_re * d_real - x_im * d_imag)
        out[5 + 2 * r] = y_im * d_first - (x_im * d_real + x_re * d_imag)
    return jnp.concatenate(out, 0)


def step_kernel(count, *refs):
    every, refs = beside(refs, count)
    select_ref, z_ref, pen_ref, scale_ref, prod_ref, gains_ref, out_ref = refs[:7]
    scratch = refs[7:]
    normal = pick(every, select_ref[...])
    gains = solve(normal, scale_ref[...], pen_ref[...], z_ref[...])
    gains_ref[...] = gains
    normal_terms(gains[:, :LANES], prod_ref, *scratch, out_ref)


def first_total_kernel(gains_ref, basis_ref, out_ref):
    basis = basis_ref[...]
    total = nn(gains_ref[...], basis, precision=HIGH)
    part = basis[: basis.shape[0] // 8]
    gram = lax.dot_general(
        part, part, (((0,), (0,)), ((), ())), preferred_element_type=F32, precision=HIGH
    )
    out_ref[:GAIN_ROWS, :] = total
    out_ref[GAIN_ROWS:, :] = gram[:KPAD]


def total_kernel(gains_ref, dual_ref, basis_ref, out_ref):
    out_ref[...] = nn(gains_ref[...] + dual_ref[...], basis_ref[...], precision=HIGH)


def inverse_of_three(d):
    def minor(r, c):
        (r0, r1), (c0, c1) = [[k for k in range(3) if k != n] for n in (r, c)]
        value = d[r0][c0] * d[r1][c1] - d[r0][c1] * d[r1][c0]
        return value if (r + c) % 2 == 0 else -value

    minors = [[minor(r, c) for c in range(3)] for r in range(3)]
    over = 1.0 / (d[0][0] * minors[0][0] + d[0][1] * minors[0][1] + d[0][2] * minors[0][2])
    return [[minors[c][r] * over for c in range(3)] for r in range(3)]


def invert(gram):
    row, lane = iota(gram.shape, 0), iota(gram.shape, 1)
    inner = (row < NPOLY) & (lane < NPOLY)
    work = jnp.where(inner, gram + jnp.where(row == lane, ridge, 0.0), 0.0)
    lanes = iota((1, gram.shape[1]), 1)
    for p in range(0, NPOLY, 3):
        rows = [work[p + a : p + a + 1] for a in range(3)]
        block = inverse_of_three(
            [
                [jnp.broadcast_to(rows[a][:, p + b : p + b + 1], lanes.shape) for b in range(3)]
                for a in range(3)
            ]
        )
        columns = [work[:, p + b : p + b + 1] for b in range(3)]
        here = (lane >= p) & (lane < p + 3)
        rows = [jnp.where(here[:1], 0.0, x) for x in rows]
        pivots = []
        for a in range(3):
            pivot = block[a][0] * rows[0] + block[a][1] * rows[1] + block[a][2] * rows[2]
            for b in range(3):
                pivot = jnp.where(lanes == p + b, block[a][b], pivot)
            pivots.append(pivot)
        work = jnp.where(here, 0.0, work)
        for b in range(3):
            work = work - columns[b] * pivots[b]
        for a in range(3):
            work = jnp.where(row == p + a, pivots[a], work)
    return work


def settle(total, inverse, basis_ref, gains, z_ref, dual_ref):
    coeff = nn(total, inverse, precision=HIGH)
    consensus = nt(coeff, basis_ref[...], precision=HIGH)
    z_ref[...] = 2.0 * consensus - gains
    dual_ref[...] = gains - consensus


def band_total(refs):
    totals = [ref[...] for ref in refs]
    while len(totals) > 1:
        totals = [totals[n] + totals[n + 1] for n in range(0, len(totals), 2)]
    return totals[0]


def first_consensus_kernel(
    one_ref, two_ref, gains_ref, basis_ref, z_ref, dual_ref, inverse_ref
):
    total = one_ref[...] + two_ref[...]
    small = invert(total[GAIN_ROWS:])
    row, lane = iota((LANES, LANES), 0), iota((LANES, LANES), 1)
    spread = ((row == lane % KPAD) & (row < KPAD)).astype(F32)
    wide = nn(jnp.concatenate([small] * (LANES // KPAD), 0), spread, precision=HIGH)
    inverse = jnp.where(row // KPAD == lane // KPAD, wide, 0.0)
    inverse_ref[...] = inverse
    settle(total[:GAIN_ROWS], inverse, basis_ref, gains_ref[...], z_ref, dual_ref)


def consensus_kernel(
    one_ref, two_ref, gains_ref, old_ref, basis_ref, inverse_ref, z_ref, dual_ref
):
    total = one_ref[...] + two_ref[...]
    gains = gains_ref[...] + old_ref[...]
    settle(total, inverse_ref[...], basis_ref, gains, z_ref, dual_ref)


def last_kernel(count, blocks, intervals, *refs):
    every, refs = beside(refs, count)
    select_ref, z_ref, pen_ref, scale_ref, dual_ref, turned_ref, gains_ref, out_ref = refs
    own = slice(LANES, 2 * LANES)
    normal = pick(every, select_ref[own, :])
    gains = solve(normal, scale_ref[:, own], pen_ref[:, own], z_ref[:, own])
    gains_ref[...] = gains
    owned = blocks * BLOCK
    here = iota((owned, LANES), 0) // BLOCK == iota((owned, LANES), 1) // intervals
    summed = gains + dual_ref[:, own]
    parts = [summed[m * BLOCK : (m + 1) * BLOCK] for m in range(8)]
    parts = [jnp.where(here, jnp.concatenate([x] * blocks, 0), 0.0) for x in parts]
    high, mid, low = split(jnp.concatenate(parts, 0))
    turned = turned_ref[...]
    first, second = nt(turned, high), nt(turned[: 2 * KPAD], mid)
    small = first[2 * KPAD :] + second[KPAD:] + nt(turned[:KPAD], low)
    total = first[:KPAD] + ((first[KPAD : 2 * KPAD] + second[:KPAD]) + small)
    chunks = total.shape[1] // LANES
    for c in range(chunks):
        lanes = slice(c * LANES, (c + 1) * LANES)
        out_ref[8 * c : 8 * c + 8, :] = total[:8, lanes]
        out_ref[8 * chunks + c : 8 * chunks + c + 1, :] = total[8:9, lanes]
    rest = 9 * chunks
    out_ref[rest:, :] = jnp.zeros((out_ref.shape[0] - rest, LANES), F32)


def gains_kernel(blocks, intervals, gains_ref, out_ref):
    owned = blocks * BLOCK
    place = (iota((intervals, LANES), 0) == iota((intervals, LANES), 1) % intervals).astype(BF16)
    here = iota((owned, LANES), 0) // BLOCK == iota((owned, LANES), 1) // intervals
    for m in range(8):
        part = gains_ref[m * BLOCK : (m + 1) * BLOCK, :]
        out_ref[m] = turn(place, jnp.where(here, jnp.concatenate([part] * blocks, 0), 0.0))


def split(values):
    high = values.astype(BF16)
    rest = values - high.astype(F32)
    mid = rest.astype(BF16)
    return high, mid, (rest - mid.astype(F32)).astype(BF16)


def turn(place, values):
    high, mid, low = split(values)
    return (nt(place, high) + nt(place, mid)) + nt(place, low)


def coefficient_kernel(bands, *refs):
    inverse_ref, out_ref = refs[bands:]
    total = band_total(refs[:bands])
    owned = out_ref.shape[2]
    chunks = 8 * owned // LANES
    inverse = inverse_ref[:KPAD, :KPAD]
    eight = jnp.concatenate([total[8 * c : 8 * c + 8] for c in range(chunks)], 1)
    ninth = jnp.concatenate([total[8 * chunks + c : 8 * chunks + c + 1] for c in range(chunks)], 1)
    coeff = nn(inverse[:, :8], eight, precision=HIGH) + inverse[:, 8:9] * ninth
    for m in range(8):
        out_ref[:, m, :] = coeff[:NPOLY, m * owned : (m + 1) * owned]


def call(kernel, operands, shapes, scratch=(), hbm=False, flops=20_000_000):
    vmem = pl.BlockSpec(memory_space=pltpu.VMEM)
    in_specs = [vmem] * len(operands)
    moved = sum(x.size * x.dtype.itemsize for x in (*operands, *shapes))
    if hbm:
        in_specs = [pl.BlockSpec(memory_space=pltpu.HBM)] * len(operands)
        operands = [pltpu.with_memory_space_constraint(x, pltpu.HBM) for x in operands]
    return pl.pallas_call(
        kernel,
        out_shape=shapes,
        in_specs=in_specs,
        out_specs=[vmem] * len(shapes),
        scratch_shapes=list(scratch),
        compiler_params=pltpu.CompilerParams(vmem_limit_bytes=14 * 1024 * 1024),
        cost_estimate=pl.CostEstimate(flops=flops, bytes_accessed=moved, transcendentals=0),
    )(*operands)


def share_base(x, last=(), ties=(2,), ahead=False):
    devices = lax.axis_size("base")
    mine = [x] + [
        lax.ppermute(x, "base", [(d, d ^ (2 * k)) for d in range(devices)])
        for k in range(1, devices // 2)
    ]
    if ahead:
        mine[3:] = after(mine[3:], (), flops=5_000_000_000)
    if last:
        for k, y in zip(ties, after([mine[k] for k in ties], last)):
            mine[k] = y
    other = [lax.ppermute(y, "base", [(d, d ^ 1) for d in range(devices)]) for y in mine]
    return mine + other


def share_band(x):
    devices = lax.axis_size("band")
    return [x] + [
        lax.ppermute(x, "band", [(d, d ^ k) for d in range(devices)]) for k in range(1, devices)
    ]


def sum_band(x):
    devices = lax.axis_size("band")
    step = 1
    while 2 * step < devices:
        x = x + lax.ppermute(x, "band", [(d, d ^ step) for d in range(devices)])
        step = 2 * step
    return x, lax.ppermute(x, "band", [(d, d ^ step) for d in range(devices)])


def on_device(visibilities, model, start_gains, penalty, pairs, flags, chan_band):
    tiles, channels, cells = visibilities.shape[1:]
    intervals = start_gains.shape[1]
    owned = start_gains.shape[2]
    blocks = owned // BLOCK
    count = lax.axis_size("base")
    bands = lax.axis_size("band")
    width = tiles * channels

    def shape(*extent, dtype=F32):
        return jax.ShapeDtypeStruct(extent, dtype)

    wide = shape(GAIN_ROWS, 2 * LANES)
    narrow = shape(GAIN_ROWS, LANES)
    single = shape(BLOCK, 2 * LANES)
    terms = shape(TERM_ROWS, LANES)
    square = shape(2 * LANES, LANES)

    (greeting,) = call(
        functools.partial(greet_kernel, blocks, intervals),
        (pairs, start_gains, penalty.reshape(1, owned), flags),
        [shape(GAIN_ROWS + 8, LANES)],
        [
            pltpu.SMEM(pairs.shape, jnp.int32),
            pltpu.VMEM(start_gains.shape, F32),
            pltpu.VMEM((1, owned), F32),
            pltpu.VMEM(flags.shape, jnp.int32),
            pltpu.SemaphoreType.DMA((4,)),
        ],
        hbm=True,
    )
    products, keys, at, basis, chans = call(
        functools.partial(prepare_kernel, blocks, intervals, bands),
        (
            pairs,
            chan_band.reshape(1, channels),
            flags,
            visibilities.reshape(8, width, cells),
            model.reshape(8, width, cells),
        ),
        [
            shape(PRODUCTS, BLOCK // 2, BLOCK, 2 * tiles * intervals),
            square,
            square,
            square,
            shape(8, 2 * LANES),
        ],
        [
            pltpu.SMEM(pairs.shape, jnp.int32),
            pltpu.VMEM((1, channels), jnp.int32),
            pltpu.VMEM(flags.shape, jnp.int32),
            *[pltpu.VMEM((8, width, cells), BF16)] * 2,
            pltpu.VMEM((8, cells, width), F32),
            pltpu.SemaphoreType.DMA((5,)),
        ],
        hbm=True,
        flops=2_000_000_000,
    )
    greetings = share_base(greeting, last=(chans,))
    scratch = [
        pltpu.VMEM((12, BLOCK // 2, LANES), F32),
        pltpu.VMEM((2, 12, BLOCK // 2, LANES), F32),
        pltpu.VMEM((12, BLOCK // 2, LANES), F32),
    ]

    gains, message = call(
        functools.partial(first_kernel, count),
        (*greetings, keys, products),
        [narrow, terms],
        scratch,
    )
    z, pen, scale, select, turned = call(
        functools.partial(state_kernel, count, blocks, intervals),
        (*greetings, keys, at, gains, chans, basis),
        [
            wide,
            single,
            single,
            shape(2 * LANES, count * LANES, dtype=BF16),
            shape(3 * KPAD, LANES, dtype=BF16),
        ],
    )
    pieces = share_base(message, last=(scale,), ties=(1, 2))
    gains, message = call(
        functools.partial(step_kernel, count),
        (*pieces, select, z, pen, scale, products),
        [wide, terms],
        scratch,
    )
    (part,) = call(first_total_kernel, (gains, basis), [shape(GAIN_ROWS + KPAD, LANES)])
    z, dual, inverse = call(
        first_consensus_kernel, (*sum_band(part), gains, basis), [wide, wide, narrow]
    )
    pieces = share_base(message, last=(z,), ties=(1, 2), ahead=True)
    gains, message = call(
        functools.partial(step_kernel, count),
        (*pieces, select, z, pen, scale, products),
        [wide, terms],
        scratch,
    )
    (part,) = call(total_kernel, (gains, dual, basis), [narrow])
    z, dual = call(consensus_kernel, (*sum_band(part), gains, dual, basis, inverse), [wide, wide])
    pieces = share_base(message, last=(z,), ties=(1, 2), ahead=True)
    chunks = 8 * owned // LANES
    gains, part = call(
        functools.partial(last_kernel, count, blocks, intervals),
        (*pieces, select, z, pen, scale, dual, turned),
        [narrow, shape(8 * chunks + -(-chunks // 8) * 8, LANES)],
    )
    parts = share_band(part)
    (out,) = call(
        functools.partial(gains_kernel, blocks, intervals),
        (gains,),
        [shape(8, intervals, owned)],
    )
    (coefficients,) = call(
        functools.partial(coefficient_kernel, bands),
        (*parts, inverse),
        [shape(NPOLY, 8, owned)],
    )
    return (out, jnp.transpose(coefficients, (1, 0, 2)))


def solution(mesh):
    in_specs = (
        P(None, "base", "band", None),
        P(None, "base", "band", None),
        P(None, "band", "base"),
        P("base"),
        P("base", None),
        P("base", None),
        P("band"),
    )
    out_specs = (P(None, "band", "base"), P(None, None, "base"))
    return jax.shard_map(
        on_device, mesh=mesh, in_specs=in_specs, out_specs=out_specs, check_vma=False
    )
```

```python
import functools

import jax
import jax.numpy as jnp
from jax import lax
from jax.experimental import pallas as pl
from jax.experimental.pallas import tpu as pltpu
from jax.sharding import PartitionSpec as P

BLOCK = 16
NPOLY = 9
KPAD = 16
ITERS = 3
LANES = 128
F32 = jnp.float32
BF16 = jnp.bfloat16
HIGH = lax.Precision.HIGHEST

ridge = 0.5

GAIN_ROWS = 8 * BLOCK
TERM_ROWS = 12 * BLOCK
PRODUCTS = 48
CROSS = ((0, 1), (0, 2), (0, 3), (1, 2), (1, 3), (2, 3))


def nt(left, right, **kw):
    return lax.dot_general(
        left, right, (((1,), (1,)), ((), ())), preferred_element_type=F32, **kw
    )


def nn(left, right, **kw):
    return lax.dot_general(
        left, right, (((1,), (0,)), ((), ())), preferred_element_type=F32, **kw
    )


def pick(values, select, dot=nt):
    high = values.astype(BF16)
    low = (values - high.astype(F32)).astype(BF16)
    rows = values.shape[0]
    out = dot(jnp.concatenate([high, low], 0), select)
    return out[:rows] + out[rows:]


def iota(shape, axis):
    return lax.broadcasted_iota(jnp.int32, shape, axis)


def add(terms):
    total = None
    for sign, x, y in terms:
        if total is None:
            total = x * y if sign > 0 else -(x * y)
        else:
            total = total + x * y if sign > 0 else total - x * y
    return total


def apply_gains(pairs, gains, turned):
    re, im = [], []
    for r in range(2):
        for c in range(2):
            to_re, to_im = [], []
            for k in range(2):
                for n in range(2):
                    x_re, x_im = pairs(k, r, n, c) if turned else pairs(r, k, c, n)
                    g_re, g_im = gains[2 * k + n], gains[4 + 2 * k + n]
                    sign = -1 if turned else 1
                    to_re += [(1, x_re, g_re), (-sign, x_im, g_im)]
                    to_im += [(1, x_re, g_im), (sign, x_im, g_re)]
            re.append(add(to_re))
            im.append(add(to_im))
    return re + im


def square(gains):
    return [
        add([(1, gains[n], gains[n]) for n in (0, 2, 4, 6)]),
        add([(1, gains[n], gains[n]) for n in (1, 3, 5, 7)]),
        add([(1, gains[n], gains[n + 1]) for n in (0, 2, 4, 6)]),
        add([(1, gains[0], gains[5]), (-1, gains[4], gains[1])])
        + add([(1, gains[2], gains[7]), (-1, gains[6], gains[3])]),
    ]


def outer_first(own, cross, q):
    out = []
    for r in range(2):
        x_re, x_im = cross(r, 0, r, 1)
        twice = add([(1, x_re, q[2]), (-1, x_im, q[3])])
        out.append(add([(1, own[r][0], q[0]), (1, own[r][1], q[1])]) + (twice + twice))
    (a_re, a_im), (b_re, b_im) = cross(0, 0, 1, 0), cross(0, 1, 1, 1)
    (c_re, c_im), (d_re, d_im) = cross(0, 0, 1, 1), cross(0, 1, 1, 0)
    out.append(
        add([(1, a_re, q[0]), (1, b_re, q[1]), (1, c_re + d_re, q[2]), (-1, c_im - d_im, q[3])])
    )
    out.append(
        add([(1, a_im, q[0]), (1, b_im, q[1]), (1, c_im + d_im, q[2]), (1, c_re - d_re, q[3])])
    )
    return out


def outer_second(own, cross, q):
    out = []
    for c in range(2):
        x_re, x_im = cross(0, c, 1, c)
        twice = add([(1, x_re, q[2]), (1, x_im, q[3])])
        out.append(add([(1, own[0][c], q[0]), (1, own[1][c], q[1])]) + (twice + twice))
    (a_re, a_im), (b_re, b_im) = cross(0, 0, 0, 1), cross(1, 0, 1, 1)
    (c_re, c_im), (d_re, d_im) = cross(0, 0, 1, 1), cross(0, 1, 1, 0)
    out.append(
        add([(1, a_re, q[0]), (1, b_re, q[1]), (1, c_re + d_re, q[2]), (1, c_im + d_im, q[3])])
    )
    out.append(
        add([(-1, a_im, q[0]), (-1, b_im, q[1]), (1, c_re - d_re, q[3]), (-1, c_im - d_im, q[2])])
    )
    return out


def slot_key(index, pairs, scale, intervals):
    at = index // intervals
    tiles = len(pairs)
    block = jnp.zeros(index.shape, F32)
    for slot in range(2 * tiles):
        value = pairs[slot % tiles][slot // tiles]
        block = jnp.where(at == slot, value.astype(F32), block)
    if scale > 1:
        block = block * scale + (index % intervals).astype(F32)
    return block


def scalar_pairs(pair_ref):
    return [[pair_ref[t, side] for side in range(2)] for t in range(pair_ref.shape[0])]


def owner_key(index, me, blocks, intervals, none, scale=None):
    at = index // intervals
    key = me * blocks + at
    if scale != 1:
        key = key * intervals + index % intervals
    return jnp.where(at < blocks, key, none).astype(F32)


def cell_weights(pairs, flags):
    cells = flags.shape[1]
    cell = iota((1, cells), 1)
    diagonal = (cell // BLOCK == cell % BLOCK).astype(F32)
    rows = []
    for t, pair in enumerate(pairs):
        same = (pair[0] == pair[1]).astype(F32)
        rows.append(flags[t : t + 1, :] * (1.0 - same * diagonal))
    return rows


def greet_kernel(
    blocks, intervals, pair_hbm, start_hbm, penalty_hbm, flag_hbm, out_ref, again_ref, pair_ref, start_ref,
    penalty_ref, flag_ref, sems
):
    copies = [
        pltpu.make_async_copy(source, target, sems.at[n])
        for n, (source, target) in enumerate(
            [
                (start_hbm, start_ref),
                (pair_hbm, pair_ref),
                (flag_hbm, flag_ref),
                (penalty_hbm, penalty_ref),
            ]
        )
    ]
    for copy in copies:
        copy.start()
    for copy in copies[1:]:
        copy.wait()
    owned = blocks * BLOCK
    cells = flag_ref.shape[1]
    me = lax.axis_index("base")
    pairs = scalar_pairs(pair_ref)
    tiles = len(pairs)
    weights = cell_weights(pairs, flag_ref[...].astype(F32))
    lane = iota((cells, LANES), 1)
    cell = iota((cells, LANES), 0)
    at, inside = lane // BLOCK, lane % BLOCK
    member = jnp.where(at < tiles, cell // BLOCK, cell % BLOCK) == inside
    station_w = jnp.zeros((8, LANES), F32)
    for t in range(tiles):
        fold = (member & (at % tiles == t) & (at < 2 * tiles)).astype(BF16)
        station_w = station_w + nn(jnp.broadcast_to(weights[t], (8, cells)).astype(BF16), fold)
    lane = iota((8, LANES), 1)
    row = iota((8, LANES), 0)
    wide = intervals // BLOCK
    slot_at = jnp.where(lane // BLOCK < 2 * tiles, slot_key(lane * wide, pairs, 1, intervals), -2.0)
    owner_at = jnp.where(lane // BLOCK < blocks, (me * blocks + lane // BLOCK).astype(F32), -2.0)
    keys = jnp.where(row == 0, slot_key(lane, pairs, intervals, intervals), 0.0)
    keys = jnp.where(row == 1, owner_key(lane, me, blocks, intervals, -2), keys)
    keys = jnp.where(row == 3, owner_at, keys)
    keys = jnp.where(row == 4, station_w, keys)
    out_ref[GAIN_ROWS:, :] = jnp.where(row == 5, slot_at, keys)
    out_ref[GAIN_ROWS + 2 : GAIN_ROWS + 3, :owned] = penalty_ref[...]
    copies[0].wait()
    place = (iota((BLOCK, owned), 0) == iota((BLOCK, owned), 1) % BLOCK).astype(BF16)
    here = iota((LANES, owned), 0) // intervals == iota((LANES, owned), 1) // BLOCK
    for m in range(8):
        plane = start_ref[m]
        plane = jnp.where(here, jnp.concatenate([plane] * (LANES // intervals), 0), 0.0)
        high = plane.astype(BF16)
        low = (plane - high.astype(F32)).astype(BF16)
        out_ref[m * BLOCK : (m + 1) * BLOCK, :] = nt(place, high) + nt(place, low)
    again_ref[...] = out_ref[...]


def prepare_kernel(
    blocks, intervals, bands, pair_hbm, chan_hbm, flag_hbm, vis_hbm, model_hbm, prod_ref, key_ref,
    at_ref, basis_ref, chans_ref, pair_ref, chan_ref, flag_ref, vis_ref, model_ref, mt_ref, sems
):
    planes, width, cells = vis_ref.shape
    moves = [
        (model_hbm, model_ref),
        (vis_hbm, vis_ref),
        (pair_hbm, pair_ref),
        (chan_hbm, chan_ref),
        (flag_hbm, flag_ref),
    ]
    copies = [
        pltpu.make_async_copy(source, target, sems.at[n])
        for n, (source, target) in enumerate(moves)
    ]
    for copy in copies:
        copy.start()
    for copy in copies[2:]:
        copy.wait()
    pairs = scalar_pairs(pair_ref)
    tiles = len(pairs)
    channels = width // tiles
    me = lax.axis_index("base")
    row = iota((2 * LANES, LANES), 0)
    lane = iota((2 * LANES, LANES), 1)
    for ref, scale in ((key_ref, intervals), (at_ref, 1)):
        ref[...] = jnp.where(
            row < LANES,
            slot_key(row, pairs, scale, intervals),
            owner_key(row - LANES, me, blocks, intervals, -1, scale),
        )
    band_at = lax.axis_index("band")
    local = chan_ref[...] - band_at * intervals
    chan = (band_at * channels + iota((1, channels), 1)).astype(F32)
    xpos = -1.0 + (2.0 * chan + 1.0) / (channels * bands)
    member = (iota((2 * LANES, channels), 0) % intervals == local).astype(F32)
    chans = jnp.sum(member, 1, keepdims=True)
    chans_ref[...] = nt(jnp.ones((8, channels), BF16), member.astype(BF16))
    centre = jnp.sum(member * xpos, 1, keepdims=True) / chans
    terms = [jnp.ones((2 * LANES, LANES), F32), jnp.broadcast_to(centre, (2 * LANES, LANES))]
    for order in range(2, NPOLY):
        terms.append(2.0 * terms[1] * terms[-1] - terms[-2])
    basis = jnp.zeros((2 * LANES, LANES), F32)
    for order in range(NPOLY):
        basis = jnp.where(lane % KPAD == order, terms[order], basis)
    basis_ref[...] = jnp.where(row // intervals == lane // KPAD, basis, 0.0)
    lanes = 2 * tiles * intervals
    row = iota((lanes, 2 * width), 0)
    lane = iota((lanes, 2 * width), 1)
    at = jnp.concatenate([local] * (2 * tiles), 1)
    fold = ((row // intervals == lane // channels) & (row % intervals == at)).astype(BF16)
    ident = (iota((cells, cells), 0) == iota((cells, cells), 1)).astype(BF16)
    rows = cell_weights(pairs, flag_ref[...].astype(F32))
    weight = jnp.concatenate([jnp.broadcast_to(w, (channels, cells)) for w in rows], 0)
    half = cells // 2

    def put(at, product):
        beside = jnp.concatenate([product[:half], product[half:]], 1)
        prod_ref[at] = pick(beside, fold).reshape(prod_ref.shape[1:])

    copies[0].wait()
    for m in range(planes):
        masked = (model_ref[m].astype(F32) * weight).astype(BF16)
        mt_ref[m] = nt(ident, masked)
    for x in range(4):
        put(32 + x, mt_ref[x] * mt_ref[x] + mt_ref[4 + x] * mt_ref[4 + x])
    for n, (x, y) in enumerate(CROSS):
        x_re, x_im, y_re, y_im = mt_ref[x], mt_ref[4 + x], mt_ref[y], mt_ref[4 + y]
        put(36 + n, x_re * y_re + x_im * y_im)
        put(42 + n, x_im * y_re - x_re * y_im)
    copies[1].wait()
    for x in range(4):
        v_re, v_im = nt(ident, vis_ref[x]), nt(ident, vis_ref[4 + x])
        for y in range(4):
            m_re, m_im = mt_ref[y], mt_ref[4 + y]
            put(4 * x + y, v_re * m_re + v_im * m_im)
            put(16 + 4 * x + y, v_im * m_re - v_re * m_im)


def tie_kernel(*refs):
    pass


def after(values, others, flops=0):
    place = pl.BlockSpec(memory_space=pl.ANY)
    return pl.pallas_call(
        tie_kernel,
        out_shape=[jax.ShapeDtypeStruct(x.shape, x.dtype) for x in values],
        in_specs=[place] * (len(values) + len(others)),
        out_specs=[place] * len(values),
        input_output_aliases={n: n for n in range(len(values))},
        compiler_params=pltpu.CompilerParams(vmem_limit_bytes=1024 * 1024),
        cost_estimate=pl.CostEstimate(flops=flops, bytes_accessed=0, transcendentals=0),
    )(*values, *others)


def normal_terms(gains, prod_ref, first_s, second_s, a_s, out_ref):
    half = BLOCK // 2
    low = iota((half, LANES), 1) < LANES // 2

    def swap(x):
        return pltpu.roll(x, LANES // 2, 1)

    first, second = [], [[], []]
    for m in range(8):
        part = [gains[m * BLOCK + h * half : m * BLOCK + (h + 1) * half] for h in range(2)]
        first.append(jnp.where(low, part[0], swap(part[1])))
        for h in range(2):
            second[h].append(jnp.where(low, swap(part[h]), part[h]))
    for n, x in enumerate(first + square(first)):
        first_s[n] = x
    for h in range(2):
        for n, x in enumerate(second[h] + square(second[h])):
            second_s[h, n] = x

    def step(i, totals):
        partial = None
        new = []
        one = [first_s[n, pl.ds(i, 1), :] for n in range(12)]
        for h in range(2):
            two = [second_s[h, n] for n in range(12)]

            def load(n):
                return prod_ref[n, i, h * half : (h + 1) * half, :]

            def pairs(r, k, c, n):
                at = (2 * r + k) * 4 + 2 * c + n
                return load(at), load(16 + at)

            def cross(r, k, c, n):
                at = CROSS.index((2 * r + k, 2 * c + n))
                return load(36 + at), load(42 + at)

            own = [[load(32 + 2 * r + k) for k in range(2)] for r in range(2)]
            terms = apply_gains(pairs, two[:8], False) + outer_first(own, cross, two[8:])
            partial = terms if partial is None else [x + y for x, y in zip(partial, terms)]
            terms = apply_gains(pairs, one[:8], True) + outer_second(own, cross, one[8:])
            new += [x + y for x, y in zip(totals[12 * h : 12 * (h + 1)], terms)]
        for k in range(12):
            a_s[k, pl.ds(i, 1), :] = jnp.sum(partial[k], 0, keepdims=True)
        return tuple(new)

    zero = jnp.zeros((half, LANES), F32)
    totals = lax.fori_loop(0, half, step, (zero,) * 24, unroll=4)
    for k in range(12):
        mine = a_s[k]
        for h in range(2):
            other = totals[12 * h + k]
            other = other + swap(other)
            at = k * BLOCK + h * half
            out_ref[at : at + half, :] = jnp.where(low, swap(mine) if h else mine, other)


def key_match(rows, lanes):
    count = lanes.shape[1] // LANES
    return (jnp.concatenate([rows] * count, 1) == lanes).astype(BF16)


def beside(refs, count):
    return jnp.concatenate([p[...] for p in refs[:count]], 1), refs[count:]


def first_kernel(count, *refs):
    every, refs = beside(refs, count)
    key_ref, prod_ref, gains_ref, out_ref = refs[:4]
    scratch = refs[4:]
    select = key_match(key_ref[:LANES, :], every[GAIN_ROWS + 1 : GAIN_ROWS + 2])
    gains = pick(every[:GAIN_ROWS], select)
    gains_ref[...] = gains
    normal_terms(gains, prod_ref, *scratch, out_ref)


def state_kernel(count, blocks, intervals, *refs):
    every, refs = beside(refs, count)
    key_ref, at_ref, gains_ref, chans_ref, basis_ref = refs[:5]
    z_ref, pen_ref, scale_ref, select_ref, turned_ref = refs[5:]
    place = (iota((KPAD, LANES), 0) == iota((KPAD, LANES), 1) % KPAD).astype(BF16)
    for n, piece in enumerate(split(turn(place, basis_ref[LANES:, :]))):
        turned_ref[n * KPAD : (n + 1) * KPAD, :] = piece
    rows = every[GAIN_ROWS:]
    z_ref[:, :LANES] = gains_ref[...]
    z_ref[:, LANES:] = every[:GAIN_ROWS, :LANES]
    select_ref[...] = key_match(key_ref[...], rows[0:1])
    lanes = rows.shape[1]
    diagonal = iota((BLOCK, lanes), 0) == iota((BLOCK, lanes), 1) % BLOCK
    at = at_ref[...]
    pen = pick(jnp.where(diagonal, rows[2:3], 0.0), key_match(at, rows[3:4]))
    unused = iota(pen.shape, 1) >= LANES + blocks * intervals
    pen_ref[...] = jnp.where(unused, 1.0, pen)
    weights = pick(jnp.where(diagonal, rows[4:5], 0.0), key_match(at, rows[5:6]))
    scale_ref[...] = 1.0 / jnp.maximum(weights * chans_ref[0:1, :], 1.0)


def solve(normal, scale, pen, consensus):
    part = [normal[BLOCK * k : BLOCK * (k + 1)] * scale for k in range(12)]
    rhs = [part[m] + pen * consensus[BLOCK * m : BLOCK * (m + 1)] for m in range(8)]
    h_first = part[8] + pen
    h_second = part[9] + pen
    h_real, h_imag = part[10], part[11]
    determ = h_first * h_second - h_real * h_real - h_imag * h_imag
    over = 1.0 / determ
    d_first, d_second = h_first * over, h_second * over
    d_real, d_imag = h_real * over, h_imag * over
    out = [None] * 8
    for r in range(2):
        x_re, y_re = rhs[2 * r], rhs[2 * r + 1]
        x_im, y_im = rhs[4 + 2 * r], rhs[5 + 2 * r]
        out[2 * r] = x_re * d_second - (y_re * d_real + y_im * d_imag)
        out[4 + 2 * r] = x_im * d_second - (y_im * d_real - y_re * d_imag)
        out[2 * r + 1] = y_re * d_first - (x_re * d_real - x_im * d_imag)
        out[5 + 2 * r] = y_im * d_first - (x_im * d_real + x_re * d_imag)
    return jnp.concatenate(out, 0)


def step_kernel(count, *refs):
    every, refs = beside(refs, count)
    select_ref, z_ref, pen_ref, scale_ref, prod_ref, gains_ref, out_ref = refs[:7]
    scratch = refs[7:]
    normal = pick(every, select_ref[...])
    gains = solve(normal, scale_ref[...], pen_ref[...], z_ref[...])
    gains_ref[...] = gains
    normal_terms(gains[:, :LANES], prod_ref, *scratch, out_ref)


def first_total_kernel(gains_ref, basis_ref, out_ref):
    basis = basis_ref[...]
    total = nn(gains_ref[...], basis, precision=HIGH)
    part = basis[: basis.shape[0] // 8]
    gram = lax.dot_general(
        part, part, (((0,), (0,)), ((), ())), preferred_element_type=F32, precision=HIGH
    )
    out_ref[:GAIN_ROWS, :] = total
    out_ref[GAIN_ROWS:, :] = gram[:KPAD]


def total_kernel(gains_ref, dual_ref, basis_ref, out_ref):
    out_ref[...] = nn(gains_ref[...] + dual_ref[...], basis_ref[...], precision=HIGH)


def inverse_of_three(d):
    def minor(r, c):
        (r0, r1), (c0, c1) = [[k for k in range(3) if k != n] for n in (r, c)]
        value = d[r0][c0] * d[r1][c1] - d[r0][c1] * d[r1][c0]
        return value if (r + c) % 2 == 0 else -value

    minors = [[minor(r, c) for c in range(3)] for r in range(3)]
    over = 1.0 / (d[0][0] * minors[0][0] + d[0][1] * minors[0][1] + d[0][2] * minors[0][2])
    return [[minors[c][r] * over for c in range(3)] for r in range(3)]


def invert(gram):
    row, lane = iota(gram.shape, 0), iota(gram.shape, 1)
    inner = (row < NPOLY) & (lane < NPOLY)
    work = jnp.where(inner, gram + jnp.where(row == lane, ridge, 0.0), 0.0)
    lanes = iota((1, gram.shape[1]), 1)
    for p in range(0, NPOLY, 3):
        rows = [work[p + a : p + a + 1] for a in range(3)]
        block = inverse_of_three(
            [
                [jnp.broadcast_to(rows[a][:, p + b : p + b + 1], lanes.shape) for b in range(3)]
                for a in range(3)
            ]
        )
        columns = [work[:, p + b : p + b + 1] for b in range(3)]
        here = (lane >= p) & (lane < p + 3)
        rows = [jnp.where(here[:1], 0.0, x) for x in rows]
        pivots = []
        for a in range(3):
            pivot = block[a][0] * rows[0] + block[a][1] * rows[1] + block[a][2] * rows[2]
            for b in range(3):
                pivot = jnp.where(lanes == p + b, block[a][b], pivot)
            pivots.append(pivot)
        work = jnp.where(here, 0.0, work)
        for b in range(3):
            work = work - columns[b] * pivots[b]
        for a in range(3):
            work = jnp.where(row == p + a, pivots[a], work)
    return work


def settle(total, inverse, basis_ref, gains, z_ref, dual_ref):
    coeff = nn(total, inverse, precision=HIGH)
    consensus = nt(coeff, basis_ref[...], precision=HIGH)
    z_ref[...] = 2.0 * consensus - gains
    dual_ref[...] = gains - consensus


def band_total(refs):
    totals = [ref[...] for ref in refs]
    while len(totals) > 1:
        totals = [totals[n] + totals[n + 1] for n in range(0, len(totals), 2)]
    return totals[0]


def first_consensus_kernel(
    one_ref, two_ref, gains_ref, basis_ref, z_ref, dual_ref, inverse_ref
):
    total = one_ref[...] + two_ref[...]
    small = invert(total[GAIN_ROWS:])
    row, lane = iota((LANES, LANES), 0), iota((LANES, LANES), 1)
    spread = ((row == lane % KPAD) & (row < KPAD)).astype(F32)
    wide = nn(jnp.concatenate([small] * (LANES // KPAD), 0), spread, precision=HIGH)
    inverse = jnp.where(row // KPAD == lane // KPAD, wide, 0.0)
    inverse_ref[...] = inverse
    settle(total[:GAIN_ROWS], inverse, basis_ref, gains_ref[...], z_ref, dual_ref)


def consensus_kernel(
    one_ref, two_ref, gains_ref, old_ref, basis_ref, inverse_ref, z_ref, dual_ref
):
    total = one_ref[...] + two_ref[...]
    gains = gains_ref[...] + old_ref[...]
    settle(total, inverse_ref[...], basis_ref, gains, z_ref, dual_ref)


def last_kernel(count, blocks, intervals, *refs):
    every, refs = beside(refs, count)
    select_ref, z_ref, pen_ref, scale_ref, dual_ref, turned_ref, gains_ref, out_ref = refs
    own = slice(LANES, 2 * LANES)
    normal = pick(every, select_ref[own, :])
    gains = solve(normal, scale_ref[:, own], pen_ref[:, own], z_ref[:, own])
    gains_ref[...] = gains
    owned = blocks * BLOCK
    here = iota((owned, LANES), 0) // BLOCK == iota((owned, LANES), 1) // intervals
    summed = gains + dual_ref[:, own]
    parts = [summed[m * BLOCK : (m + 1) * BLOCK] for m in range(8)]
    parts = [jnp.where(here, jnp.concatenate([x] * blocks, 0), 0.0) for x in parts]
    high, mid, low = split(jnp.concatenate(parts, 0))
    turned = turned_ref[...]
    first, second = nt(turned, high), nt(turned[: 2 * KPAD], mid)
    small = first[2 * KPAD :] + second[KPAD:] + nt(turned[:KPAD], low)
    total = first[:KPAD] + ((first[KPAD : 2 * KPAD] + second[:KPAD]) + small)
    chunks = total.shape[1] // LANES
    for c in range(chunks):
        lanes = slice(c * LANES, (c + 1) * LANES)
        out_ref[8 * c : 8 * c + 8, :] = total[:8, lanes]
        out_ref[8 * chunks + c : 8 * chunks + c + 1, :] = total[8:9, lanes]
    rest = 9 * chunks
    out_ref[rest:, :] = jnp.zeros((out_ref.shape[0] - rest, LANES), F32)


def gains_kernel(blocks, intervals, gains_ref, out_ref):
    owned = blocks * BLOCK
    place = (iota((intervals, LANES), 0) == iota((intervals, LANES), 1) % intervals).astype(BF16)
    here = iota((owned, LANES), 0) // BLOCK == iota((owned, LANES), 1) // intervals
    for m in range(8):
        part = gains_ref[m * BLOCK : (m + 1) * BLOCK, :]
        out_ref[m] = turn(place, jnp.where(here, jnp.concatenate([part] * blocks, 0), 0.0))


def split(values):
    high = values.astype(BF16)
    rest = values - high.astype(F32)
    mid = rest.astype(BF16)
    return high, mid, (rest - mid.astype(F32)).astype(BF16)


def turn(place, values):
    high, mid, low = split(values)
    return (nt(place, high) + nt(place, mid)) + nt(place, low)


def coefficient_kernel(bands, *refs):
    inverse_ref, out_ref = refs[bands:]
    total = band_total(refs[:bands])
    owned = out_ref.shape[2]
    chunks = 8 * owned // LANES
    inverse = inverse_ref[:KPAD, :KPAD]
    eight = jnp.concatenate([total[8 * c : 8 * c + 8] for c in range(chunks)], 1)
    ninth = jnp.concatenate([total[8 * chunks + c : 8 * chunks + c + 1] for c in range(chunks)], 1)
    coeff = nn(inverse[:, :8], eight, precision=HIGH) + inverse[:, 8:9] * ninth
    for m in range(8):
        out_ref[:, m, :] = coeff[:NPOLY, m * owned : (m + 1) * owned]


def call(kernel, operands, shapes, scratch=(), hbm=False, flops=20_000_000):
    vmem = pl.BlockSpec(memory_space=pltpu.VMEM)
    in_specs = [vmem] * len(operands)
    moved = sum(x.size * x.dtype.itemsize for x in (*operands, *shapes))
    if hbm:
        in_specs = [pl.BlockSpec(memory_space=pltpu.HBM)] * len(operands)
        operands = [pltpu.with_memory_space_constraint(x, pltpu.HBM) for x in operands]
    return pl.pallas_call(
        kernel,
        out_shape=shapes,
        in_specs=in_specs,
        out_specs=[vmem] * len(shapes),
        scratch_shapes=list(scratch),
        compiler_params=pltpu.CompilerParams(vmem_limit_bytes=14 * 1024 * 1024),
        cost_estimate=pl.CostEstimate(flops=flops, bytes_accessed=moved, transcendentals=0),
    )(*operands)


def share_base(x, last=(), ties=(2,), ahead=False, again=None):
    devices = lax.axis_size("base")
    mine = [x] + [
        lax.ppermute(x, "base", [(d, d ^ (2 * k)) for d in range(devices)])
        for k in range(1, devices // 2)
    ]
    if ahead:
        mine[2:3] = after(mine[2:3], (), flops=5_000_000_000)
    if last:
        for k, y in zip(ties, after([mine[k] for k in ties], last)):
            mine[k] = y
    sent = list(mine)
    if again is not None:
        (sent[0],) = after([again], last)
    other = [lax.ppermute(y, "base", [(d, d ^ 1) for d in range(devices)]) for y in sent]
    return mine + other


def share_band(x):
    devices = lax.axis_size("band")
    return [x] + [
        lax.ppermute(x, "band", [(d, d ^ k) for d in range(devices)]) for k in range(1, devices)
    ]


def sum_band(x):
    devices = lax.axis_size("band")
    step = 1
    while 2 * step < devices:
        x = x + lax.ppermute(x, "band", [(d, d ^ step) for d in range(devices)])
        step = 2 * step
    return x, lax.ppermute(x, "band", [(d, d ^ step) for d in range(devices)])


def on_device(visibilities, model, start_gains, penalty, pairs, flags, chan_band):
    tiles, channels, cells = visibilities.shape[1:]
    intervals = start_gains.shape[1]
    owned = start_gains.shape[2]
    blocks = owned // BLOCK
    count = lax.axis_size("base")
    bands = lax.axis_size("band")
    width = tiles * channels

    def shape(*extent, dtype=F32):
        return jax.ShapeDtypeStruct(extent, dtype)

    wide = shape(GAIN_ROWS, 2 * LANES)
    narrow = shape(GAIN_ROWS, LANES)
    single = shape(BLOCK, 2 * LANES)
    terms = shape(TERM_ROWS, LANES)
    square = shape(2 * LANES, LANES)

    greeting, again = call(
        functools.partial(greet_kernel, blocks, intervals),
        (pairs, start_gains, penalty.reshape(1, owned), flags),
        [shape(GAIN_ROWS + 8, LANES)] * 2,
        [
            pltpu.SMEM(pairs.shape, jnp.int32),
            pltpu.VMEM(start_gains.shape, F32),
            pltpu.VMEM((1, owned), F32),
            pltpu.VMEM(flags.shape, jnp.int32),
            pltpu.SemaphoreType.DMA((4,)),
        ],
        hbm=True,
    )
    products, keys, at, basis, chans = call(
        functools.partial(prepare_kernel, blocks, intervals, bands),
        (
            pairs,
            chan_band.reshape(1, channels),
            flags,
            visibilities.reshape(8, width, cells),
            model.reshape(8, width, cells),
        ),
        [
            shape(PRODUCTS, BLOCK // 2, BLOCK, 2 * tiles * intervals),
            square,
            square,
            square,
            shape(8, 2 * LANES),
        ],
        [
            pltpu.SMEM(pairs.shape, jnp.int32),
            pltpu.VMEM((1, channels), jnp.int32),
            pltpu.VMEM(flags.shape, jnp.int32),
            *[pltpu.VMEM((8, width, cells), BF16)] * 2,
            pltpu.VMEM((8, cells, width), F32),
            pltpu.SemaphoreType.DMA((5,)),
        ],
        hbm=True,
        flops=2_000_000_000,
    )
    greetings = share_base(greeting, last=(chans,), again=again)
    scratch = [
        pltpu.VMEM((12, BLOCK // 2, LANES), F32),
        pltpu.VMEM((2, 12, BLOCK // 2, LANES), F32),
        pltpu.VMEM((12, BLOCK // 2, LANES), F32),
    ]

    gains, message = call(
        functools.partial(first_kernel, count),
        (*greetings, keys, products),
        [narrow, terms],
        scratch,
    )
    z, pen, scale, select, turned = call(
        functools.partial(state_kernel, count, blocks, intervals),
        (*greetings, keys, at, gains, chans, basis),
        [
            wide,
            single,
            single,
            shape(2 * LANES, count * LANES, dtype=BF16),
            shape(3 * KPAD, LANES, dtype=BF16),
        ],
    )
    pieces = share_base(message, last=(scale,), ties=(1, 2))
    gains, message = call(
        functools.partial(step_kernel, count),
        (*pieces, select, z, pen, scale, products),
        [wide, terms],
        scratch,
    )
    (part,) = call(first_total_kernel, (gains, basis), [shape(GAIN_ROWS + KPAD, LANES)])
    z, dual, inverse = call(
        first_consensus_kernel, (*sum_band(part), gains, basis), [wide, wide, narrow]
    )
    pieces = share_base(message, last=(z,), ties=(3,), ahead=True)
    gains, message = call(
        functools.partial(step_kernel, count),
        (*pieces, select, z, pen, scale, products),
        [wide, terms],
        scratch,
    )
    (part,) = call(total_kernel, (gains, dual, basis), [narrow])
    z, dual = call(consensus_kernel, (*sum_band(part), gains, dual, basis, inverse), [wide, wide])
    pieces = share_base(message, last=(z,), ties=(3,), ahead=True)
    chunks = 8 * owned // LANES
    gains, part = call(
        functools.partial(last_kernel, count, blocks, intervals),
        (*pieces, select, z, pen, scale, dual, turned),
        [narrow, shape(8 * chunks + -(-chunks // 8) * 8, LANES)],
    )
    parts = share_band(part)
    (out,) = call(
        functools.partial(gains_kernel, blocks, intervals),
        (gains,),
        [shape(8, intervals, owned)],
    )
    (coefficients,) = call(
        functools.partial(coefficient_kernel, bands),
        (*parts, inverse),
        [shape(NPOLY, 8, owned)],
    )
    return (out, jnp.transpose(coefficients, (1, 0, 2)))


def solution(mesh):
    in_specs = (
        P(None, "base", "band", None),
        P(None, "base", "band", None),
        P(None, "band", "base"),
        P("base"),
        P("base", None),
        P("base", None),
        P("band"),
    )
    out_specs = (P(None, "band", "base"), P(None, None, "base"))
    return jax.shard_map(
        on_device, mesh=mesh, in_specs=in_specs, out_specs=out_specs, check_vma=False
    )
```

```python
import functools

import jax
import jax.numpy as jnp
from jax import lax
from jax.experimental import pallas as pl
from jax.experimental.pallas import tpu as pltpu
from jax.sharding import PartitionSpec as P

BLOCK = 16
NPOLY = 9
KPAD = 16
ITERS = 3
LANES = 128
F32 = jnp.float32
BF16 = jnp.bfloat16
HIGH = lax.Precision.HIGHEST

ridge = 0.5

GAIN_ROWS = 8 * BLOCK
TERM_ROWS = 12 * BLOCK
PRODUCTS = 48
CROSS = ((0, 1), (0, 2), (0, 3), (1, 2), (1, 3), (2, 3))


def nt(left, right, **kw):
    return lax.dot_general(
        left, right, (((1,), (1,)), ((), ())), preferred_element_type=F32, **kw
    )


def nn(left, right, **kw):
    return lax.dot_general(
        left, right, (((1,), (0,)), ((), ())), preferred_element_type=F32, **kw
    )


def pick(values, select, dot=nt):
    high = values.astype(BF16)
    low = (values - high.astype(F32)).astype(BF16)
    rows = values.shape[0]
    out = dot(jnp.concatenate([high, low], 0), select)
    return out[:rows] + out[rows:]


def iota(shape, axis):
    return lax.broadcasted_iota(jnp.int32, shape, axis)


def add(terms):
    total = None
    for sign, x, y in terms:
        if total is None:
            total = x * y if sign > 0 else -(x * y)
        else:
            total = total + x * y if sign > 0 else total - x * y
    return total


def apply_gains(pairs, gains, turned):
    re, im = [], []
    for r in range(2):
        for c in range(2):
            to_re, to_im = [], []
            for k in range(2):
                for n in range(2):
                    x_re, x_im = pairs(k, r, n, c) if turned else pairs(r, k, c, n)
                    g_re, g_im = gains[2 * k + n], gains[4 + 2 * k + n]
                    sign = -1 if turned else 1
                    to_re += [(1, x_re, g_re), (-sign, x_im, g_im)]
                    to_im += [(1, x_re, g_im), (sign, x_im, g_re)]
            re.append(add(to_re))
            im.append(add(to_im))
    return re + im


def square(gains):
    return [
        add([(1, gains[n], gains[n]) for n in (0, 2, 4, 6)]),
        add([(1, gains[n], gains[n]) for n in (1, 3, 5, 7)]),
        add([(1, gains[n], gains[n + 1]) for n in (0, 2, 4, 6)]),
        add([(1, gains[0], gains[5]), (-1, gains[4], gains[1])])
        + add([(1, gains[2], gains[7]), (-1, gains[6], gains[3])]),
    ]


def outer_first(own, cross, q):
    out = []
    for r in range(2):
        x_re, x_im = cross(r, 0, r, 1)
        twice = add([(1, x_re, q[2]), (-1, x_im, q[3])])
        out.append(add([(1, own[r][0], q[0]), (1, own[r][1], q[1])]) + (twice + twice))
    (a_re, a_im), (b_re, b_im) = cross(0, 0, 1, 0), cross(0, 1, 1, 1)
    (c_re, c_im), (d_re, d_im) = cross(0, 0, 1, 1), cross(0, 1, 1, 0)
    out.append(
        add([(1, a_re, q[0]), (1, b_re, q[1]), (1, c_re + d_re, q[2]), (-1, c_im - d_im, q[3])])
    )
    out.append(
        add([(1, a_im, q[0]), (1, b_im, q[1]), (1, c_im + d_im, q[2]), (1, c_re - d_re, q[3])])
    )
    return out


def outer_second(own, cross, q):
    out = []
    for c in range(2):
        x_re, x_im = cross(0, c, 1, c)
        twice = add([(1, x_re, q[2]), (1, x_im, q[3])])
        out.append(add([(1, own[0][c], q[0]), (1, own[1][c], q[1])]) + (twice + twice))
    (a_re, a_im), (b_re, b_im) = cross(0, 0, 0, 1), cross(1, 0, 1, 1)
    (c_re, c_im), (d_re, d_im) = cross(0, 0, 1, 1), cross(0, 1, 1, 0)
    out.append(
        add([(1, a_re, q[0]), (1, b_re, q[1]), (1, c_re + d_re, q[2]), (1, c_im + d_im, q[3])])
    )
    out.append(
        add([(-1, a_im, q[0]), (-1, b_im, q[1]), (1, c_re - d_re, q[3]), (-1, c_im - d_im, q[2])])
    )
    return out


def slot_key(index, pairs, scale, intervals):
    at = index // intervals
    tiles = len(pairs)
    block = jnp.zeros(index.shape, F32)
    for slot in range(2 * tiles):
        value = pairs[slot % tiles][slot // tiles]
        block = jnp.where(at == slot, value.astype(F32), block)
    if scale > 1:
        block = block * scale + (index % intervals).astype(F32)
    return block


def scalar_pairs(pair_ref):
    return [[pair_ref[t, side] for side in range(2)] for t in range(pair_ref.shape[0])]


def owner_key(index, me, blocks, intervals, none, scale=None):
    at = index // intervals
    key = me * blocks + at
    if scale != 1:
        key = key * intervals + index % intervals
    return jnp.where(at < blocks, key, none).astype(F32)


def cell_weights(pairs, flags):
    cells = flags.shape[1]
    cell = iota((1, cells), 1)
    diagonal = (cell // BLOCK == cell % BLOCK).astype(F32)
    rows = []
    for t, pair in enumerate(pairs):
        same = (pair[0] == pair[1]).astype(F32)
        rows.append(flags[t : t + 1, :] * (1.0 - same * diagonal))
    return rows


def greet_kernel(
    blocks, intervals, pair_hbm, start_hbm, penalty_hbm, flag_hbm, out_ref, pair_ref, start_ref,
    penalty_ref, flag_ref, sems
):
    copies = [
        pltpu.make_async_copy(source, target, sems.at[n])
        for n, (source, target) in enumerate(
            [
                (start_hbm, start_ref),
                (pair_hbm, pair_ref),
                (flag_hbm, flag_ref),
                (penalty_hbm, penalty_ref),
            ]
        )
    ]
    for copy in copies:
        copy.start()
    for copy in copies[1:]:
        copy.wait()
    owned = blocks * BLOCK
    cells = flag_ref.shape[1]
    me = lax.axis_index("base")
    pairs = scalar_pairs(pair_ref)
    tiles = len(pairs)
    weights = cell_weights(pairs, flag_ref[...].astype(F32))
    lane = iota((cells, LANES), 1)
    cell = iota((cells, LANES), 0)
    at, inside = lane // BLOCK, lane % BLOCK
    member = jnp.where(at < tiles, cell // BLOCK, cell % BLOCK) == inside
    station_w = jnp.zeros((8, LANES), F32)
    for t in range(tiles):
        fold = (member & (at % tiles == t) & (at < 2 * tiles)).astype(BF16)
        station_w = station_w + nn(jnp.broadcast_to(weights[t], (8, cells)).astype(BF16), fold)
    lane = iota((8, LANES), 1)
    row = iota((8, LANES), 0)
    wide = intervals // BLOCK
    slot_at = jnp.where(lane // BLOCK < 2 * tiles, slot_key(lane * wide, pairs, 1, intervals), -2.0)
    owner_at = jnp.where(lane // BLOCK < blocks, (me * blocks + lane // BLOCK).astype(F32), -2.0)
    keys = jnp.where(row == 0, slot_key(lane, pairs, intervals, intervals), 0.0)
    keys = jnp.where(row == 1, owner_key(lane, me, blocks, intervals, -2), keys)
    keys = jnp.where(row == 3, owner_at, keys)
    keys = jnp.where(row == 4, station_w, keys)
    out_ref[GAIN_ROWS:, :] = jnp.where(row == 5, slot_at, keys)
    out_ref[GAIN_ROWS + 2 : GAIN_ROWS + 3, :owned] = penalty_ref[...]
    copies[0].wait()
    place = (iota((BLOCK, owned), 0) == iota((BLOCK, owned), 1) % BLOCK).astype(BF16)
    here = iota((LANES, owned), 0) // intervals == iota((LANES, owned), 1) // BLOCK
    parts = []
    for m in range(8):
        plane = jnp.concatenate([start_ref[m]] * (LANES // intervals), 0)
        parts.append(jnp.where(here, plane, 0.0))
    parts = jnp.concatenate(parts, 0)
    high = parts.astype(BF16)
    low = (parts - high.astype(F32)).astype(BF16)
    turned = nt(place, high) + nt(place, low)
    for m in range(8):
        out_ref[m * BLOCK : (m + 1) * BLOCK, :] = turned[:, m * LANES : (m + 1) * LANES]


def prepare_kernel(
    blocks, intervals, bands, pair_hbm, chan_hbm, flag_hbm, vis_hbm, model_hbm, prod_ref, key_ref,
    at_ref, basis_ref, chans_ref, pair_ref, chan_ref, flag_ref, vis_ref, model_ref, mt_ref, sems
):
    planes, width, cells = vis_ref.shape
    moves = [
        (model_hbm, model_ref),
        (vis_hbm, vis_ref),
        (pair_hbm, pair_ref),
        (chan_hbm, chan_ref),
        (flag_hbm, flag_ref),
    ]
    copies = [
        pltpu.make_async_copy(source, target, sems.at[n])
        for n, (source, target) in enumerate(moves)
    ]
    for copy in copies:
        copy.start()
    for copy in copies[2:]:
        copy.wait()
    pairs = scalar_pairs(pair_ref)
    tiles = len(pairs)
    channels = width // tiles
    me = lax.axis_index("base")
    row = iota((2 * LANES, LANES), 0)
    lane = iota((2 * LANES, LANES), 1)
    for ref, scale in ((key_ref, intervals), (at_ref, 1)):
        ref[...] = jnp.where(
            row < LANES,
            slot_key(row, pairs, scale, intervals),
            owner_key(row - LANES, me, blocks, intervals, -1, scale),
        )
    band_at = lax.axis_index("band")
    local = chan_ref[...] - band_at * intervals
    chan = (band_at * channels + iota((1, channels), 1)).astype(F32)
    xpos = -1.0 + (2.0 * chan + 1.0) / (channels * bands)
    member = (iota((2 * LANES, channels), 0) % intervals == local).astype(F32)
    chans = jnp.sum(member, 1, keepdims=True)
    chans_ref[...] = nt(jnp.ones((8, channels), BF16), member.astype(BF16))
    centre = jnp.sum(member * xpos, 1, keepdims=True) / chans
    terms = [jnp.ones((2 * LANES, LANES), F32), jnp.broadcast_to(centre, (2 * LANES, LANES))]
    for order in range(2, NPOLY):
        terms.append(2.0 * terms[1] * terms[-1] - terms[-2])
    basis = jnp.zeros((2 * LANES, LANES), F32)
    for order in range(NPOLY):
        basis = jnp.where(lane % KPAD == order, terms[order], basis)
    basis_ref[...] = jnp.where(row // intervals == lane // KPAD, basis, 0.0)
    lanes = 2 * tiles * intervals
    row = iota((lanes, 2 * width), 0)
    lane = iota((lanes, 2 * width), 1)
    at = jnp.concatenate([local] * (2 * tiles), 1)
    fold = ((row // intervals == lane // channels) & (row % intervals == at)).astype(BF16)
    ident = (iota((cells, cells), 0) == iota((cells, cells), 1)).astype(BF16)
    rows = cell_weights(pairs, flag_ref[...].astype(F32))
    weight = jnp.concatenate([jnp.broadcast_to(w, (channels, cells)) for w in rows], 0)
    half = cells // 2

    def put(at, products):
        beside = [jnp.concatenate([x[:half], x[half:]], 1) for x in products]
        count = len(products)
        shape = (count,) + prod_ref.shape[1:]
        prod_ref[at : at + count] = pick(jnp.concatenate(beside, 0), fold).reshape(shape)

    copies[0].wait()
    for m in range(planes):
        masked = (model_ref[m].astype(F32) * weight).astype(BF16)
        mt_ref[m] = nt(ident, masked)
    put(32, [mt_ref[x] * mt_ref[x] + mt_ref[4 + x] * mt_ref[4 + x] for x in range(4)])
    put(36, [mt_ref[x] * mt_ref[y] + mt_ref[4 + x] * mt_ref[4 + y] for x, y in CROSS])
    put(42, [mt_ref[4 + x] * mt_ref[y] - mt_ref[x] * mt_ref[4 + y] for x, y in CROSS])
    copies[1].wait()
    for x in range(4):
        v_re, v_im = nt(ident, vis_ref[x]), nt(ident, vis_ref[4 + x])
        put(4 * x, [v_re * mt_ref[y] + v_im * mt_ref[4 + y] for y in range(4)])
        put(16 + 4 * x, [v_im * mt_ref[y] - v_re * mt_ref[4 + y] for y in range(4)])


def tie_kernel(*refs):
    pass


def after(values, others, flops=0):
    place = pl.BlockSpec(memory_space=pl.ANY)
    return pl.pallas_call(
        tie_kernel,
        out_shape=[jax.ShapeDtypeStruct(x.shape, x.dtype) for x in values],
        in_specs=[place] * (len(values) + len(others)),
        out_specs=[place] * len(values),
        input_output_aliases={n: n for n in range(len(values))},
        compiler_params=pltpu.CompilerParams(vmem_limit_bytes=1024 * 1024),
        cost_estimate=pl.CostEstimate(flops=flops, bytes_accessed=0, transcendentals=0),
    )(*values, *others)


def normal_terms(gains, prod_ref, first_s, second_s, a_s, out_ref):
    half = BLOCK // 2
    low = iota((half, LANES), 1) < LANES // 2

    def swap(x):
        return pltpu.roll(x, LANES // 2, 1)

    first, second = [], [[], []]
    for m in range(8):
        part = [gains[m * BLOCK + h * half : m * BLOCK + (h + 1) * half] for h in range(2)]
        first.append(jnp.where(low, part[0], swap(part[1])))
        for h in range(2):
            second[h].append(jnp.where(low, swap(part[h]), part[h]))
    for n, x in enumerate(first + square(first)):
        first_s[n] = x
    for h in range(2):
        for n, x in enumerate(second[h] + square(second[h])):
            second_s[h, n] = x

    def step(i, totals):
        partial = None
        new = []
        one = [first_s[n, pl.ds(i, 1), :] for n in range(12)]
        for h in range(2):
            two = [second_s[h, n] for n in range(12)]

            def load(n):
                return prod_ref[n, i, h * half : (h + 1) * half, :]

            def pairs(r, k, c, n):
                at = (2 * r + k) * 4 + 2 * c + n
                return load(at), load(16 + at)

            def cross(r, k, c, n):
                at = CROSS.index((2 * r + k, 2 * c + n))
                return load(36 + at), load(42 + at)

            own = [[load(32 + 2 * r + k) for k in range(2)] for r in range(2)]
            terms = apply_gains(pairs, two[:8], False) + outer_first(own, cross, two[8:])
            partial = terms if partial is None else [x + y for x, y in zip(partial, terms)]
            terms = apply_gains(pairs, one[:8], True) + outer_second(own, cross, one[8:])
            new += [x + y for x, y in zip(totals[12 * h : 12 * (h + 1)], terms)]
        for k in range(12):
            a_s[k, pl.ds(i, 1), :] = jnp.sum(partial[k], 0, keepdims=True)
        return tuple(new)

    zero = jnp.zeros((half, LANES), F32)
    totals = lax.fori_loop(0, half, step, (zero,) * 24, unroll=4)
    for k in range(12):
        mine = a_s[k]
        for h in range(2):
            other = totals[12 * h + k]
            other = other + swap(other)
            at = k * BLOCK + h * half
            out_ref[at : at + half, :] = jnp.where(low, swap(mine) if h else mine, other)


def key_match(rows, lanes):
    count = lanes.shape[1] // LANES
    return (jnp.concatenate([rows] * count, 1) == lanes).astype(BF16)


def beside(refs, count):
    return jnp.concatenate([p[...] for p in refs[:count]], 1), refs[count:]


def first_kernel(count, *refs):
    every, refs = beside(refs, count)
    key_ref, prod_ref, gains_ref, out_ref = refs[:4]
    scratch = refs[4:]
    select = key_match(key_ref[:LANES, :], every[GAIN_ROWS + 1 : GAIN_ROWS + 2])
    gains = pick(every[:GAIN_ROWS], select)
    gains_ref[...] = gains
    normal_terms(gains, prod_ref, *scratch, out_ref)


def state_kernel(count, blocks, intervals, *refs):
    every, refs = beside(refs, count)
    key_ref, at_ref, gains_ref, chans_ref, basis_ref = refs[:5]
    z_ref, pen_ref, scale_ref, select_ref, turned_ref = refs[5:]
    place = (iota((KPAD, LANES), 0) == iota((KPAD, LANES), 1) % KPAD).astype(BF16)
    for n, piece in enumerate(split(turn(place, basis_ref[LANES:, :]))):
        turned_ref[n * KPAD : (n + 1) * KPAD, :] = piece
    rows = every[GAIN_ROWS:]
    z_ref[:, :LANES] = gains_ref[...]
    z_ref[:, LANES:] = every[:GAIN_ROWS, :LANES]
    select_ref[...] = key_match(key_ref[...], rows[0:1])
    lanes = rows.shape[1]
    diagonal = iota((BLOCK, lanes), 0) == iota((BLOCK, lanes), 1) % BLOCK
    at = at_ref[...]
    pen = pick(jnp.where(diagonal, rows[2:3], 0.0), key_match(at, rows[3:4]))
    unused = iota(pen.shape, 1) >= LANES + blocks * intervals
    pen_ref[...] = jnp.where(unused, 1.0, pen)
    weights = pick(jnp.where(diagonal, rows[4:5], 0.0), key_match(at, rows[5:6]))
    scale_ref[...] = 1.0 / jnp.maximum(weights * chans_ref[0:1, :], 1.0)


def solve(normal, scale, pen, consensus):
    part = [normal[BLOCK * k : BLOCK * (k + 1)] * scale for k in range(12)]
    rhs = [part[m] + pen * consensus[BLOCK * m : BLOCK * (m + 1)] for m in range(8)]
    h_first = part[8] + pen
    h_second = part[9] + pen
    h_real, h_imag = part[10], part[11]
    determ = h_first * h_second - h_real * h_real - h_imag * h_imag
    over = 1.0 / determ
    d_first, d_second = h_first * over, h_second * over
    d_real, d_imag = h_real * over, h_imag * over
    out = [None] * 8
    for r in range(2):
        x_re, y_re = rhs[2 * r], rhs[2 * r + 1]
        x_im, y_im = rhs[4 + 2 * r], rhs[5 + 2 * r]
        out[2 * r] = x_re * d_second - (y_re * d_real + y_im * d_imag)
        out[4 + 2 * r] = x_im * d_second - (y_im * d_real - y_re * d_imag)
        out[2 * r + 1] = y_re * d_first - (x_re * d_real - x_im * d_imag)
        out[5 + 2 * r] = y_im * d_first - (x_im * d_real + x_re * d_imag)
    return jnp.concatenate(out, 0)


def step_kernel(count, *refs):
    every, refs = beside(refs, count)
    select_ref, z_ref, pen_ref, scale_ref, prod_ref, gains_ref, out_ref = refs[:7]
    scratch = refs[7:]
    normal = pick(every, select_ref[...])
    gains = solve(normal, scale_ref[...], pen_ref[...], z_ref[...])
    gains_ref[...] = gains
    normal_terms(gains[:, :LANES], prod_ref, *scratch, out_ref)


def first_total_kernel(gains_ref, basis_ref, out_ref):
    basis = basis_ref[...]
    total = nn(gains_ref[...], basis, precision=HIGH)
    part = basis[: basis.shape[0] // 8]
    gram = lax.dot_general(
        part, part, (((0,), (0,)), ((), ())), preferred_element_type=F32, precision=HIGH
    )
    out_ref[:GAIN_ROWS, :] = total
    out_ref[GAIN_ROWS:, :] = gram[:KPAD]


def total_kernel(gains_ref, dual_ref, basis_ref, out_ref):
    out_ref[...] = nn(gains_ref[...] + dual_ref[...], basis_ref[...], precision=HIGH)


def inverse_of_three(d):
    def minor(r, c):
        (r0, r1), (c0, c1) = [[k for k in range(3) if k != n] for n in (r, c)]
        value = d[r0][c0] * d[r1][c1] - d[r0][c1] * d[r1][c0]
        return value if (r + c) % 2 == 0 else -value

    minors = [[minor(r, c) for c in range(3)] for r in range(3)]
    over = 1.0 / (d[0][0] * minors[0][0] + d[0][1] * minors[0][1] + d[0][2] * minors[0][2])
    return [[minors[c][r] * over for c in range(3)] for r in range(3)]


def invert(gram):
    row, lane = iota(gram.shape, 0), iota(gram.shape, 1)
    inner = (row < NPOLY) & (lane < NPOLY)
    work = jnp.where(inner, gram + jnp.where(row == lane, ridge, 0.0), 0.0)
    lanes = iota((1, gram.shape[1]), 1)
    for p in range(0, NPOLY, 3):
        rows = [work[p + a : p + a + 1] for a in range(3)]
        block = inverse_of_three(
            [
                [jnp.broadcast_to(rows[a][:, p + b : p + b + 1], lanes.shape) for b in range(3)]
                for a in range(3)
            ]
        )
        columns = [work[:, p + b : p + b + 1] for b in range(3)]
        here = (lane >= p) & (lane < p + 3)
        rows = [jnp.where(here[:1], 0.0, x) for x in rows]
        pivots = []
        for a in range(3):
            pivot = block[a][0] * rows[0] + block[a][1] * rows[1] + block[a][2] * rows[2]
            for b in range(3):
                pivot = jnp.where(lanes == p + b, block[a][b], pivot)
            pivots.append(pivot)
        work = jnp.where(here, 0.0, work)
        for b in range(3):
            work = work - columns[b] * pivots[b]
        for a in range(3):
            work = jnp.where(row == p + a, pivots[a], work)
    return work


def settle(total, inverse, basis_ref, gains, z_ref, dual_ref):
    coeff = nn(total, inverse, precision=HIGH)
    consensus = nt(coeff, basis_ref[...], precision=HIGH)
    z_ref[...] = 2.0 * consensus - gains
    dual_ref[...] = gains - consensus


def band_total(refs):
    totals = [ref[...] for ref in refs]
    while len(totals) > 1:
        totals = [totals[n] + totals[n + 1] for n in range(0, len(totals), 2)]
    return totals[0]


def first_consensus_kernel(
    one_ref, two_ref, gains_ref, basis_ref, z_ref, dual_ref, inverse_ref
):
    total = one_ref[...] + two_ref[...]
    small = invert(total[GAIN_ROWS:])
    row, lane = iota((LANES, LANES), 0), iota((LANES, LANES), 1)
    spread = ((row == lane % KPAD) & (row < KPAD)).astype(F32)
    wide = nn(jnp.concatenate([small] * (LANES // KPAD), 0), spread, precision=HIGH)
    inverse = jnp.where(row // KPAD == lane // KPAD, wide, 0.0)
    inverse_ref[...] = inverse
    settle(total[:GAIN_ROWS], inverse, basis_ref, gains_ref[...], z_ref, dual_ref)


def consensus_kernel(
    one_ref, two_ref, gains_ref, old_ref, basis_ref, inverse_ref, z_ref, dual_ref
):
    total = one_ref[...] + two_ref[...]
    gains = gains_ref[...] + old_ref[...]
    settle(total, inverse_ref[...], basis_ref, gains, z_ref, dual_ref)


def last_kernel(count, blocks, intervals, *refs):
    every, refs = beside(refs, count)
    select_ref, z_ref, pen_ref, scale_ref, dual_ref, turned_ref, gains_ref, out_ref = refs
    own = slice(LANES, 2 * LANES)
    normal = pick(every, select_ref[own, :])
    gains = solve(normal, scale_ref[:, own], pen_ref[:, own], z_ref[:, own])
    gains_ref[...] = gains
    owned = blocks * BLOCK
    here = iota((owned, LANES), 0) // BLOCK == iota((owned, LANES), 1) // intervals
    summed = gains + dual_ref[:, own]
    parts = [summed[m * BLOCK : (m + 1) * BLOCK] for m in range(8)]
    parts = [jnp.where(here, jnp.concatenate([x] * blocks, 0), 0.0) for x in parts]
    high, mid, low = split(jnp.concatenate(parts, 0))
    turned = turned_ref[...]
    first, second = nt(turned, high), nt(turned[: 2 * KPAD], mid)
    small = first[2 * KPAD :] + second[KPAD:] + nt(turned[:KPAD], low)
    total = first[:KPAD] + ((first[KPAD : 2 * KPAD] + second[:KPAD]) + small)
    chunks = total.shape[1] // LANES
    for c in range(chunks):
        lanes = slice(c * LANES, (c + 1) * LANES)
        out_ref[8 * c : 8 * c + 8, :] = total[:8, lanes]
        out_ref[8 * chunks + c : 8 * chunks + c + 1, :] = total[8:9, lanes]
    rest = 9 * chunks
    out_ref[rest:, :] = jnp.zeros((out_ref.shape[0] - rest, LANES), F32)


def gains_kernel(blocks, intervals, gains_ref, out_ref):
    owned = blocks * BLOCK
    place = (iota((intervals, LANES), 0) == iota((intervals, LANES), 1) % intervals).astype(BF16)
    here = iota((owned, LANES), 0) // BLOCK == iota((owned, LANES), 1) // intervals
    for m in range(8):
        part = gains_ref[m * BLOCK : (m + 1) * BLOCK, :]
        out_ref[m] = turn(place, jnp.where(here, jnp.concatenate([part] * blocks, 0), 0.0))


def split(values):
    high = values.astype(BF16)
    rest = values - high.astype(F32)
    mid = rest.astype(BF16)
    return high, mid, (rest - mid.astype(F32)).astype(BF16)


def turn(place, values):
    high, mid, low = split(values)
    return (nt(place, high) + nt(place, mid)) + nt(place, low)


def coefficient_kernel(bands, *refs):
    inverse_ref, out_ref = refs[bands:]
    total = band_total(refs[:bands])
    owned = out_ref.shape[2]
    chunks = 8 * owned // LANES
    inverse = inverse_ref[:KPAD, :KPAD]
    eight = jnp.concatenate([total[8 * c : 8 * c + 8] for c in range(chunks)], 1)
    ninth = jnp.concatenate([total[8 * chunks + c : 8 * chunks + c + 1] for c in range(chunks)], 1)
    coeff = nn(inverse[:, :8], eight, precision=HIGH) + inverse[:, 8:9] * ninth
    for m in range(8):
        out_ref[:, m, :] = coeff[:NPOLY, m * owned : (m + 1) * owned]


def call(kernel, operands, shapes, scratch=(), hbm=False, flops=20_000_000):
    vmem = pl.BlockSpec(memory_space=pltpu.VMEM)
    in_specs = [vmem] * len(operands)
    moved = sum(x.size * x.dtype.itemsize for x in (*operands, *shapes))
    if hbm:
        in_specs = [pl.BlockSpec(memory_space=pltpu.HBM)] * len(operands)
        operands = [pltpu.with_memory_space_constraint(x, pltpu.HBM) for x in operands]
    return pl.pallas_call(
        kernel,
        out_shape=shapes,
        in_specs=in_specs,
        out_specs=[vmem] * len(shapes),
        scratch_shapes=list(scratch),
        compiler_params=pltpu.CompilerParams(vmem_limit_bytes=14 * 1024 * 1024),
        cost_estimate=pl.CostEstimate(flops=flops, bytes_accessed=moved, transcendentals=0),
    )(*operands)


def share_base(x, last=(), ties=(2,), ahead=False):
    devices = lax.axis_size("base")
    mine = [x] + [
        lax.ppermute(x, "base", [(d, d ^ (2 * k)) for d in range(devices)])
        for k in range(1, devices // 2)
    ]
    if ahead:
        mine[3:] = after(mine[3:], (), flops=5_000_000_000)
    if last:
        for k, y in zip(ties, after([mine[k] for k in ties], last)):
            mine[k] = y
    other = [lax.ppermute(y, "base", [(d, d ^ 1) for d in range(devices)]) for y in mine]
    return mine + other


def share_band(x):
    devices = lax.axis_size("band")
    return [x] + [
        lax.ppermute(x, "band", [(d, d ^ k) for d in range(devices)]) for k in range(1, devices)
    ]


def sum_band(x):
    devices = lax.axis_size("band")
    step = 1
    while 2 * step < devices:
        x = x + lax.ppermute(x, "band", [(d, d ^ step) for d in range(devices)])
        step = 2 * step
    return x, lax.ppermute(x, "band", [(d, d ^ step) for d in range(devices)])


def on_device(visibilities, model, start_gains, penalty, pairs, flags, chan_band):
    tiles, channels, cells = visibilities.shape[1:]
    intervals = start_gains.shape[1]
    owned = start_gains.shape[2]
    blocks = owned // BLOCK
    count = lax.axis_size("base")
    bands = lax.axis_size("band")
    width = tiles * channels

    def shape(*extent, dtype=F32):
        return jax.ShapeDtypeStruct(extent, dtype)

    wide = shape(GAIN_ROWS, 2 * LANES)
    narrow = shape(GAIN_ROWS, LANES)
    single = shape(BLOCK, 2 * LANES)
    terms = shape(TERM_ROWS, LANES)
    square = shape(2 * LANES, LANES)

    (greeting,) = call(
        functools.partial(greet_kernel, blocks, intervals),
        (pairs, start_gains, penalty.reshape(1, owned), flags),
        [shape(GAIN_ROWS + 8, LANES)],
        [
            pltpu.SMEM(pairs.shape, jnp.int32),
            pltpu.VMEM(start_gains.shape, F32),
            pltpu.VMEM((1, owned), F32),
            pltpu.VMEM(flags.shape, jnp.int32),
            pltpu.SemaphoreType.DMA((4,)),
        ],
        hbm=True,
    )
    products, keys, at, basis, chans = call(
        functools.partial(prepare_kernel, blocks, intervals, bands),
        (
            pairs,
            chan_band.reshape(1, channels),
            flags,
            visibilities.reshape(8, width, cells),
            model.reshape(8, width, cells),
        ),
        [
            shape(PRODUCTS, BLOCK // 2, BLOCK, 2 * tiles * intervals),
            square,
            square,
            square,
            shape(8, 2 * LANES),
        ],
        [
            pltpu.SMEM(pairs.shape, jnp.int32),
            pltpu.VMEM((1, channels), jnp.int32),
            pltpu.VMEM(flags.shape, jnp.int32),
            *[pltpu.VMEM((8, width, cells), BF16)] * 2,
            pltpu.VMEM((8, cells, width), F32),
            pltpu.SemaphoreType.DMA((5,)),
        ],
        hbm=True,
        flops=2_000_000_000,
    )
    greetings = share_base(greeting, last=(chans,))
    scratch = [
        pltpu.VMEM((12, BLOCK // 2, LANES), F32),
        pltpu.VMEM((2, 12, BLOCK // 2, LANES), F32),
        pltpu.VMEM((12, BLOCK // 2, LANES), F32),
    ]

    gains, message = call(
        functools.partial(first_kernel, count),
        (*greetings, keys, products),
        [narrow, terms],
        scratch,
    )
    z, pen, scale, select, turned = call(
        functools.partial(state_kernel, count, blocks, intervals),
        (*greetings, keys, at, gains, chans, basis),
        [
            wide,
            single,
            single,
            shape(2 * LANES, count * LANES, dtype=BF16),
            shape(3 * KPAD, LANES, dtype=BF16),
        ],
    )
    pieces = share_base(message, last=(scale,), ties=(1, 2))
    gains, message = call(
        functools.partial(step_kernel, count),
        (*pieces, select, z, pen, scale, products),
        [wide, terms],
        scratch,
    )
    (part,) = call(first_total_kernel, (gains, basis), [shape(GAIN_ROWS + KPAD, LANES)])
    z, dual, inverse = call(
        first_consensus_kernel, (*sum_band(part), gains, basis), [wide, wide, narrow]
    )
    pieces = share_base(message, last=(z,), ties=(1, 2), ahead=True)
    gains, message = call(
        functools.partial(step_kernel, count),
        (*pieces, select, z, pen, scale, products),
        [wide, terms],
        scratch,
    )
    (part,) = call(total_kernel, (gains, dual, basis), [narrow])
    z, dual = call(consensus_kernel, (*sum_band(part), gains, dual, basis, inverse), [wide, wide])
    pieces = share_base(message, last=(z,), ties=(1, 2), ahead=True)
    chunks = 8 * owned // LANES
    gains, part = call(
        functools.partial(last_kernel, count, blocks, intervals),
        (*pieces, select, z, pen, scale, dual, turned),
        [narrow, shape(8 * chunks + -(-chunks // 8) * 8, LANES)],
    )
    parts = share_band(part)
    (out,) = call(
        functools.partial(gains_kernel, blocks, intervals),
        (gains,),
        [shape(8, intervals, owned)],
    )
    (coefficients,) = call(
        functools.partial(coefficient_kernel, bands),
        (*parts, inverse),
        [shape(NPOLY, 8, owned)],
    )
    return (out, jnp.transpose(coefficients, (1, 0, 2)))


def solution(mesh):
    in_specs = (
        P(None, "base", "band", None),
        P(None, "base", "band", None),
        P(None, "band", "base"),
        P("base"),
        P("base", None),
        P("base", None),
        P("band"),
    )
    out_specs = (P(None, "band", "base"), P(None, None, "base"))
    return jax.shard_map(
        on_device, mesh=mesh, in_specs=in_specs, out_specs=out_specs, check_vma=False
    )
```

```python
import functools

import jax
import jax.numpy as jnp
from jax import lax
from jax.experimental import pallas as pl
from jax.experimental.pallas import tpu as pltpu
from jax.sharding import PartitionSpec as P

BLOCK = 16
NPOLY = 9
KPAD = 16
ITERS = 3
LANES = 128
F32 = jnp.float32
BF16 = jnp.bfloat16
HIGH = lax.Precision.HIGHEST

ridge = 0.5

GAIN_ROWS = 8 * BLOCK
TERM_ROWS = 12 * BLOCK
PRODUCTS = 48
CROSS = ((0, 1), (0, 2), (0, 3), (1, 2), (1, 3), (2, 3))


def nt(left, right, **kw):
    return lax.dot_general(
        left, right, (((1,), (1,)), ((), ())), preferred_element_type=F32, **kw
    )


def nn(left, right, **kw):
    return lax.dot_general(
        left, right, (((1,), (0,)), ((), ())), preferred_element_type=F32, **kw
    )


def pick(values, select, dot=nt):
    high = values.astype(BF16)
    low = (values - high.astype(F32)).astype(BF16)
    rows = values.shape[0]
    out = dot(jnp.concatenate([high, low], 0), select)
    return out[:rows] + out[rows:]


def iota(shape, axis):
    return lax.broadcasted_iota(jnp.int32, shape, axis)


def add(terms):
    total = None
    for sign, x, y in terms:
        if total is None:
            total = x * y if sign > 0 else -(x * y)
        else:
            total = total + x * y if sign > 0 else total - x * y
    return total


def apply_gains(pairs, gains, turned):
    re, im = [], []
    for r in range(2):
        for c in range(2):
            to_re, to_im = [], []
            for k in range(2):
                for n in range(2):
                    x_re, x_im = pairs(k, r, n, c) if turned else pairs(r, k, c, n)
                    g_re, g_im = gains[2 * k + n], gains[4 + 2 * k + n]
                    sign = -1 if turned else 1
                    to_re += [(1, x_re, g_re), (-sign, x_im, g_im)]
                    to_im += [(1, x_re, g_im), (sign, x_im, g_re)]
            re.append(add(to_re))
            im.append(add(to_im))
    return re + im


def square(gains):
    return [
        add([(1, gains[n], gains[n]) for n in (0, 2, 4, 6)]),
        add([(1, gains[n], gains[n]) for n in (1, 3, 5, 7)]),
        add([(1, gains[n], gains[n + 1]) for n in (0, 2, 4, 6)]),
        add([(1, gains[0], gains[5]), (-1, gains[4], gains[1])])
        + add([(1, gains[2], gains[7]), (-1, gains[6], gains[3])]),
    ]


def outer_first(own, cross, q):
    out = []
    for r in range(2):
        x_re, x_im = cross(r, 0, r, 1)
        twice = add([(1, x_re, q[2]), (-1, x_im, q[3])])
        out.append(add([(1, own[r][0], q[0]), (1, own[r][1], q[1])]) + (twice + twice))
    (a_re, a_im), (b_re, b_im) = cross(0, 0, 1, 0), cross(0, 1, 1, 1)
    (c_re, c_im), (d_re, d_im) = cross(0, 0, 1, 1), cross(0, 1, 1, 0)
    out.append(
        add([(1, a_re, q[0]), (1, b_re, q[1]), (1, c_re + d_re, q[2]), (-1, c_im - d_im, q[3])])
    )
    out.append(
        add([(1, a_im, q[0]), (1, b_im, q[1]), (1, c_im + d_im, q[2]), (1, c_re - d_re, q[3])])
    )
    return out


def outer_second(own, cross, q):
    out = []
    for c in range(2):
        x_re, x_im = cross(0, c, 1, c)
        twice = add([(1, x_re, q[2]), (1, x_im, q[3])])
        out.append(add([(1, own[0][c], q[0]), (1, own[1][c], q[1])]) + (twice + twice))
    (a_re, a_im), (b_re, b_im) = cross(0, 0, 0, 1), cross(1, 0, 1, 1)
    (c_re, c_im), (d_re, d_im) = cross(0, 0, 1, 1), cross(0, 1, 1, 0)
    out.append(
        add([(1, a_re, q[0]), (1, b_re, q[1]), (1, c_re + d_re, q[2]), (1, c_im + d_im, q[3])])
    )
    out.append(
        add([(-1, a_im, q[0]), (-1, b_im, q[1]), (1, c_re - d_re, q[3]), (-1, c_im - d_im, q[2])])
    )
    return out


def slot_key(index, pairs, scale, intervals):
    at = index // intervals
    tiles = len(pairs)
    block = jnp.zeros(index.shape, F32)
    for slot in range(2 * tiles):
        value = pairs[slot % tiles][slot // tiles]
        block = jnp.where(at == slot, value.astype(F32), block)
    if scale > 1:
        block = block * scale + (index % intervals).astype(F32)
    return block


def scalar_pairs(pair_ref):
    return [[pair_ref[t, side] for side in range(2)] for t in range(pair_ref.shape[0])]


def owner_key(index, me, blocks, intervals, none, scale=None):
    at = index // intervals
    key = me * blocks + at
    if scale != 1:
        key = key * intervals + index % intervals
    return jnp.where(at < blocks, key, none).astype(F32)


def cell_weights(pairs, flags):
    cells = flags.shape[1]
    cell = iota((1, cells), 1)
    diagonal = (cell // BLOCK == cell % BLOCK).astype(F32)
    rows = []
    for t, pair in enumerate(pairs):
        same = (pair[0] == pair[1]).astype(F32)
        rows.append(flags[t : t + 1, :] * (1.0 - same * diagonal))
    return rows


def greet_kernel(
    blocks, intervals, pair_hbm, start_hbm, penalty_hbm, flag_hbm, out_ref, pair_ref, start_ref,
    penalty_ref, flag_ref, sems
):
    copies = [
        pltpu.make_async_copy(source, target, sems.at[n])
        for n, (source, target) in enumerate(
            [
                (start_hbm, start_ref),
                (pair_hbm, pair_ref),
                (flag_hbm, flag_ref),
                (penalty_hbm, penalty_ref),
            ]
        )
    ]
    for copy in copies:
        copy.start()
    for copy in copies[1:]:
        copy.wait()
    owned = blocks * BLOCK
    cells = flag_ref.shape[1]
    me = lax.axis_index("base")
    pairs = scalar_pairs(pair_ref)
    tiles = len(pairs)
    weights = cell_weights(pairs, flag_ref[...].astype(F32))
    lane = iota((cells, LANES), 1)
    cell = iota((cells, LANES), 0)
    at, inside = lane // BLOCK, lane % BLOCK
    member = jnp.where(at < tiles, cell // BLOCK, cell % BLOCK) == inside
    station_w = jnp.zeros((8, LANES), F32)
    for t in range(tiles):
        fold = (member & (at % tiles == t) & (at < 2 * tiles)).astype(BF16)
        station_w = station_w + nn(jnp.broadcast_to(weights[t], (8, cells)).astype(BF16), fold)
    lane = iota((8, LANES), 1)
    row = iota((8, LANES), 0)
    wide = intervals // BLOCK
    slot_at = jnp.where(lane // BLOCK < 2 * tiles, slot_key(lane * wide, pairs, 1, intervals), -2.0)
    owner_at = jnp.where(lane // BLOCK < blocks, (me * blocks + lane // BLOCK).astype(F32), -2.0)
    keys = jnp.where(row == 0, slot_key(lane, pairs, intervals, intervals), 0.0)
    keys = jnp.where(row == 1, owner_key(lane, me, blocks, intervals, -2), keys)
    keys = jnp.where(row == 3, owner_at, keys)
    keys = jnp.where(row == 4, station_w, keys)
    out_ref[GAIN_ROWS:, :] = jnp.where(row == 5, slot_at, keys)
    out_ref[GAIN_ROWS + 2 : GAIN_ROWS + 3, :owned] = penalty_ref[...]
    copies[0].wait()
    place = (iota((BLOCK, owned), 0) == iota((BLOCK, owned), 1) % BLOCK).astype(BF16)
    here = iota((LANES, owned), 0) // intervals == iota((LANES, owned), 1) // BLOCK
    parts = []
    for m in range(8):
        plane = jnp.concatenate([start_ref[m]] * (LANES // intervals), 0)
        parts.append(jnp.where(here, plane, 0.0))
    parts = jnp.concatenate(parts, 0)
    high = parts.astype(BF16)
    low = (parts - high.astype(F32)).astype(BF16)
    turned = nt(place, high) + nt(place, low)
    for m in range(8):
        out_ref[m * BLOCK : (m + 1) * BLOCK, :] = turned[:, m * LANES : (m + 1) * LANES]


def prepare_kernel(
    blocks, intervals, bands, pair_hbm, chan_hbm, flag_hbm, vis_hbm, model_hbm, prod_ref, key_ref,
    at_ref, basis_ref, chans_ref, pair_ref, chan_ref, flag_ref, vis_ref, model_ref, mt_ref, sems
):
    planes, width, cells = vis_ref.shape
    moves = [
        (model_hbm, model_ref),
        (vis_hbm, vis_ref),
        (pair_hbm, pair_ref),
        (chan_hbm, chan_ref),
        (flag_hbm, flag_ref),
    ]
    copies = [
        pltpu.make_async_copy(source, target, sems.at[n])
        for n, (source, target) in enumerate(moves)
    ]
    for copy in copies[:1] + copies[2:]:
        copy.start()
    for copy in copies[2:]:
        copy.wait()
    pairs = scalar_pairs(pair_ref)
    tiles = len(pairs)
    channels = width // tiles
    me = lax.axis_index("base")
    row = iota((2 * LANES, LANES), 0)
    lane = iota((2 * LANES, LANES), 1)
    for ref, scale in ((key_ref, intervals), (at_ref, 1)):
        ref[...] = jnp.where(
            row < LANES,
            slot_key(row, pairs, scale, intervals),
            owner_key(row - LANES, me, blocks, intervals, -1, scale),
        )
    band_at = lax.axis_index("band")
    local = chan_ref[...] - band_at * intervals
    chan = (band_at * channels + iota((1, channels), 1)).astype(F32)
    xpos = -1.0 + (2.0 * chan + 1.0) / (channels * bands)
    member = (iota((2 * LANES, channels), 0) % intervals == local).astype(F32)
    chans = jnp.sum(member, 1, keepdims=True)
    chans_ref[...] = nt(jnp.ones((8, channels), BF16), member.astype(BF16))
    centre = jnp.sum(member * xpos, 1, keepdims=True) / chans
    terms = [jnp.ones((2 * LANES, LANES), F32), jnp.broadcast_to(centre, (2 * LANES, LANES))]
    for order in range(2, NPOLY):
        terms.append(2.0 * terms[1] * terms[-1] - terms[-2])
    basis = jnp.zeros((2 * LANES, LANES), F32)
    for order in range(NPOLY):
        basis = jnp.where(lane % KPAD == order, terms[order], basis)
    basis_ref[...] = jnp.where(row // intervals == lane // KPAD, basis, 0.0)
    lanes = 2 * tiles * intervals
    row = iota((lanes, 2 * width), 0)
    lane = iota((lanes, 2 * width), 1)
    at = jnp.concatenate([local] * (2 * tiles), 1)
    fold = ((row // intervals == lane // channels) & (row % intervals == at)).astype(BF16)
    ident = (iota((cells, cells), 0) == iota((cells, cells), 1)).astype(BF16)
    rows = cell_weights(pairs, flag_ref[...].astype(F32))
    weight = jnp.concatenate([jnp.broadcast_to(w, (channels, cells)) for w in rows], 0)
    half = cells // 2

    def put(at, product):
        beside = jnp.concatenate([product[:half], product[half:]], 1)
        prod_ref[at] = pick(beside, fold).reshape(prod_ref.shape[1:])

    copies[0].wait()
    copies[1].start()
    for m in range(planes):
        masked = (model_ref[m].astype(F32) * weight).astype(BF16)
        mt_ref[m] = nt(ident, masked)
    for x in range(4):
        put(32 + x, mt_ref[x] * mt_ref[x] + mt_ref[4 + x] * mt_ref[4 + x])
    for n, (x, y) in enumerate(CROSS):
        x_re, x_im, y_re, y_im = mt_ref[x], mt_ref[4 + x], mt_ref[y], mt_ref[4 + y]
        put(36 + n, x_re * y_re + x_im * y_im)
        put(42 + n, x_im * y_re - x_re * y_im)
    copies[1].wait()
    for x in range(4):
        v_re, v_im = nt(ident, vis_ref[x]), nt(ident, vis_ref[4 + x])
        for y in range(4):
            m_re, m_im = mt_ref[y], mt_ref[4 + y]
            put(4 * x + y, v_re * m_re + v_im * m_im)
            put(16 + 4 * x + y, v_im * m_re - v_re * m_im)


def tie_kernel(*refs):
    pass


def after(values, others, flops=0):
    place = pl.BlockSpec(memory_space=pl.ANY)
    return pl.pallas_call(
        tie_kernel,
        out_shape=[jax.ShapeDtypeStruct(x.shape, x.dtype) for x in values],
        in_specs=[place] * (len(values) + len(others)),
        out_specs=[place] * len(values),
        input_output_aliases={n: n for n in range(len(values))},
        compiler_params=pltpu.CompilerParams(vmem_limit_bytes=1024 * 1024),
        cost_estimate=pl.CostEstimate(flops=flops, bytes_accessed=0, transcendentals=0),
    )(*values, *others)


def normal_terms(gains, prod_ref, first_s, second_s, a_s, out_ref):
    half = BLOCK // 2
    low = iota((half, LANES), 1) < LANES // 2

    def swap(x):
        return pltpu.roll(x, LANES // 2, 1)

    first, second = [], [[], []]
    for m in range(8):
        part = [gains[m * BLOCK + h * half : m * BLOCK + (h + 1) * half] for h in range(2)]
        first.append(jnp.where(low, part[0], swap(part[1])))
        for h in range(2):
            second[h].append(jnp.where(low, swap(part[h]), part[h]))
    for n, x in enumerate(first + square(first)):
        first_s[n] = x
    for h in range(2):
        for n, x in enumerate(second[h] + square(second[h])):
            second_s[h, n] = x

    def step(i, totals):
        partial = None
        new = []
        one = [first_s[n, pl.ds(i, 1), :] for n in range(12)]
        for h in range(2):
            two = [second_s[h, n] for n in range(12)]

            def load(n):
                return prod_ref[n, i, h * half : (h + 1) * half, :]

            def pairs(r, k, c, n):
                at = (2 * r + k) * 4 + 2 * c + n
                return load(at), load(16 + at)

            def cross(r, k, c, n):
                at = CROSS.index((2 * r + k, 2 * c + n))
                return load(36 + at), load(42 + at)

            own = [[load(32 + 2 * r + k) for k in range(2)] for r in range(2)]
            terms = apply_gains(pairs, two[:8], False) + outer_first(own, cross, two[8:])
            partial = terms if partial is None else [x + y for x, y in zip(partial, terms)]
            terms = apply_gains(pairs, one[:8], True) + outer_second(own, cross, one[8:])
            new += [x + y for x, y in zip(totals[12 * h : 12 * (h + 1)], terms)]
        for k in range(12):
            a_s[k, pl.ds(i, 1), :] = jnp.sum(partial[k], 0, keepdims=True)
        return tuple(new)

    zero = jnp.zeros((half, LANES), F32)
    totals = lax.fori_loop(0, half, step, (zero,) * 24, unroll=4)
    for k in range(12):
        mine = a_s[k]
        for h in range(2):
            other = totals[12 * h + k]
            other = other + swap(other)
            at = k * BLOCK + h * half
            out_ref[at : at + half, :] = jnp.where(low, swap(mine) if h else mine, other)


def key_match(rows, lanes):
    count = lanes.shape[1] // LANES
    return (jnp.concatenate([rows] * count, 1) == lanes).astype(BF16)


def beside(refs, count):
    return jnp.concatenate([p[...] for p in refs[:count]], 1), refs[count:]


def first_kernel(count, *refs):
    every, refs = beside(refs, count)
    key_ref, prod_ref, gains_ref, out_ref = refs[:4]
    scratch = refs[4:]
    select = key_match(key_ref[:LANES, :], every[GAIN_ROWS + 1 : GAIN_ROWS + 2])
    gains = pick(every[:GAIN_ROWS], select)
    gains_ref[...] = gains
    normal_terms(gains, prod_ref, *scratch, out_ref)


def state_kernel(count, blocks, intervals, *refs):
    every, refs = beside(refs, count)
    key_ref, at_ref, gains_ref, chans_ref, basis_ref = refs[:5]
    z_ref, pen_ref, scale_ref, select_ref, turned_ref = refs[5:]
    place = (iota((KPAD, LANES), 0) == iota((KPAD, LANES), 1) % KPAD).astype(BF16)
    for n, piece in enumerate(split(turn(place, basis_ref[LANES:, :]))):
        turned_ref[n * KPAD : (n + 1) * KPAD, :] = piece
    rows = every[GAIN_ROWS:]
    z_ref[:, :LANES] = gains_ref[...]
    z_ref[:, LANES:] = every[:GAIN_ROWS, :LANES]
    select_ref[...] = key_match(key_ref[...], rows[0:1])
    lanes = rows.shape[1]
    diagonal = iota((BLOCK, lanes), 0) == iota((BLOCK, lanes), 1) % BLOCK
    at = at_ref[...]
    pen = pick(jnp.where(diagonal, rows[2:3], 0.0), key_match(at, rows[3:4]))
    unused = iota(pen.shape, 1) >= LANES + blocks * intervals
    pen_ref[...] = jnp.where(unused, 1.0, pen)
    weights = pick(jnp.where(diagonal, rows[4:5], 0.0), key_match(at, rows[5:6]))
    scale_ref[...] = 1.0 / jnp.maximum(weights * chans_ref[0:1, :], 1.0)


def solve(normal, scale, pen, consensus):
    part = [normal[BLOCK * k : BLOCK * (k + 1)] * scale for k in range(12)]
    rhs = [part[m] + pen * consensus[BLOCK * m : BLOCK * (m + 1)] for m in range(8)]
    h_first = part[8] + pen
    h_second = part[9] + pen
    h_real, h_imag = part[10], part[11]
    determ = h_first * h_second - h_real * h_real - h_imag * h_imag
    over = 1.0 / determ
    d_first, d_second = h_first * over, h_second * over
    d_real, d_imag = h_real * over, h_imag * over
    out = [None] * 8
    for r in range(2):
        x_re, y_re = rhs[2 * r], rhs[2 * r + 1]
        x_im, y_im = rhs[4 + 2 * r], rhs[5 + 2 * r]
        out[2 * r] = x_re * d_second - (y_re * d_real + y_im * d_imag)
        out[4 + 2 * r] = x_im * d_second - (y_im * d_real - y_re * d_imag)
        out[2 * r + 1] = y_re * d_first - (x_re * d_real - x_im * d_imag)
        out[5 + 2 * r] = y_im * d_first - (x_im * d_real + x_re * d_imag)
    return jnp.concatenate(out, 0)


def step_kernel(count, *refs):
    every, refs = beside(refs, count)
    select_ref, z_ref, pen_ref, scale_ref, prod_ref, gains_ref, out_ref = refs[:7]
    scratch = refs[7:]
    normal = pick(every, select_ref[...])
    gains = solve(normal, scale_ref[...], pen_ref[...], z_ref[...])
    gains_ref[...] = gains
    normal_terms(gains[:, :LANES], prod_ref, *scratch, out_ref)


def first_total_kernel(gains_ref, basis_ref, out_ref):
    basis = basis_ref[...]
    total = nn(gains_ref[...], basis, precision=HIGH)
    part = basis[: basis.shape[0] // 8]
    gram = lax.dot_general(
        part, part, (((0,), (0,)), ((), ())), preferred_element_type=F32, precision=HIGH
    )
    out_ref[:GAIN_ROWS, :] = total
    out_ref[GAIN_ROWS:, :] = gram[:KPAD]


def total_kernel(gains_ref, dual_ref, basis_ref, out_ref):
    out_ref[...] = nn(gains_ref[...] + dual_ref[...], basis_ref[...], precision=HIGH)


def inverse_of_three(d):
    def minor(r, c):
        (r0, r1), (c0, c1) = [[k for k in range(3) if k != n] for n in (r, c)]
        value = d[r0][c0] * d[r1][c1] - d[r0][c1] * d[r1][c0]
        return value if (r + c) % 2 == 0 else -value

    minors = [[minor(r, c) for c in range(3)] for r in range(3)]
    over = 1.0 / (d[0][0] * minors[0][0] + d[0][1] * minors[0][1] + d[0][2] * minors[0][2])
    return [[minors[c][r] * over for c in range(3)] for r in range(3)]


def invert(gram):
    row, lane = iota(gram.shape, 0), iota(gram.shape, 1)
    inner = (row < NPOLY) & (lane < NPOLY)
    work = jnp.where(inner, gram + jnp.where(row == lane, ridge, 0.0), 0.0)
    lanes = iota((1, gram.shape[1]), 1)
    for p in range(0, NPOLY, 3):
        rows = [work[p + a : p + a + 1] for a in range(3)]
        block = inverse_of_three(
            [
                [jnp.broadcast_to(rows[a][:, p + b : p + b + 1], lanes.shape) for b in range(3)]
                for a in range(3)
            ]
        )
        columns = [work[:, p + b : p + b + 1] for b in range(3)]
        here = (lane >= p) & (lane < p + 3)
        rows = [jnp.where(here[:1], 0.0, x) for x in rows]
        pivots = []
        for a in range(3):
            pivot = block[a][0] * rows[0] + block[a][1] * rows[1] + block[a][2] * rows[2]
            for b in range(3):
                pivot = jnp.where(lanes == p + b, block[a][b], pivot)
            pivots.append(pivot)
        work = jnp.where(here, 0.0, work)
        for b in range(3):
            work = work - columns[b] * pivots[b]
        for a in range(3):
            work = jnp.where(row == p + a, pivots[a], work)
    return work


def settle(total, inverse, basis_ref, gains, z_ref, dual_ref):
    coeff = nn(total, inverse, precision=HIGH)
    consensus = nt(coeff, basis_ref[...], precision=HIGH)
    z_ref[...] = 2.0 * consensus - gains
    dual_ref[...] = gains - consensus


def band_total(refs):
    totals = [ref[...] for ref in refs]
    while len(totals) > 1:
        totals = [totals[n] + totals[n + 1] for n in range(0, len(totals), 2)]
    return totals[0]


def first_consensus_kernel(
    one_ref, two_ref, gains_ref, basis_ref, z_ref, dual_ref, inverse_ref
):
    total = one_ref[...] + two_ref[...]
    small = invert(total[GAIN_ROWS:])
    row, lane = iota((LANES, LANES), 0), iota((LANES, LANES), 1)
    spread = ((row == lane % KPAD) & (row < KPAD)).astype(F32)
    wide = nn(jnp.concatenate([small] * (LANES // KPAD), 0), spread, precision=HIGH)
    inverse = jnp.where(row // KPAD == lane // KPAD, wide, 0.0)
    inverse_ref[...] = inverse
    settle(total[:GAIN_ROWS], inverse, basis_ref, gains_ref[...], z_ref, dual_ref)


def consensus_kernel(
    one_ref, two_ref, gains_ref, old_ref, basis_ref, inverse_ref, z_ref, dual_ref
):
    total = one_ref[...] + two_ref[...]
    gains = gains_ref[...] + old_ref[...]
    settle(total, inverse_ref[...], basis_ref, gains, z_ref, dual_ref)


def last_kernel(count, blocks, intervals, *refs):
    every, refs = beside(refs, count)
    select_ref, z_ref, pen_ref, scale_ref, dual_ref, turned_ref, gains_ref, out_ref = refs
    own = slice(LANES, 2 * LANES)
    normal = pick(every, select_ref[own, :])
    gains = solve(normal, scale_ref[:, own], pen_ref[:, own], z_ref[:, own])
    gains_ref[...] = gains
    owned = blocks * BLOCK
    here = iota((owned, LANES), 0) // BLOCK == iota((owned, LANES), 1) // intervals
    summed = gains + dual_ref[:, own]
    parts = [summed[m * BLOCK : (m + 1) * BLOCK] for m in range(8)]
    parts = [jnp.where(here, jnp.concatenate([x] * blocks, 0), 0.0) for x in parts]
    high, mid, low = split(jnp.concatenate(parts, 0))
    turned = turned_ref[...]
    first, second = nt(turned, high), nt(turned[: 2 * KPAD], mid)
    small = first[2 * KPAD :] + second[KPAD:] + nt(turned[:KPAD], low)
    total = first[:KPAD] + ((first[KPAD : 2 * KPAD] + second[:KPAD]) + small)
    chunks = total.shape[1] // LANES
    for c in range(chunks):
        lanes = slice(c * LANES, (c + 1) * LANES)
        out_ref[8 * c : 8 * c + 8, :] = total[:8, lanes]
        out_ref[8 * chunks + c : 8 * chunks + c + 1, :] = total[8:9, lanes]
    rest = 9 * chunks
    out_ref[rest:, :] = jnp.zeros((out_ref.shape[0] - rest, LANES), F32)


def gains_kernel(blocks, intervals, gains_ref, out_ref):
    owned = blocks * BLOCK
    place = (iota((intervals, LANES), 0) == iota((intervals, LANES), 1) % intervals).astype(BF16)
    here = iota((owned, LANES), 0) // BLOCK == iota((owned, LANES), 1) // intervals
    for m in range(8):
        part = gains_ref[m * BLOCK : (m + 1) * BLOCK, :]
        out_ref[m] = turn(place, jnp.where(here, jnp.concatenate([part] * blocks, 0), 0.0))


def split(values):
    high = values.astype(BF16)
    rest = values - high.astype(F32)
    mid = rest.astype(BF16)
    return high, mid, (rest - mid.astype(F32)).astype(BF16)


def turn(place, values):
    high, mid, low = split(values)
    return (nt(place, high) + nt(place, mid)) + nt(place, low)


def coefficient_kernel(bands, *refs):
    inverse_ref, out_ref = refs[bands:]
    total = band_total(refs[:bands])
    owned = out_ref.shape[2]
    chunks = 8 * owned // LANES
    inverse = inverse_ref[:KPAD, :KPAD]
    eight = jnp.concatenate([total[8 * c : 8 * c + 8] for c in range(chunks)], 1)
    ninth = jnp.concatenate([total[8 * chunks + c : 8 * chunks + c + 1] for c in range(chunks)], 1)
    coeff = nn(inverse[:, :8], eight, precision=HIGH) + inverse[:, 8:9] * ninth
    for m in range(8):
        out_ref[:, m, :] = coeff[:NPOLY, m * owned : (m + 1) * owned]


def call(kernel, operands, shapes, scratch=(), hbm=False, flops=20_000_000):
    vmem = pl.BlockSpec(memory_space=pltpu.VMEM)
    in_specs = [vmem] * len(operands)
    moved = sum(x.size * x.dtype.itemsize for x in (*operands, *shapes))
    if hbm:
        in_specs = [pl.BlockSpec(memory_space=pltpu.HBM)] * len(operands)
        operands = [pltpu.with_memory_space_constraint(x, pltpu.HBM) for x in operands]
    return pl.pallas_call(
        kernel,
        out_shape=shapes,
        in_specs=in_specs,
        out_specs=[vmem] * len(shapes),
        scratch_shapes=list(scratch),
        compiler_params=pltpu.CompilerParams(vmem_limit_bytes=14 * 1024 * 1024),
        cost_estimate=pl.CostEstimate(flops=flops, bytes_accessed=moved, transcendentals=0),
    )(*operands)


def share_base(x, last=(), ties=(2,), ahead=False):
    devices = lax.axis_size("base")
    mine = [x] + [
        lax.ppermute(x, "base", [(d, d ^ (2 * k)) for d in range(devices)])
        for k in range(1, devices // 2)
    ]
    if ahead:
        mine[3:] = after(mine[3:], (), flops=5_000_000_000)
    if last:
        for k, y in zip(ties, after([mine[k] for k in ties], last)):
            mine[k] = y
    other = [lax.ppermute(y, "base", [(d, d ^ 1) for d in range(devices)]) for y in mine]
    return mine + other


def share_band(x):
    devices = lax.axis_size("band")
    return [x] + [
        lax.ppermute(x, "band", [(d, d ^ k) for d in range(devices)]) for k in range(1, devices)
    ]


def sum_band(x):
    devices = lax.axis_size("band")
    step = 1
    while 2 * step < devices:
        x = x + lax.ppermute(x, "band", [(d, d ^ step) for d in range(devices)])
        step = 2 * step
    return x, lax.ppermute(x, "band", [(d, d ^ step) for d in range(devices)])


def on_device(visibilities, model, start_gains, penalty, pairs, flags, chan_band):
    tiles, channels, cells = visibilities.shape[1:]
    intervals = start_gains.shape[1]
    owned = start_gains.shape[2]
    blocks = owned // BLOCK
    count = lax.axis_size("base")
    bands = lax.axis_size("band")
    width = tiles * channels

    def shape(*extent, dtype=F32):
        return jax.ShapeDtypeStruct(extent, dtype)

    wide = shape(GAIN_ROWS, 2 * LANES)
    narrow = shape(GAIN_ROWS, LANES)
    single = shape(BLOCK, 2 * LANES)
    terms = shape(TERM_ROWS, LANES)
    square = shape(2 * LANES, LANES)

    (greeting,) = call(
        functools.partial(greet_kernel, blocks, intervals),
        (pairs, start_gains, penalty.reshape(1, owned), flags),
        [shape(GAIN_ROWS + 8, LANES)],
        [
            pltpu.SMEM(pairs.shape, jnp.int32),
            pltpu.VMEM(start_gains.shape, F32),
            pltpu.VMEM((1, owned), F32),
            pltpu.VMEM(flags.shape, jnp.int32),
            pltpu.SemaphoreType.DMA((4,)),
        ],
        hbm=True,
    )
    products, keys, at, basis, chans = call(
        functools.partial(prepare_kernel, blocks, intervals, bands),
        (
            pairs,
            chan_band.reshape(1, channels),
            flags,
            visibilities.reshape(8, width, cells),
            model.reshape(8, width, cells),
        ),
        [
            shape(PRODUCTS, BLOCK // 2, BLOCK, 2 * tiles * intervals),
            square,
            square,
            square,
            shape(8, 2 * LANES),
        ],
        [
            pltpu.SMEM(pairs.shape, jnp.int32),
            pltpu.VMEM((1, channels), jnp.int32),
            pltpu.VMEM(flags.shape, jnp.int32),
            *[pltpu.VMEM((8, width, cells), BF16)] * 2,
            pltpu.VMEM((8, cells, width), F32),
            pltpu.SemaphoreType.DMA((5,)),
        ],
        hbm=True,
        flops=2_000_000_000,
    )
    greetings = share_base(greeting, last=(chans,), ties=(1, 2))
    scratch = [
        pltpu.VMEM((12, BLOCK // 2, LANES), F32),
        pltpu.VMEM((2, 12, BLOCK // 2, LANES), F32),
        pltpu.VMEM((12, BLOCK // 2, LANES), F32),
    ]

    gains, message = call(
        functools.partial(first_kernel, count),
        (*greetings, keys, products),
        [narrow, terms],
        scratch,
    )
    z, pen, scale, select, turned = call(
        functools.partial(state_kernel, count, blocks, intervals),
        (*greetings, keys, at, gains, chans, basis),
        [
            wide,
            single,
            single,
            shape(2 * LANES, count * LANES, dtype=BF16),
            shape(3 * KPAD, LANES, dtype=BF16),
        ],
    )
    pieces = share_base(message, last=(scale,), ties=(1, 2))
    gains, message = call(
        functools.partial(step_kernel, count),
        (*pieces, select, z, pen, scale, products),
        [wide, terms],
        scratch,
    )
    (part,) = call(first_total_kernel, (gains, basis), [shape(GAIN_ROWS + KPAD, LANES)])
    z, dual, inverse = call(
        first_consensus_kernel, (*sum_band(part), gains, basis), [wide, wide, narrow]
    )
    pieces = share_base(message, last=(z,), ties=(1, 2), ahead=True)
    gains, message = call(
        functools.partial(step_kernel, count),
        (*pieces, select, z, pen, scale, products),
        [wide, terms],
        scratch,
    )
    (part,) = call(total_kernel, (gains, dual, basis), [narrow])
    z, dual = call(consensus_kernel, (*sum_band(part), gains, dual, basis, inverse), [wide, wide])
    pieces = share_base(message, last=(z,), ties=(1, 2), ahead=True)
    chunks = 8 * owned // LANES
    gains, part = call(
        functools.partial(last_kernel, count, blocks, intervals),
        (*pieces, select, z, pen, scale, dual, turned),
        [narrow, shape(8 * chunks + -(-chunks // 8) * 8, LANES)],
    )
    parts = share_band(part)
    (out,) = call(
        functools.partial(gains_kernel, blocks, intervals),
        (gains,),
        [shape(8, intervals, owned)],
    )
    (coefficients,) = call(
        functools.partial(coefficient_kernel, bands),
        (*parts, inverse),
        [shape(NPOLY, 8, owned)],
    )
    return (out, jnp.transpose(coefficients, (1, 0, 2)))


def solution(mesh):
    in_specs = (
        P(None, "base", "band", None),
        P(None, "base", "band", None),
        P(None, "band", "base"),
        P("base"),
        P("base", None),
        P("base", None),
        P("band"),
    )
    out_specs = (P(None, "band", "base"), P(None, None, "base"))
    return jax.shard_map(
        on_device, mesh=mesh, in_specs=in_specs, out_specs=out_specs, check_vma=False
    )
```

```python
import functools

import jax
import jax.numpy as jnp
from jax import lax
from jax.experimental import pallas as pl
from jax.experimental.pallas import tpu as pltpu
from jax.sharding import PartitionSpec as P

BLOCK = 16
NPOLY = 9
KPAD = 16
ITERS = 3
LANES = 128
F32 = jnp.float32
BF16 = jnp.bfloat16
HIGH = lax.Precision.HIGHEST

ridge = 0.5

GAIN_ROWS = 8 * BLOCK
TERM_ROWS = 12 * BLOCK
PRODUCTS = 48
CROSS = ((0, 1), (0, 2), (0, 3), (1, 2), (1, 3), (2, 3))


def nt(left, right, **kw):
    return lax.dot_general(
        left, right, (((1,), (1,)), ((), ())), preferred_element_type=F32, **kw
    )


def nn(left, right, **kw):
    return lax.dot_general(
        left, right, (((1,), (0,)), ((), ())), preferred_element_type=F32, **kw
    )


def pick(values, select, dot=nt):
    high = values.astype(BF16)
    low = (values - high.astype(F32)).astype(BF16)
    rows = values.shape[0]
    out = dot(jnp.concatenate([high, low], 0), select)
    return out[:rows] + out[rows:]


def iota(shape, axis):
    return lax.broadcasted_iota(jnp.int32, shape, axis)


def add(terms):
    total = None
    for sign, x, y in terms:
        if total is None:
            total = x * y if sign > 0 else -(x * y)
        else:
            total = total + x * y if sign > 0 else total - x * y
    return total


def apply_gains(pairs, gains, turned):
    re, im = [], []
    for r in range(2):
        for c in range(2):
            to_re, to_im = [], []
            for k in range(2):
                for n in range(2):
                    x_re, x_im = pairs(k, r, n, c) if turned else pairs(r, k, c, n)
                    g_re, g_im = gains[2 * k + n], gains[4 + 2 * k + n]
                    sign = -1 if turned else 1
                    to_re += [(1, x_re, g_re), (-sign, x_im, g_im)]
                    to_im += [(1, x_re, g_im), (sign, x_im, g_re)]
            re.append(add(to_re))
            im.append(add(to_im))
    return re + im


def square(gains):
    return [
        add([(1, gains[n], gains[n]) for n in (0, 2, 4, 6)]),
        add([(1, gains[n], gains[n]) for n in (1, 3, 5, 7)]),
        add([(1, gains[n], gains[n + 1]) for n in (0, 2, 4, 6)]),
        add([(1, gains[0], gains[5]), (-1, gains[4], gains[1])])
        + add([(1, gains[2], gains[7]), (-1, gains[6], gains[3])]),
    ]


def outer_first(own, cross, q):
    out = []
    for r in range(2):
        x_re, x_im = cross(r, 0, r, 1)
        twice = add([(1, x_re, q[2]), (-1, x_im, q[3])])
        out.append(add([(1, own[r][0], q[0]), (1, own[r][1], q[1])]) + (twice + twice))
    (a_re, a_im), (b_re, b_im) = cross(0, 0, 1, 0), cross(0, 1, 1, 1)
    (c_re, c_im), (d_re, d_im) = cross(0, 0, 1, 1), cross(0, 1, 1, 0)
    out.append(
        add([(1, a_re, q[0]), (1, b_re, q[1]), (1, c_re + d_re, q[2]), (-1, c_im - d_im, q[3])])
    )
    out.append(
        add([(1, a_im, q[0]), (1, b_im, q[1]), (1, c_im + d_im, q[2]), (1, c_re - d_re, q[3])])
    )
    return out


def outer_second(own, cross, q):
    out = []
    for c in range(2):
        x_re, x_im = cross(0, c, 1, c)
        twice = add([(1, x_re, q[2]), (1, x_im, q[3])])
        out.append(add([(1, own[0][c], q[0]), (1, own[1][c], q[1])]) + (twice + twice))
    (a_re, a_im), (b_re, b_im) = cross(0, 0, 0, 1), cross(1, 0, 1, 1)
    (c_re, c_im), (d_re, d_im) = cross(0, 0, 1, 1), cross(0, 1, 1, 0)
    out.append(
        add([(1, a_re, q[0]), (1, b_re, q[1]), (1, c_re + d_re, q[2]), (1, c_im + d_im, q[3])])
    )
    out.append(
        add([(-1, a_im, q[0]), (-1, b_im, q[1]), (1, c_re - d_re, q[3]), (-1, c_im - d_im, q[2])])
    )
    return out


def slot_key(index, pairs, scale, intervals):
    at = index // intervals
    tiles = len(pairs)
    block = jnp.zeros(index.shape, F32)
    for slot in range(2 * tiles):
        value = pairs[slot % tiles][slot // tiles]
        block = jnp.where(at == slot, value.astype(F32), block)
    if scale > 1:
        block = block * scale + (index % intervals).astype(F32)
    return block


def scalar_pairs(pair_ref):
    return [[pair_ref[t, side] for side in range(2)] for t in range(pair_ref.shape[0])]


def owner_key(index, me, blocks, intervals, none, scale=None):
    at = index // intervals
    key = me * blocks + at
    if scale != 1:
        key = key * intervals + index % intervals
    return jnp.where(at < blocks, key, none).astype(F32)


def cell_weights(pairs, flags):
    cells = flags.shape[1]
    cell = iota((1, cells), 1)
    diagonal = (cell // BLOCK == cell % BLOCK).astype(F32)
    rows = []
    for t, pair in enumerate(pairs):
        same = (pair[0] == pair[1]).astype(F32)
        rows.append(flags[t : t + 1, :] * (1.0 - same * diagonal))
    return rows


def greet_kernel(
    blocks, intervals, pair_hbm, start_hbm, penalty_hbm, flag_hbm, out_ref, pair_ref, start_ref,
    penalty_ref, flag_ref, sems
):
    copies = [
        pltpu.make_async_copy(source, target, sems.at[n])
        for n, (source, target) in enumerate(
            [
                (start_hbm, start_ref),
                (pair_hbm, pair_ref),
                (flag_hbm, flag_ref),
                (penalty_hbm, penalty_ref),
            ]
        )
    ]
    for copy in copies:
        copy.start()
    for copy in copies[1:]:
        copy.wait()
    owned = blocks * BLOCK
    cells = flag_ref.shape[1]
    me = lax.axis_index("base")
    pairs = scalar_pairs(pair_ref)
    tiles = len(pairs)
    weights = cell_weights(pairs, flag_ref[...].astype(F32))
    lane = iota((cells, LANES), 1)
    cell = iota((cells, LANES), 0)
    at, inside = lane // BLOCK, lane % BLOCK
    member = jnp.where(at < tiles, cell // BLOCK, cell % BLOCK) == inside
    station_w = jnp.zeros((8, LANES), F32)
    for t in range(tiles):
        fold = (member & (at % tiles == t) & (at < 2 * tiles)).astype(BF16)
        station_w = station_w + nn(jnp.broadcast_to(weights[t], (8, cells)).astype(BF16), fold)
    lane = iota((8, LANES), 1)
    row = iota((8, LANES), 0)
    wide = intervals // BLOCK
    slot_at = jnp.where(lane // BLOCK < 2 * tiles, slot_key(lane * wide, pairs, 1, intervals), -2.0)
    owner_at = jnp.where(lane // BLOCK < blocks, (me * blocks + lane // BLOCK).astype(F32), -2.0)
    keys = jnp.where(row == 0, slot_key(lane, pairs, intervals, intervals), 0.0)
    keys = jnp.where(row == 1, owner_key(lane, me, blocks, intervals, -2), keys)
    keys = jnp.where(row == 3, owner_at, keys)
    keys = jnp.where(row == 4, station_w, keys)
    out_ref[GAIN_ROWS:, :] = jnp.where(row == 5, slot_at, keys)
    out_ref[GAIN_ROWS + 2 : GAIN_ROWS + 3, :owned] = penalty_ref[...]
    copies[0].wait()
    place = (iota((BLOCK, owned), 0) == iota((BLOCK, owned), 1) % BLOCK).astype(BF16)
    here = iota((LANES, owned), 0) // intervals == iota((LANES, owned), 1) // BLOCK
    parts = []
    for m in range(8):
        plane = jnp.concatenate([start_ref[m]] * (LANES // intervals), 0)
        parts.append(jnp.where(here, plane, 0.0))
    parts = jnp.concatenate(parts, 0)
    high = parts.astype(BF16)
    low = (parts - high.astype(F32)).astype(BF16)
    turned = nt(place, high) + nt(place, low)
    for m in range(8):
        out_ref[m * BLOCK : (m + 1) * BLOCK, :] = turned[:, m * LANES : (m + 1) * LANES]


def prepare_kernel(
    blocks, intervals, bands, pair_hbm, chan_hbm, flag_hbm, vis_hbm, model_hbm, prod_ref, key_ref,
    at_ref, basis_ref, chans_ref, pair_ref, chan_ref, flag_ref, vis_ref, model_ref, mt_ref, sems
):
    planes, width, cells = vis_ref.shape
    moves = [
        (model_hbm, model_ref),
        (vis_hbm, vis_ref),
        (pair_hbm, pair_ref),
        (chan_hbm, chan_ref),
        (flag_hbm, flag_ref),
    ]
    copies = [
        pltpu.make_async_copy(source, target, sems.at[n])
        for n, (source, target) in enumerate(moves)
    ]
    for copy in copies[:1] + copies[2:]:
        copy.start()
    for copy in copies[2:]:
        copy.wait()
    pairs = scalar_pairs(pair_ref)
    tiles = len(pairs)
    channels = width // tiles
    me = lax.axis_index("base")
    row = iota((2 * LANES, LANES), 0)
    lane = iota((2 * LANES, LANES), 1)
    for ref, scale in ((key_ref, intervals), (at_ref, 1)):
        ref[...] = jnp.where(
            row < LANES,
            slot_key(row, pairs, scale, intervals),
            owner_key(row - LANES, me, blocks, intervals, -1, scale),
        )
    band_at = lax.axis_index("band")
    local = chan_ref[...] - band_at * intervals
    chan = (band_at * channels + iota((1, channels), 1)).astype(F32)
    xpos = -1.0 + (2.0 * chan + 1.0) / (channels * bands)
    member = (iota((2 * LANES, channels), 0) % intervals == local).astype(F32)
    chans = jnp.sum(member, 1, keepdims=True)
    chans_ref[...] = nt(jnp.ones((8, channels), BF16), member.astype(BF16))
    centre = jnp.sum(member * xpos, 1, keepdims=True) / chans
    terms = [jnp.ones((2 * LANES, LANES), F32), jnp.broadcast_to(centre, (2 * LANES, LANES))]
    for order in range(2, NPOLY):
        terms.append(2.0 * terms[1] * terms[-1] - terms[-2])
    basis = jnp.zeros((2 * LANES, LANES), F32)
    for order in range(NPOLY):
        basis = jnp.where(lane % KPAD == order, terms[order], basis)
    basis_ref[...] = jnp.where(row // intervals == lane // KPAD, basis, 0.0)
    lanes = 2 * tiles * intervals
    row = iota((lanes, 2 * width), 0)
    lane = iota((lanes, 2 * width), 1)
    at = jnp.concatenate([local] * (2 * tiles), 1)
    fold = ((row // intervals == lane // channels) & (row % intervals == at)).astype(BF16)
    ident = (iota((cells, cells), 0) == iota((cells, cells), 1)).astype(BF16)
    rows = cell_weights(pairs, flag_ref[...].astype(F32))
    weight = jnp.concatenate([jnp.broadcast_to(w, (channels, cells)) for w in rows], 0)
    half = cells // 2

    def put(at, product):
        beside = jnp.concatenate([product[:half], product[half:]], 1)
        prod_ref[at] = pick(beside, fold).reshape(prod_ref.shape[1:])

    copies[0].wait()
    copies[1].start()
    for m in range(planes):
        masked = (model_ref[m].astype(F32) * weight).astype(BF16)
        mt_ref[m] = nt(ident, masked)
    for x in range(4):
        put(32 + x, mt_ref[x] * mt_ref[x] + mt_ref[4 + x] * mt_ref[4 + x])
    for n, (x, y) in enumerate(CROSS):
        x_re, x_im, y_re, y_im = mt_ref[x], mt_ref[4 + x], mt_ref[y], mt_ref[4 + y]
        put(36 + n, x_re * y_re + x_im * y_im)
        put(42 + n, x_im * y_re - x_re * y_im)
    copies[1].wait()
    for x in range(4):
        v_re, v_im = nt(ident, vis_ref[x]), nt(ident, vis_ref[4 + x])
        for y in range(4):
            m_re, m_im = mt_ref[y], mt_ref[4 + y]
            put(4 * x + y, v_re * m_re + v_im * m_im)
            put(16 + 4 * x + y, v_im * m_re - v_re * m_im)


def tie_kernel(*refs):
    pass


def after(values, others, flops=0):
    place = pl.BlockSpec(memory_space=pl.ANY)
    return pl.pallas_call(
        tie_kernel,
        out_shape=[jax.ShapeDtypeStruct(x.shape, x.dtype) for x in values],
        in_specs=[place] * (len(values) + len(others)),
        out_specs=[place] * len(values),
        input_output_aliases={n: n for n in range(len(values))},
        compiler_params=pltpu.CompilerParams(vmem_limit_bytes=1024 * 1024),
        cost_estimate=pl.CostEstimate(flops=flops, bytes_accessed=0, transcendentals=0),
    )(*values, *others)


def normal_terms(gains, prod_ref, first_s, second_s, a_s, out_ref):
    half = BLOCK // 2
    low = iota((half, LANES), 1) < LANES // 2

    def swap(x):
        return pltpu.roll(x, LANES // 2, 1)

    first, second = [], [[], []]
    for m in range(8):
        part = [gains[m * BLOCK + h * half : m * BLOCK + (h + 1) * half] for h in range(2)]
        first.append(jnp.where(low, part[0], swap(part[1])))
        for h in range(2):
            second[h].append(jnp.where(low, swap(part[h]), part[h]))
    for n, x in enumerate(first + square(first)):
        first_s[n] = x
    for h in range(2):
        for n, x in enumerate(second[h] + square(second[h])):
            second_s[h, n] = x

    def step(i, totals):
        partial = None
        new = []
        one = [first_s[n, pl.ds(i, 1), :] for n in range(12)]
        for h in range(2):
            two = [second_s[h, n] for n in range(12)]

            def load(n):
                return prod_ref[n, i, h * half : (h + 1) * half, :]

            def pairs(r, k, c, n):
                at = (2 * r + k) * 4 + 2 * c + n
                return load(at), load(16 + at)

            def cross(r, k, c, n):
                at = CROSS.index((2 * r + k, 2 * c + n))
                return load(36 + at), load(42 + at)

            own = [[load(32 + 2 * r + k) for k in range(2)] for r in range(2)]
            terms = apply_gains(pairs, two[:8], False) + outer_first(own, cross, two[8:])
            partial = terms if partial is None else [x + y for x, y in zip(partial, terms)]
            terms = apply_gains(pairs, one[:8], True) + outer_second(own, cross, one[8:])
            new += [x + y for x, y in zip(totals[12 * h : 12 * (h + 1)], terms)]
        for k in range(12):
            a_s[k, pl.ds(i, 1), :] = jnp.sum(partial[k], 0, keepdims=True)
        return tuple(new)

    zero = jnp.zeros((half, LANES), F32)
    totals = lax.fori_loop(0, half, step, (zero,) * 24, unroll=4)
    for k in range(12):
        mine = a_s[k]
        for h in range(2):
            other = totals[12 * h + k]
            other = other + swap(other)
            at = k * BLOCK + h * half
            out_ref[at : at + half, :] = jnp.where(low, swap(mine) if h else mine, other)


def key_match(rows, lanes):
    count = lanes.shape[1] // LANES
    return (jnp.concatenate([rows] * count, 1) == lanes).astype(BF16)


def beside(refs, count):
    return jnp.concatenate([p[...] for p in refs[:count]], 1), refs[count:]


def first_kernel(count, *refs):
    every, refs = beside(refs, count)
    key_ref, prod_ref, gains_ref, out_ref = refs[:4]
    scratch = refs[4:]
    select = key_match(key_ref[:LANES, :], every[GAIN_ROWS + 1 : GAIN_ROWS + 2])
    gains = pick(every[:GAIN_ROWS], select)
    gains_ref[...] = gains
    normal_terms(gains, prod_ref, *scratch, out_ref)


def state_kernel(count, blocks, intervals, *refs):
    every, refs = beside(refs, count)
    key_ref, at_ref, gains_ref, chans_ref, basis_ref = refs[:5]
    z_ref, pen_ref, scale_ref, select_ref, turned_ref = refs[5:]
    place = (iota((KPAD, LANES), 0) == iota((KPAD, LANES), 1) % KPAD).astype(BF16)
    for n, piece in enumerate(split(turn(place, basis_ref[LANES:, :]))):
        turned_ref[n * KPAD : (n + 1) * KPAD, :] = piece
    rows = every[GAIN_ROWS:]
    z_ref[:, :LANES] = gains_ref[...]
    z_ref[:, LANES:] = every[:GAIN_ROWS, :LANES]
    select_ref[...] = key_match(key_ref[...], rows[0:1])
    lanes = rows.shape[1]
    diagonal = iota((BLOCK, lanes), 0) == iota((BLOCK, lanes), 1) % BLOCK
    at = at_ref[...]
    pen = pick(jnp.where(diagonal, rows[2:3], 0.0), key_match(at, rows[3:4]))
    unused = iota(pen.shape, 1) >= LANES + blocks * intervals
    pen_ref[...] = jnp.where(unused, 1.0, pen)
    weights = pick(jnp.where(diagonal, rows[4:5], 0.0), key_match(at, rows[5:6]))
    scale_ref[...] = 1.0 / jnp.maximum(weights * chans_ref[0:1, :], 1.0)


def solve(normal, scale, pen, consensus):
    part = [normal[BLOCK * k : BLOCK * (k + 1)] * scale for k in range(12)]
    rhs = [part[m] + pen * consensus[BLOCK * m : BLOCK * (m + 1)] for m in range(8)]
    h_first = part[8] + pen
    h_second = part[9] + pen
    h_real, h_imag = part[10], part[11]
    determ = h_first * h_second - h_real * h_real - h_imag * h_imag
    over = 1.0 / determ
    d_first, d_second = h_first * over, h_second * over
    d_real, d_imag = h_real * over, h_imag * over
    out = [None] * 8
    for r in range(2):
        x_re, y_re = rhs[2 * r], rhs[2 * r + 1]
        x_im, y_im = rhs[4 + 2 * r], rhs[5 + 2 * r]
        out[2 * r] = x_re * d_second - (y_re * d_real + y_im * d_imag)
        out[4 + 2 * r] = x_im * d_second - (y_im * d_real - y_re * d_imag)
        out[2 * r + 1] = y_re * d_first - (x_re * d_real - x_im * d_imag)
        out[5 + 2 * r] = y_im * d_first - (x_im * d_real + x_re * d_imag)
    return jnp.concatenate(out, 0)


def step_kernel(count, *refs):
    every, refs = beside(refs, count)
    select_ref, z_ref, pen_ref, scale_ref, prod_ref, gains_ref, out_ref = refs[:7]
    scratch = refs[7:]
    normal = pick(every, select_ref[...])
    gains = solve(normal, scale_ref[...], pen_ref[...], z_ref[...])
    gains_ref[...] = gains
    normal_terms(gains[:, :LANES], prod_ref, *scratch, out_ref)


def first_total_kernel(gains_ref, basis_ref, out_ref):
    basis = basis_ref[...]
    total = nn(gains_ref[...], basis, precision=HIGH)
    part = basis[: basis.shape[0] // 8]
    gram = lax.dot_general(
        part, part, (((0,), (0,)), ((), ())), preferred_element_type=F32, precision=HIGH
    )
    out_ref[:GAIN_ROWS, :] = total
    out_ref[GAIN_ROWS:, :] = gram[:KPAD]


def total_kernel(gains_ref, dual_ref, basis_ref, out_ref):
    out_ref[...] = nn(gains_ref[...] + dual_ref[...], basis_ref[...], precision=HIGH)


def inverse_of_three(d):
    def minor(r, c):
        (r0, r1), (c0, c1) = [[k for k in range(3) if k != n] for n in (r, c)]
        value = d[r0][c0] * d[r1][c1] - d[r0][c1] * d[r1][c0]
        return value if (r + c) % 2 == 0 else -value

    minors = [[minor(r, c) for c in range(3)] for r in range(3)]
    over = 1.0 / (d[0][0] * minors[0][0] + d[0][1] * minors[0][1] + d[0][2] * minors[0][2])
    return [[minors[c][r] * over for c in range(3)] for r in range(3)]


def invert(gram):
    row, lane = iota(gram.shape, 0), iota(gram.shape, 1)
    inner = (row < NPOLY) & (lane < NPOLY)
    work = jnp.where(inner, gram + jnp.where(row == lane, ridge, 0.0), 0.0)
    lanes = iota((1, gram.shape[1]), 1)
    for p in range(0, NPOLY, 3):
        rows = [work[p + a : p + a + 1] for a in range(3)]
        block = inverse_of_three(
            [
                [jnp.broadcast_to(rows[a][:, p + b : p + b + 1], lanes.shape) for b in range(3)]
                for a in range(3)
            ]
        )
        columns = [work[:, p + b : p + b + 1] for b in range(3)]
        here = (lane >= p) & (lane < p + 3)
        rows = [jnp.where(here[:1], 0.0, x) for x in rows]
        pivots = []
        for a in range(3):
            pivot = block[a][0] * rows[0] + block[a][1] * rows[1] + block[a][2] * rows[2]
            for b in range(3):
                pivot = jnp.where(lanes == p + b, block[a][b], pivot)
            pivots.append(pivot)
        work = jnp.where(here, 0.0, work)
        for b in range(3):
            work = work - columns[b] * pivots[b]
        for a in range(3):
            work = jnp.where(row == p + a, pivots[a], work)
    return work


def settle(total, inverse, basis_ref, gains, z_ref, dual_ref):
    coeff = nn(total, inverse, precision=HIGH)
    consensus = nt(coeff, basis_ref[...], precision=HIGH)
    z_ref[...] = 2.0 * consensus - gains
    dual_ref[...] = gains - consensus


def band_total(refs):
    totals = [ref[...] for ref in refs]
    while len(totals) > 1:
        totals = [totals[n] + totals[n + 1] for n in range(0, len(totals), 2)]
    return totals[0]


def first_consensus_kernel(
    one_ref, two_ref, gains_ref, basis_ref, z_ref, dual_ref, inverse_ref
):
    total = one_ref[...] + two_ref[...]
    small = invert(total[GAIN_ROWS:])
    row, lane = iota((LANES, LANES), 0), iota((LANES, LANES), 1)
    spread = ((row == lane % KPAD) & (row < KPAD)).astype(F32)
    wide = nn(jnp.concatenate([small] * (LANES // KPAD), 0), spread, precision=HIGH)
    inverse = jnp.where(row // KPAD == lane // KPAD, wide, 0.0)
    inverse_ref[...] = inverse
    settle(total[:GAIN_ROWS], inverse, basis_ref, gains_ref[...], z_ref, dual_ref)


def consensus_kernel(
    one_ref, two_ref, gains_ref, old_ref, basis_ref, inverse_ref, z_ref, dual_ref
):
    total = one_ref[...] + two_ref[...]
    gains = gains_ref[...] + old_ref[...]
    settle(total, inverse_ref[...], basis_ref, gains, z_ref, dual_ref)


def last_kernel(count, blocks, intervals, *refs):
    every, refs = beside(refs, count)
    select_ref, z_ref, pen_ref, scale_ref, dual_ref, turned_ref, gains_ref, out_ref = refs
    own = slice(LANES, 2 * LANES)
    normal = pick(every, select_ref[own, :])
    gains = solve(normal, scale_ref[:, own], pen_ref[:, own], z_ref[:, own])
    gains_ref[...] = gains
    owned = blocks * BLOCK
    here = iota((owned, LANES), 0) // BLOCK == iota((owned, LANES), 1) // intervals
    summed = gains + dual_ref[:, own]
    parts = [summed[m * BLOCK : (m + 1) * BLOCK] for m in range(8)]
    parts = [jnp.where(here, jnp.concatenate([x] * blocks, 0), 0.0) for x in parts]
    high, mid, low = split(jnp.concatenate(parts, 0))
    turned = turned_ref[...]
    first, second = nt(turned, high), nt(turned[: 2 * KPAD], mid)
    small = first[2 * KPAD :] + second[KPAD:] + nt(turned[:KPAD], low)
    total = first[:KPAD] + ((first[KPAD : 2 * KPAD] + second[:KPAD]) + small)
    chunks = total.shape[1] // LANES
    for c in range(chunks):
        lanes = slice(c * LANES, (c + 1) * LANES)
        out_ref[8 * c : 8 * c + 8, :] = total[:8, lanes]
        out_ref[8 * chunks + c : 8 * chunks + c + 1, :] = total[8:9, lanes]
    rest = 9 * chunks
    out_ref[rest:, :] = jnp.zeros((out_ref.shape[0] - rest, LANES), F32)


def gains_kernel(blocks, intervals, gains_ref, out_ref):
    owned = blocks * BLOCK
    place = (iota((intervals, LANES), 0) == iota((intervals, LANES), 1) % intervals).astype(BF16)
    here = iota((owned, LANES), 0) // BLOCK == iota((owned, LANES), 1) // intervals
    for m in range(8):
        part = gains_ref[m * BLOCK : (m + 1) * BLOCK, :]
        out_ref[m] = turn(place, jnp.where(here, jnp.concatenate([part] * blocks, 0), 0.0))


def split(values):
    high = values.astype(BF16)
    rest = values - high.astype(F32)
    mid = rest.astype(BF16)
    return high, mid, (rest - mid.astype(F32)).astype(BF16)


def turn(place, values):
    high, mid, low = split(values)
    return (nt(place, high) + nt(place, mid)) + nt(place, low)


def coefficient_kernel(bands, *refs):
    inverse_ref, out_ref = refs[bands:]
    total = band_total(refs[:bands])
    owned = out_ref.shape[2]
    chunks = 8 * owned // LANES
    inverse = inverse_ref[:KPAD, :KPAD]
    eight = jnp.concatenate([total[8 * c : 8 * c + 8] for c in range(chunks)], 1)
    ninth = jnp.concatenate([total[8 * chunks + c : 8 * chunks + c + 1] for c in range(chunks)], 1)
    coeff = nn(inverse[:, :8], eight, precision=HIGH) + inverse[:, 8:9] * ninth
    for m in range(8):
        out_ref[:, m, :] = coeff[:NPOLY, m * owned : (m + 1) * owned]


def call(kernel, operands, shapes, scratch=(), hbm=False, flops=20_000_000):
    vmem = pl.BlockSpec(memory_space=pltpu.VMEM)
    in_specs = [vmem] * len(operands)
    moved = sum(x.size * x.dtype.itemsize for x in (*operands, *shapes))
    if hbm:
        in_specs = [pl.BlockSpec(memory_space=pltpu.HBM)] * len(operands)
        operands = [pltpu.with_memory_space_constraint(x, pltpu.HBM) for x in operands]
    return pl.pallas_call(
        kernel,
        out_shape=shapes,
        in_specs=in_specs,
        out_specs=[vmem] * len(shapes),
        scratch_shapes=list(scratch),
        compiler_params=pltpu.CompilerParams(vmem_limit_bytes=14 * 1024 * 1024),
        cost_estimate=pl.CostEstimate(flops=flops, bytes_accessed=moved, transcendentals=0),
    )(*operands)


def share_base(x, last=(), ties=(2,), ahead=False):
    devices = lax.axis_size("base")
    mine = [x] + [
        lax.ppermute(x, "base", [(d, d ^ (2 * k)) for d in range(devices)])
        for k in range(1, devices // 2)
    ]
    if ahead:
        mine[3:] = after(mine[3:], (), flops=5_000_000_000)
    if last:
        for k, y in zip(ties, after([mine[k] for k in ties], last)):
            mine[k] = y
    other = [lax.ppermute(y, "base", [(d, d ^ 1) for d in range(devices)]) for y in mine]
    return mine + other


def share_band(x):
    devices = lax.axis_size("band")
    return [x] + [
        lax.ppermute(x, "band", [(d, d ^ k) for d in range(devices)]) for k in range(1, devices)
    ]


def sum_band(x):
    devices = lax.axis_size("band")
    step = 1
    while 2 * step < devices:
        x = x + lax.ppermute(x, "band", [(d, d ^ step) for d in range(devices)])
        step = 2 * step
    return x, lax.ppermute(x, "band", [(d, d ^ step) for d in range(devices)])


def on_device(visibilities, model, start_gains, penalty, pairs, flags, chan_band):
    tiles, channels, cells = visibilities.shape[1:]
    intervals = start_gains.shape[1]
    owned = start_gains.shape[2]
    blocks = owned // BLOCK
    count = lax.axis_size("base")
    bands = lax.axis_size("band")
    width = tiles * channels

    def shape(*extent, dtype=F32):
        return jax.ShapeDtypeStruct(extent, dtype)

    wide = shape(GAIN_ROWS, 2 * LANES)
    narrow = shape(GAIN_ROWS, LANES)
    single = shape(BLOCK, 2 * LANES)
    terms = shape(TERM_ROWS, LANES)
    square = shape(2 * LANES, LANES)

    (greeting,) = call(
        functools.partial(greet_kernel, blocks, intervals),
        (pairs, start_gains, penalty.reshape(1, owned), flags),
        [shape(GAIN_ROWS + 8, LANES)],
        [
            pltpu.SMEM(pairs.shape, jnp.int32),
            pltpu.VMEM(start_gains.shape, F32),
            pltpu.VMEM((1, owned), F32),
            pltpu.VMEM(flags.shape, jnp.int32),
            pltpu.SemaphoreType.DMA((4,)),
        ],
        hbm=True,
    )
    products, keys, at, basis, chans = call(
        functools.partial(prepare_kernel, blocks, intervals, bands),
        (
            pairs,
            chan_band.reshape(1, channels),
            flags,
            visibilities.reshape(8, width, cells),
            model.reshape(8, width, cells),
        ),
        [
            shape(PRODUCTS, BLOCK // 2, BLOCK, 2 * tiles * intervals),
            square,
            square,
            square,
            shape(8, 2 * LANES),
        ],
        [
            pltpu.SMEM(pairs.shape, jnp.int32),
            pltpu.VMEM((1, channels), jnp.int32),
            pltpu.VMEM(flags.shape, jnp.int32),
            *[pltpu.VMEM((8, width, cells), BF16)] * 2,
            pltpu.VMEM((8, cells, width), F32),
            pltpu.SemaphoreType.DMA((5,)),
        ],
        hbm=True,
        flops=2_000_000_000,
    )
    greetings = share_base(greeting, last=(chans,), ties=(1, 2))
    scratch = [
        pltpu.VMEM((12, BLOCK // 2, LANES), F32),
        pltpu.VMEM((2, 12, BLOCK // 2, LANES), F32),
        pltpu.VMEM((12, BLOCK // 2, LANES), F32),
    ]

    gains, message = call(
        functools.partial(first_kernel, count),
        (*greetings, keys, products),
        [narrow, terms],
        scratch,
    )
    z, pen, scale, select, turned = call(
        functools.partial(state_kernel, count, blocks, intervals),
        (*greetings, keys, at, gains, chans, basis),
        [
            wide,
            single,
            single,
            shape(2 * LANES, count * LANES, dtype=BF16),
            shape(3 * KPAD, LANES, dtype=BF16),
        ],
    )
    pieces = share_base(message, last=(scale,), ties=(1, 2))
    gains, message = call(
        functools.partial(step_kernel, count),
        (*pieces, select, z, pen, scale, products),
        [wide, terms],
        scratch,
    )
    (part,) = call(first_total_kernel, (gains, basis), [shape(GAIN_ROWS + KPAD, LANES)])
    z, dual, inverse = call(
        first_consensus_kernel, (*sum_band(part), gains, basis), [wide, wide, narrow]
    )
    pieces = share_base(message, last=(z,), ties=(2,), ahead=True)
    gains, message = call(
        functools.partial(step_kernel, count),
        (*pieces, select, z, pen, scale, products),
        [wide, terms],
        scratch,
    )
    (part,) = call(total_kernel, (gains, dual, basis), [narrow])
    z, dual = call(consensus_kernel, (*sum_band(part), gains, dual, basis, inverse), [wide, wide])
    pieces = share_base(message, last=(z,), ties=(2,), ahead=True)
    chunks = 8 * owned // LANES
    gains, part = call(
        functools.partial(last_kernel, count, blocks, intervals),
        (*pieces, select, z, pen, scale, dual, turned),
        [narrow, shape(8 * chunks + -(-chunks // 8) * 8, LANES)],
    )
    parts = share_band(part)
    (out,) = call(
        functools.partial(gains_kernel, blocks, intervals),
        (gains,),
        [shape(8, intervals, owned)],
    )
    (coefficients,) = call(
        functools.partial(coefficient_kernel, bands),
        (*parts, inverse),
        [shape(NPOLY, 8, owned)],
    )
    return (out, jnp.transpose(coefficients, (1, 0, 2)))


def solution(mesh):
    in_specs = (
        P(None, "base", "band", None),
        P(None, "base", "band", None),
        P(None, "band", "base"),
        P("base"),
        P("base", None),
        P("base", None),
        P("band"),
    )
    out_specs = (P(None, "band", "base"), P(None, None, "base"))
    return jax.shard_map(
        on_device, mesh=mesh, in_specs=in_specs, out_specs=out_specs, check_vma=False
    )
```

```python
import functools

import jax
import jax.numpy as jnp
from jax import lax
from jax.experimental import pallas as pl
from jax.experimental.pallas import tpu as pltpu
from jax.sharding import PartitionSpec as P

BLOCK = 16
NPOLY = 9
KPAD = 16
ITERS = 3
LANES = 128
F32 = jnp.float32
BF16 = jnp.bfloat16
HIGH = lax.Precision.HIGHEST

ridge = 0.5

GAIN_ROWS = 8 * BLOCK
TERM_ROWS = 12 * BLOCK
PRODUCTS = 48
CROSS = ((0, 1), (0, 2), (0, 3), (1, 2), (1, 3), (2, 3))


def nt(left, right, **kw):
    return lax.dot_general(
        left, right, (((1,), (1,)), ((), ())), preferred_element_type=F32, **kw
    )


def nn(left, right, **kw):
    return lax.dot_general(
        left, right, (((1,), (0,)), ((), ())), preferred_element_type=F32, **kw
    )


def pick(values, select, dot=nt):
    high = values.astype(BF16)
    low = (values - high.astype(F32)).astype(BF16)
    rows = values.shape[0]
    out = dot(jnp.concatenate([high, low], 0), select)
    return out[:rows] + out[rows:]


def iota(shape, axis):
    return lax.broadcasted_iota(jnp.int32, shape, axis)


def add(terms):
    total = None
    for sign, x, y in terms:
        if total is None:
            total = x * y if sign > 0 else -(x * y)
        else:
            total = total + x * y if sign > 0 else total - x * y
    return total


def apply_gains(pairs, gains, turned):
    re, im = [], []
    for r in range(2):
        for c in range(2):
            to_re, to_im = [], []
            for k in range(2):
                for n in range(2):
                    x_re, x_im = pairs(k, r, n, c) if turned else pairs(r, k, c, n)
                    g_re, g_im = gains[2 * k + n], gains[4 + 2 * k + n]
                    sign = -1 if turned else 1
                    to_re += [(1, x_re, g_re), (-sign, x_im, g_im)]
                    to_im += [(1, x_re, g_im), (sign, x_im, g_re)]
            re.append(add(to_re))
            im.append(add(to_im))
    return re + im


def square(gains):
    return [
        add([(1, gains[n], gains[n]) for n in (0, 2, 4, 6)]),
        add([(1, gains[n], gains[n]) for n in (1, 3, 5, 7)]),
        add([(1, gains[n], gains[n + 1]) for n in (0, 2, 4, 6)]),
        add([(1, gains[0], gains[5]), (-1, gains[4], gains[1])])
        + add([(1, gains[2], gains[7]), (-1, gains[6], gains[3])]),
    ]


def outer_first(own, cross, q):
    out = []
    for r in range(2):
        x_re, x_im = cross(r, 0, r, 1)
        twice = add([(1, x_re, q[2]), (-1, x_im, q[3])])
        out.append(add([(1, own[r][0], q[0]), (1, own[r][1], q[1])]) + (twice + twice))
    (a_re, a_im), (b_re, b_im) = cross(0, 0, 1, 0), cross(0, 1, 1, 1)
    (c_re, c_im), (d_re, d_im) = cross(0, 0, 1, 1), cross(0, 1, 1, 0)
    out.append(
        add([(1, a_re, q[0]), (1, b_re, q[1]), (1, c_re + d_re, q[2]), (-1, c_im - d_im, q[3])])
    )
    out.append(
        add([(1, a_im, q[0]), (1, b_im, q[1]), (1, c_im + d_im, q[2]), (1, c_re - d_re, q[3])])
    )
    return out


def outer_second(own, cross, q):
    out = []
    for c in range(2):
        x_re, x_im = cross(0, c, 1, c)
        twice = add([(1, x_re, q[2]), (1, x_im, q[3])])
        out.append(add([(1, own[0][c], q[0]), (1, own[1][c], q[1])]) + (twice + twice))
    (a_re, a_im), (b_re, b_im) = cross(0, 0, 0, 1), cross(1, 0, 1, 1)
    (c_re, c_im), (d_re, d_im) = cross(0, 0, 1, 1), cross(0, 1, 1, 0)
    out.append(
        add([(1, a_re, q[0]), (1, b_re, q[1]), (1, c_re + d_re, q[2]), (1, c_im + d_im, q[3])])
    )
    out.append(
        add([(-1, a_im, q[0]), (-1, b_im, q[1]), (1, c_re - d_re, q[3]), (-1, c_im - d_im, q[2])])
    )
    return out


def slot_key(index, pairs, scale, intervals):
    at = index // intervals
    tiles = len(pairs)
    block = jnp.zeros(index.shape, F32)
    for slot in range(2 * tiles):
        value = pairs[slot % tiles][slot // tiles]
        block = jnp.where(at == slot, value.astype(F32), block)
    if scale > 1:
        block = block * scale + (index % intervals).astype(F32)
    return block


def scalar_pairs(pair_ref):
    return [[pair_ref[t, side] for side in range(2)] for t in range(pair_ref.shape[0])]


def owner_key(index, me, blocks, intervals, none, scale=None):
    at = index // intervals
    key = me * blocks + at
    if scale != 1:
        key = key * intervals + index % intervals
    return jnp.where(at < blocks, key, none).astype(F32)


def cell_weights(pairs, flags):
    cells = flags.shape[1]
    cell = iota((1, cells), 1)
    diagonal = (cell // BLOCK == cell % BLOCK).astype(F32)
    rows = []
    for t, pair in enumerate(pairs):
        same = (pair[0] == pair[1]).astype(F32)
        rows.append(flags[t : t + 1, :] * (1.0 - same * diagonal))
    return rows


def greet_kernel(
    blocks, intervals, pair_hbm, start_hbm, penalty_hbm, flag_hbm, out_ref, pair_ref, start_ref,
    penalty_ref, flag_ref, sems
):
    copies = [
        pltpu.make_async_copy(source, target, sems.at[n])
        for n, (source, target) in enumerate(
            [
                (start_hbm, start_ref),
                (pair_hbm, pair_ref),
                (flag_hbm, flag_ref),
                (penalty_hbm, penalty_ref),
            ]
        )
    ]
    for copy in copies:
        copy.start()
    for copy in copies[1:]:
        copy.wait()
    owned = blocks * BLOCK
    cells = flag_ref.shape[1]
    me = lax.axis_index("base")
    pairs = scalar_pairs(pair_ref)
    tiles = len(pairs)
    weights = cell_weights(pairs, flag_ref[...].astype(F32))
    lane = iota((cells, LANES), 1)
    cell = iota((cells, LANES), 0)
    at, inside = lane // BLOCK, lane % BLOCK
    member = jnp.where(at < tiles, cell // BLOCK, cell % BLOCK) == inside
    station_w = jnp.zeros((8, LANES), F32)
    for t in range(tiles):
        fold = (member & (at % tiles == t) & (at < 2 * tiles)).astype(BF16)
        station_w = station_w + nn(jnp.broadcast_to(weights[t], (8, cells)).astype(BF16), fold)
    lane = iota((8, LANES), 1)
    row = iota((8, LANES), 0)
    wide = intervals // BLOCK
    slot_at = jnp.where(lane // BLOCK < 2 * tiles, slot_key(lane * wide, pairs, 1, intervals), -2.0)
    owner_at = jnp.where(lane // BLOCK < blocks, (me * blocks + lane // BLOCK).astype(F32), -2.0)
    keys = jnp.where(row == 0, slot_key(lane, pairs, intervals, intervals), 0.0)
    keys = jnp.where(row == 1, owner_key(lane, me, blocks, intervals, -2), keys)
    keys = jnp.where(row == 3, owner_at, keys)
    keys = jnp.where(row == 4, station_w, keys)
    out_ref[GAIN_ROWS:, :] = jnp.where(row == 5, slot_at, keys)
    out_ref[GAIN_ROWS + 2 : GAIN_ROWS + 3, :owned] = penalty_ref[...]
    copies[0].wait()
    place = (iota((BLOCK, owned), 0) == iota((BLOCK, owned), 1) % BLOCK).astype(BF16)
    here = iota((LANES, owned), 0) // intervals == iota((LANES, owned), 1) // BLOCK
    parts = []
    for m in range(8):
        plane = jnp.concatenate([start_ref[m]] * (LANES // intervals), 0)
        parts.append(jnp.where(here, plane, 0.0))
    parts = jnp.concatenate(parts, 0)
    high = parts.astype(BF16)
    low = (parts - high.astype(F32)).astype(BF16)
    turned = nt(place, high) + nt(place, low)
    for m in range(8):
        out_ref[m * BLOCK : (m + 1) * BLOCK, :] = turned[:, m * LANES : (m + 1) * LANES]


def prepare_kernel(
    blocks, intervals, bands, pair_hbm, chan_hbm, flag_hbm, vis_hbm, model_hbm, prod_ref, key_ref,
    at_ref, basis_ref, chans_ref, pair_ref, chan_ref, flag_ref, vis_ref, model_ref, mt_ref, sems
):
    planes, width, cells = vis_ref.shape
    moves = [
        (model_hbm, model_ref),
        (vis_hbm, vis_ref),
        (pair_hbm, pair_ref),
        (chan_hbm, chan_ref),
        (flag_hbm, flag_ref),
    ]
    copies = [
        pltpu.make_async_copy(source, target, sems.at[n])
        for n, (source, target) in enumerate(moves)
    ]
    for copy in copies[:1] + copies[2:]:
        copy.start()
    for copy in copies[2:]:
        copy.wait()
    pairs = scalar_pairs(pair_ref)
    tiles = len(pairs)
    channels = width // tiles
    me = lax.axis_index("base")
    row = iota((2 * LANES, LANES), 0)
    lane = iota((2 * LANES, LANES), 1)
    for ref, scale in ((key_ref, intervals), (at_ref, 1)):
        ref[...] = jnp.where(
            row < LANES,
            slot_key(row, pairs, scale, intervals),
            owner_key(row - LANES, me, blocks, intervals, -1, scale),
        )
    band_at = lax.axis_index("band")
    local = chan_ref[...] - band_at * intervals
    chan = (band_at * channels + iota((1, channels), 1)).astype(F32)
    xpos = -1.0 + (2.0 * chan + 1.0) / (channels * bands)
    member = (iota((2 * LANES, channels), 0) % intervals == local).astype(F32)
    chans = jnp.sum(member, 1, keepdims=True)
    chans_ref[...] = nt(jnp.ones((8, channels), BF16), member.astype(BF16))
    centre = jnp.sum(member * xpos, 1, keepdims=True) / chans
    terms = [jnp.ones((2 * LANES, LANES), F32), jnp.broadcast_to(centre, (2 * LANES, LANES))]
    for order in range(2, NPOLY):
        terms.append(2.0 * terms[1] * terms[-1] - terms[-2])
    basis = jnp.zeros((2 * LANES, LANES), F32)
    for order in range(NPOLY):
        basis = jnp.where(lane % KPAD == order, terms[order], basis)
    basis_ref[...] = jnp.where(row // intervals == lane // KPAD, basis, 0.0)
    lanes = 2 * tiles * intervals
    row = iota((lanes, 2 * width), 0)
    lane = iota((lanes, 2 * width), 1)
    at = jnp.concatenate([local] * (2 * tiles), 1)
    fold = ((row // intervals == lane // channels) & (row % intervals == at)).astype(BF16)
    ident = (iota((cells, cells), 0) == iota((cells, cells), 1)).astype(BF16)
    rows = cell_weights(pairs, flag_ref[...].astype(F32))
    weight = jnp.concatenate([jnp.broadcast_to(w, (channels, cells)) for w in rows], 0)
    half = cells // 2

    def put(at, product):
        beside = jnp.concatenate([product[:half], product[half:]], 1)
        prod_ref[at] = pick(beside, fold).reshape(prod_ref.shape[1:])

    copies[0].wait()
    copies[1].start()
    for m in range(planes):
        masked = (model_ref[m].astype(F32) * weight).astype(BF16)
        mt_ref[m] = nt(ident, masked)
    for x in range(4):
        put(32 + x, mt_ref[x] * mt_ref[x] + mt_ref[4 + x] * mt_ref[4 + x])
    for n, (x, y) in enumerate(CROSS):
        x_re, x_im, y_re, y_im = mt_ref[x], mt_ref[4 + x], mt_ref[y], mt_ref[4 + y]
        put(36 + n, x_re * y_re + x_im * y_im)
        put(42 + n, x_im * y_re - x_re * y_im)
    copies[1].wait()
    for x in range(4):
        v_re, v_im = nt(ident, vis_ref[x]), nt(ident, vis_ref[4 + x])
        for y in range(4):
            m_re, m_im = mt_ref[y], mt_ref[4 + y]
            put(4 * x + y, v_re * m_re + v_im * m_im)
            put(16 + 4 * x + y, v_im * m_re - v_re * m_im)


def tie_kernel(*refs):
    pass


def after(values, others, flops=0):
    place = pl.BlockSpec(memory_space=pl.ANY)
    return pl.pallas_call(
        tie_kernel,
        out_shape=[jax.ShapeDtypeStruct(x.shape, x.dtype) for x in values],
        in_specs=[place] * (len(values) + len(others)),
        out_specs=[place] * len(values),
        input_output_aliases={n: n for n in range(len(values))},
        compiler_params=pltpu.CompilerParams(vmem_limit_bytes=1024 * 1024),
        cost_estimate=pl.CostEstimate(flops=flops, bytes_accessed=0, transcendentals=0),
    )(*values, *others)


def normal_terms(gains, prod_ref, first_s, second_s, a_s, out_ref):
    half = BLOCK // 2
    low = iota((half, LANES), 1) < LANES // 2

    def swap(x):
        return pltpu.roll(x, LANES // 2, 1)

    first, second = [], [[], []]
    for m in range(8):
        part = [gains[m * BLOCK + h * half : m * BLOCK + (h + 1) * half] for h in range(2)]
        first.append(jnp.where(low, part[0], swap(part[1])))
        for h in range(2):
            second[h].append(jnp.where(low, swap(part[h]), part[h]))
    for n, x in enumerate(first + square(first)):
        first_s[n] = x
    for h in range(2):
        for n, x in enumerate(second[h] + square(second[h])):
            second_s[h, n] = x

    def step(i, totals):
        partial = None
        new = []
        one = [first_s[n, pl.ds(i, 1), :] for n in range(12)]
        for h in range(2):
            two = [second_s[h, n] for n in range(12)]

            def load(n):
                return prod_ref[n, i, h * half : (h + 1) * half, :]

            def pairs(r, k, c, n):
                at = (2 * r + k) * 4 + 2 * c + n
                return load(at), load(16 + at)

            def cross(r, k, c, n):
                at = CROSS.index((2 * r + k, 2 * c + n))
                return load(36 + at), load(42 + at)

            own = [[load(32 + 2 * r + k) for k in range(2)] for r in range(2)]
            terms = apply_gains(pairs, two[:8], False) + outer_first(own, cross, two[8:])
            partial = terms if partial is None else [x + y for x, y in zip(partial, terms)]
            terms = apply_gains(pairs, one[:8], True) + outer_second(own, cross, one[8:])
            new += [x + y for x, y in zip(totals[12 * h : 12 * (h + 1)], terms)]
        for k in range(12):
            a_s[k, pl.ds(i, 1), :] = jnp.sum(partial[k], 0, keepdims=True)
        return tuple(new)

    zero = jnp.zeros((half, LANES), F32)
    totals = lax.fori_loop(0, half, step, (zero,) * 24, unroll=4)
    for k in range(12):
        mine = a_s[k]
        for h in range(2):
            other = totals[12 * h + k]
            other = other + swap(other)
            at = k * BLOCK + h * half
            out_ref[at : at + half, :] = jnp.where(low, swap(mine) if h else mine, other)


def key_match(rows, lanes):
    count = lanes.shape[1] // LANES
    return (jnp.concatenate([rows] * count, 1) == lanes).astype(BF16)


def beside(refs, count):
    return jnp.concatenate([p[...] for p in refs[:count]], 1), refs[count:]


def first_kernel(count, *refs):
    every, refs = beside(refs, count)
    key_ref, prod_ref, gains_ref, out_ref = refs[:4]
    scratch = refs[4:]
    select = key_match(key_ref[:LANES, :], every[GAIN_ROWS + 1 : GAIN_ROWS + 2])
    gains = pick(every[:GAIN_ROWS], select)
    gains_ref[...] = gains
    normal_terms(gains, prod_ref, *scratch, out_ref)


def state_kernel(count, blocks, intervals, *refs):
    every, refs = beside(refs, count)
    key_ref, at_ref, gains_ref, chans_ref, basis_ref = refs[:5]
    z_ref, pen_ref, scale_ref, select_ref, turned_ref = refs[5:]
    place = (iota((KPAD, LANES), 0) == iota((KPAD, LANES), 1) % KPAD).astype(BF16)
    for n, piece in enumerate(split(turn(place, basis_ref[LANES:, :]))):
        turned_ref[n * KPAD : (n + 1) * KPAD, :] = piece
    rows = every[GAIN_ROWS:]
    z_ref[:, :LANES] = gains_ref[...]
    z_ref[:, LANES:] = every[:GAIN_ROWS, :LANES]
    select_ref[...] = key_match(key_ref[...], rows[0:1])
    lanes = rows.shape[1]
    diagonal = iota((BLOCK, lanes), 0) == iota((BLOCK, lanes), 1) % BLOCK
    at = at_ref[...]
    pen = pick(jnp.where(diagonal, rows[2:3], 0.0), key_match(at, rows[3:4]))
    unused = iota(pen.shape, 1) >= LANES + blocks * intervals
    pen_ref[...] = jnp.where(unused, 1.0, pen)
    weights = pick(jnp.where(diagonal, rows[4:5], 0.0), key_match(at, rows[5:6]))
    scale_ref[...] = 1.0 / jnp.maximum(weights * chans_ref[0:1, :], 1.0)


def solve(normal, scale, pen, consensus):
    part = [normal[BLOCK * k : BLOCK * (k + 1)] * scale for k in range(12)]
    rhs = [part[m] + pen * consensus[BLOCK * m : BLOCK * (m + 1)] for m in range(8)]
    h_first = part[8] + pen
    h_second = part[9] + pen
    h_real, h_imag = part[10], part[11]
    determ = h_first * h_second - h_real * h_real - h_imag * h_imag
    over = 1.0 / determ
    d_first, d_second = h_first * over, h_second * over
    d_real, d_imag = h_real * over, h_imag * over
    out = [None] * 8
    for r in range(2):
        x_re, y_re = rhs[2 * r], rhs[2 * r + 1]
        x_im, y_im = rhs[4 + 2 * r], rhs[5 + 2 * r]
        out[2 * r] = x_re * d_second - (y_re * d_real + y_im * d_imag)
        out[4 + 2 * r] = x_im * d_second - (y_im * d_real - y_re * d_imag)
        out[2 * r + 1] = y_re * d_first - (x_re * d_real - x_im * d_imag)
        out[5 + 2 * r] = y_im * d_first - (x_im * d_real + x_re * d_imag)
    return jnp.concatenate(out, 0)


def step_kernel(count, *refs):
    every, refs = beside(refs, count)
    select_ref, z_ref, pen_ref, scale_ref, prod_ref, gains_ref, out_ref = refs[:7]
    scratch = refs[7:]
    normal = pick(every, select_ref[...])
    gains = solve(normal, scale_ref[...], pen_ref[...], z_ref[...])
    gains_ref[...] = gains
    normal_terms(gains[:, :LANES], prod_ref, *scratch, out_ref)


def first_total_kernel(gains_ref, basis_ref, out_ref):
    basis = basis_ref[...]
    total = nn(gains_ref[...], basis, precision=HIGH)
    part = basis[: basis.shape[0] // 8]
    gram = lax.dot_general(
        part, part, (((0,), (0,)), ((), ())), preferred_element_type=F32, precision=HIGH
    )
    out_ref[:GAIN_ROWS, :] = total
    out_ref[GAIN_ROWS:, :] = gram[:KPAD]


def total_kernel(gains_ref, dual_ref, basis_ref, out_ref):
    out_ref[...] = nn(gains_ref[...] + dual_ref[...], basis_ref[...], precision=HIGH)


def inverse_of_three(d):
    def minor(r, c):
        (r0, r1), (c0, c1) = [[k for k in range(3) if k != n] for n in (r, c)]
        value = d[r0][c0] * d[r1][c1] - d[r0][c1] * d[r1][c0]
        return value if (r + c) % 2 == 0 else -value

    minors = [[minor(r, c) for c in range(3)] for r in range(3)]
    over = 1.0 / (d[0][0] * minors[0][0] + d[0][1] * minors[0][1] + d[0][2] * minors[0][2])
    return [[minors[c][r] * over for c in range(3)] for r in range(3)]


def invert(gram):
    row, lane = iota(gram.shape, 0), iota(gram.shape, 1)
    inner = (row < NPOLY) & (lane < NPOLY)
    work = jnp.where(inner, gram + jnp.where(row == lane, ridge, 0.0), 0.0)
    lanes = iota((1, gram.shape[1]), 1)
    for p in range(0, NPOLY, 3):
        rows = [work[p + a : p + a + 1] for a in range(3)]
        block = inverse_of_three(
            [
                [jnp.broadcast_to(rows[a][:, p + b : p + b + 1], lanes.shape) for b in range(3)]
                for a in range(3)
            ]
        )
        columns = [work[:, p + b : p + b + 1] for b in range(3)]
        here = (lane >= p) & (lane < p + 3)
        rows = [jnp.where(here[:1], 0.0, x) for x in rows]
        pivots = []
        for a in range(3):
            pivot = block[a][0] * rows[0] + block[a][1] * rows[1] + block[a][2] * rows[2]
            for b in range(3):
                pivot = jnp.where(lanes == p + b, block[a][b], pivot)
            pivots.append(pivot)
        work = jnp.where(here, 0.0, work)
        for b in range(3):
            work = work - columns[b] * pivots[b]
        for a in range(3):
            work = jnp.where(row == p + a, pivots[a], work)
    return work


def settle(total, inverse, basis_ref, gains, z_ref, dual_ref):
    coeff = nn(total, inverse, precision=HIGH)
    consensus = nt(coeff, basis_ref[...], precision=HIGH)
    z_ref[...] = 2.0 * consensus - gains
    dual_ref[...] = gains - consensus


def band_total(refs):
    totals = [ref[...] for ref in refs]
    while len(totals) > 1:
        totals = [totals[n] + totals[n + 1] for n in range(0, len(totals), 2)]
    return totals[0]


def first_consensus_kernel(
    one_ref, two_ref, gains_ref, basis_ref, z_ref, dual_ref, inverse_ref
):
    total = one_ref[...] + two_ref[...]
    small = invert(total[GAIN_ROWS:])
    row, lane = iota((LANES, LANES), 0), iota((LANES, LANES), 1)
    spread = ((row == lane % KPAD) & (row < KPAD)).astype(F32)
    wide = nn(jnp.concatenate([small] * (LANES // KPAD), 0), spread, precision=HIGH)
    inverse = jnp.where(row // KPAD == lane // KPAD, wide, 0.0)
    inverse_ref[...] = inverse
    settle(total[:GAIN_ROWS], inverse, basis_ref, gains_ref[...], z_ref, dual_ref)


def consensus_kernel(
    one_ref, two_ref, gains_ref, old_ref, basis_ref, inverse_ref, z_ref, dual_ref
):
    total = one_ref[...] + two_ref[...]
    gains = gains_ref[...] + old_ref[...]
    settle(total, inverse_ref[...], basis_ref, gains, z_ref, dual_ref)


def last_kernel(count, blocks, intervals, *refs):
    every, refs = beside(refs, count)
    select_ref, z_ref, pen_ref, scale_ref, dual_ref, turned_ref, gains_ref, out_ref = refs
    own = slice(LANES, 2 * LANES)
    normal = pick(every, select_ref[own, :])
    gains = solve(normal, scale_ref[:, own], pen_ref[:, own], z_ref[:, own])
    gains_ref[...] = gains
    owned = blocks * BLOCK
    here = iota((owned, LANES), 0) // BLOCK == iota((owned, LANES), 1) // intervals
    summed = gains + dual_ref[:, own]
    parts = [summed[m * BLOCK : (m + 1) * BLOCK] for m in range(8)]
    parts = [jnp.where(here, jnp.concatenate([x] * blocks, 0), 0.0) for x in parts]
    high, mid, low = split(jnp.concatenate(parts, 0))
    turned = turned_ref[...]
    first, second = nt(turned, high), nt(turned[: 2 * KPAD], mid)
    small = first[2 * KPAD :] + second[KPAD:] + nt(turned[:KPAD], low)
    total = first[:KPAD] + ((first[KPAD : 2 * KPAD] + second[:KPAD]) + small)
    chunks = total.shape[1] // LANES
    for c in range(chunks):
        lanes = slice(c * LANES, (c + 1) * LANES)
        out_ref[8 * c : 8 * c + 8, :] = total[:8, lanes]
        out_ref[8 * chunks + c : 8 * chunks + c + 1, :] = total[8:9, lanes]
    rest = 9 * chunks
    out_ref[rest:, :] = jnp.zeros((out_ref.shape[0] - rest, LANES), F32)


def gains_kernel(blocks, intervals, gains_ref, out_ref):
    owned = blocks * BLOCK
    place = (iota((intervals, LANES), 0) == iota((intervals, LANES), 1) % intervals).astype(BF16)
    here = iota((owned, LANES), 0) // BLOCK == iota((owned, LANES), 1) // intervals
    for m in range(8):
        part = gains_ref[m * BLOCK : (m + 1) * BLOCK, :]
        out_ref[m] = turn(place, jnp.where(here, jnp.concatenate([part] * blocks, 0), 0.0))


def split(values):
    high = values.astype(BF16)
    rest = values - high.astype(F32)
    mid = rest.astype(BF16)
    return high, mid, (rest - mid.astype(F32)).astype(BF16)


def turn(place, values):
    high, mid, low = split(values)
    return (nt(place, high) + nt(place, mid)) + nt(place, low)


def coefficient_kernel(bands, *refs):
    inverse_ref, out_ref = refs[bands:]
    total = band_total(refs[:bands])
    owned = out_ref.shape[2]
    chunks = 8 * owned // LANES
    inverse = inverse_ref[:KPAD, :KPAD]
    eight = jnp.concatenate([total[8 * c : 8 * c + 8] for c in range(chunks)], 1)
    ninth = jnp.concatenate([total[8 * chunks + c : 8 * chunks + c + 1] for c in range(chunks)], 1)
    coeff = nn(inverse[:, :8], eight, precision=HIGH) + inverse[:, 8:9] * ninth
    for m in range(8):
        out_ref[:, m, :] = coeff[:NPOLY, m * owned : (m + 1) * owned]


def call(kernel, operands, shapes, scratch=(), hbm=False, flops=20_000_000):
    vmem = pl.BlockSpec(memory_space=pltpu.VMEM)
    in_specs = [vmem] * len(operands)
    moved = sum(x.size * x.dtype.itemsize for x in (*operands, *shapes))
    if hbm:
        in_specs = [pl.BlockSpec(memory_space=pltpu.HBM)] * len(operands)
        operands = [pltpu.with_memory_space_constraint(x, pltpu.HBM) for x in operands]
    return pl.pallas_call(
        kernel,
        out_shape=shapes,
        in_specs=in_specs,
        out_specs=[vmem] * len(shapes),
        scratch_shapes=list(scratch),
        compiler_params=pltpu.CompilerParams(vmem_limit_bytes=14 * 1024 * 1024),
        cost_estimate=pl.CostEstimate(flops=flops, bytes_accessed=moved, transcendentals=0),
    )(*operands)


def share_base(x, last=(), ties=(2,), ahead=False):
    devices = lax.axis_size("base")
    mine = [x] + [
        lax.ppermute(x, "base", [(d, d ^ (2 * k)) for d in range(devices)])
        for k in range(1, devices // 2)
    ]
    if ahead:
        mine[3:] = after(mine[3:], (), flops=5_000_000_000)
    if last:
        for k, y in zip(ties, after([mine[k] for k in ties], last)):
            mine[k] = y
    other = [lax.ppermute(y, "base", [(d, d ^ 1) for d in range(devices)]) for y in mine]
    return mine + other


def share_band(x):
    devices = lax.axis_size("band")
    return [x] + [
        lax.ppermute(x, "band", [(d, d ^ k) for d in range(devices)]) for k in range(1, devices)
    ]


def sum_band(x):
    devices = lax.axis_size("band")
    step = 1
    while 2 * step < devices:
        x = x + lax.ppermute(x, "band", [(d, d ^ step) for d in range(devices)])
        step = 2 * step
    return x, lax.ppermute(x, "band", [(d, d ^ step) for d in range(devices)])


def on_device(visibilities, model, start_gains, penalty, pairs, flags, chan_band):
    tiles, channels, cells = visibilities.shape[1:]
    intervals = start_gains.shape[1]
    owned = start_gains.shape[2]
    blocks = owned // BLOCK
    count = lax.axis_size("base")
    bands = lax.axis_size("band")
    width = tiles * channels

    def shape(*extent, dtype=F32):
        return jax.ShapeDtypeStruct(extent, dtype)

    wide = shape(GAIN_ROWS, 2 * LANES)
    narrow = shape(GAIN_ROWS, LANES)
    single = shape(BLOCK, 2 * LANES)
    terms = shape(TERM_ROWS, LANES)
    square = shape(2 * LANES, LANES)

    (greeting,) = call(
        functools.partial(greet_kernel, blocks, intervals),
        (pairs, start_gains, penalty.reshape(1, owned), flags),
        [shape(GAIN_ROWS + 8, LANES)],
        [
            pltpu.SMEM(pairs.shape, jnp.int32),
            pltpu.VMEM(start_gains.shape, F32),
            pltpu.VMEM((1, owned), F32),
            pltpu.VMEM(flags.shape, jnp.int32),
            pltpu.SemaphoreType.DMA((4,)),
        ],
        hbm=True,
    )
    products, keys, at, basis, chans = call(
        functools.partial(prepare_kernel, blocks, intervals, bands),
        (
            pairs,
            chan_band.reshape(1, channels),
            flags,
            visibilities.reshape(8, width, cells),
            model.reshape(8, width, cells),
        ),
        [
            shape(PRODUCTS, BLOCK // 2, BLOCK, 2 * tiles * intervals),
            square,
            square,
            square,
            shape(8, 2 * LANES),
        ],
        [
            pltpu.SMEM(pairs.shape, jnp.int32),
            pltpu.VMEM((1, channels), jnp.int32),
            pltpu.VMEM(flags.shape, jnp.int32),
            *[pltpu.VMEM((8, width, cells), BF16)] * 2,
            pltpu.VMEM((8, cells, width), F32),
            pltpu.SemaphoreType.DMA((5,)),
        ],
        hbm=True,
        flops=2_000_000_000,
    )
    greetings = share_base(greeting, last=(chans,))
    scratch = [
        pltpu.VMEM((12, BLOCK // 2, LANES), F32),
        pltpu.VMEM((2, 12, BLOCK // 2, LANES), F32),
        pltpu.VMEM((12, BLOCK // 2, LANES), F32),
    ]

    gains, message = call(
        functools.partial(first_kernel, count),
        (*greetings, keys, products),
        [narrow, terms],
        scratch,
    )
    z, pen, scale, select, turned = call(
        functools.partial(state_kernel, count, blocks, intervals),
        (*greetings, keys, at, gains, chans, basis),
        [
            wide,
            single,
            single,
            shape(2 * LANES, count * LANES, dtype=BF16),
            shape(3 * KPAD, LANES, dtype=BF16),
        ],
    )
    pieces = share_base(message, last=(scale,), ties=(1, 2))
    gains, message = call(
        functools.partial(step_kernel, count),
        (*pieces, select, z, pen, scale, products),
        [wide, terms],
        scratch,
    )
    (part,) = call(first_total_kernel, (gains, basis), [shape(GAIN_ROWS + KPAD, LANES)])
    z, dual, inverse = call(
        first_consensus_kernel, (*sum_band(part), gains, basis), [wide, wide, narrow]
    )
    pieces = share_base(message, last=(z,), ties=(2,), ahead=True)
    gains, message = call(
        functools.partial(step_kernel, count),
        (*pieces, select, z, pen, scale, products),
        [wide, terms],
        scratch,
    )
    (part,) = call(total_kernel, (gains, dual, basis), [narrow])
    z, dual = call(consensus_kernel, (*sum_band(part), gains, dual, basis, inverse), [wide, wide])
    pieces = share_base(message, last=(z,), ties=(2,), ahead=True)
    chunks = 8 * owned // LANES
    gains, part = call(
        functools.partial(last_kernel, count, blocks, intervals),
        (*pieces, select, z, pen, scale, dual, turned),
        [narrow, shape(8 * chunks + -(-chunks // 8) * 8, LANES)],
    )
    parts = share_band(part)
    (out,) = call(
        functools.partial(gains_kernel, blocks, intervals),
        (gains,),
        [shape(8, intervals, owned)],
    )
    (coefficients,) = call(
        functools.partial(coefficient_kernel, bands),
        (*parts, inverse),
        [shape(NPOLY, 8, owned)],
    )
    return (out, jnp.transpose(coefficients, (1, 0, 2)))


def solution(mesh):
    in_specs = (
        P(None, "base", "band", None),
        P(None, "base", "band", None),
        P(None, "band", "base"),
        P("base"),
        P("base", None),
        P("base", None),
        P("band"),
    )
    out_specs = (P(None, "band", "base"), P(None, None, "base"))
    return jax.shard_map(
        on_device, mesh=mesh, in_specs=in_specs, out_specs=out_specs, check_vma=False
    )
```

```python
import functools

import jax
import jax.numpy as jnp
from jax import lax
from jax.experimental import pallas as pl
from jax.experimental.pallas import tpu as pltpu
from jax.sharding import PartitionSpec as P

BLOCK = 16
NPOLY = 9
KPAD = 16
ITERS = 3
LANES = 128
F32 = jnp.float32
BF16 = jnp.bfloat16
HIGH = lax.Precision.HIGHEST

ridge = 0.5

GAIN_ROWS = 8 * BLOCK
TERM_ROWS = 12 * BLOCK
PRODUCTS = 48
CROSS = ((0, 1), (0, 2), (0, 3), (1, 2), (1, 3), (2, 3))


def nt(left, right, **kw):
    return lax.dot_general(
        left, right, (((1,), (1,)), ((), ())), preferred_element_type=F32, **kw
    )


def nn(left, right, **kw):
    return lax.dot_general(
        left, right, (((1,), (0,)), ((), ())), preferred_element_type=F32, **kw
    )


def pick(values, select, dot=nt):
    high = values.astype(BF16)
    low = (values - high.astype(F32)).astype(BF16)
    rows = values.shape[0]
    out = dot(jnp.concatenate([high, low], 0), select)
    return out[:rows] + out[rows:]


def iota(shape, axis):
    return lax.broadcasted_iota(jnp.int32, shape, axis)


def add(terms):
    total = None
    for sign, x, y in terms:
        if total is None:
            total = x * y if sign > 0 else -(x * y)
        else:
            total = total + x * y if sign > 0 else total - x * y
    return total


def apply_gains(pairs, gains, turned):
    re, im = [], []
    for r in range(2):
        for c in range(2):
            to_re, to_im = [], []
            for k in range(2):
                for n in range(2):
                    x_re, x_im = pairs(k, r, n, c) if turned else pairs(r, k, c, n)
                    g_re, g_im = gains[2 * k + n], gains[4 + 2 * k + n]
                    sign = -1 if turned else 1
                    to_re += [(1, x_re, g_re), (-sign, x_im, g_im)]
                    to_im += [(1, x_re, g_im), (sign, x_im, g_re)]
            re.append(add(to_re))
            im.append(add(to_im))
    return re + im


def square(gains):
    return [
        add([(1, gains[n], gains[n]) for n in (0, 2, 4, 6)]),
        add([(1, gains[n], gains[n]) for n in (1, 3, 5, 7)]),
        add([(1, gains[n], gains[n + 1]) for n in (0, 2, 4, 6)]),
        add([(1, gains[0], gains[5]), (-1, gains[4], gains[1])])
        + add([(1, gains[2], gains[7]), (-1, gains[6], gains[3])]),
    ]


def outer_first(own, cross, q):
    out = []
    for r in range(2):
        x_re, x_im = cross(r, 0, r, 1)
        twice = add([(1, x_re, q[2]), (-1, x_im, q[3])])
        out.append(add([(1, own[r][0], q[0]), (1, own[r][1], q[1])]) + (twice + twice))
    (a_re, a_im), (b_re, b_im) = cross(0, 0, 1, 0), cross(0, 1, 1, 1)
    (c_re, c_im), (d_re, d_im) = cross(0, 0, 1, 1), cross(0, 1, 1, 0)
    out.append(
        add([(1, a_re, q[0]), (1, b_re, q[1]), (1, c_re + d_re, q[2]), (-1, c_im - d_im, q[3])])
    )
    out.append(
        add([(1, a_im, q[0]), (1, b_im, q[1]), (1, c_im + d_im, q[2]), (1, c_re - d_re, q[3])])
    )
    return out


def outer_second(own, cross, q):
    out = []
    for c in range(2):
        x_re, x_im = cross(0, c, 1, c)
        twice = add([(1, x_re, q[2]), (1, x_im, q[3])])
        out.append(add([(1, own[0][c], q[0]), (1, own[1][c], q[1])]) + (twice + twice))
    (a_re, a_im), (b_re, b_im) = cross(0, 0, 0, 1), cross(1, 0, 1, 1)
    (c_re, c_im), (d_re, d_im) = cross(0, 0, 1, 1), cross(0, 1, 1, 0)
    out.append(
        add([(1, a_re, q[0]), (1, b_re, q[1]), (1, c_re + d_re, q[2]), (1, c_im + d_im, q[3])])
    )
    out.append(
        add([(-1, a_im, q[0]), (-1, b_im, q[1]), (1, c_re - d_re, q[3]), (-1, c_im - d_im, q[2])])
    )
    return out


def slot_key(index, pairs, scale, intervals):
    at = index // intervals
    tiles = len(pairs)
    block = jnp.zeros(index.shape, F32)
    for slot in range(2 * tiles):
        value = pairs[slot % tiles][slot // tiles]
        block = jnp.where(at == slot, value.astype(F32), block)
    if scale > 1:
        block = block * scale + (index % intervals).astype(F32)
    return block


def scalar_pairs(pair_ref):
    return [[pair_ref[t, side] for side in range(2)] for t in range(pair_ref.shape[0])]


def owner_key(index, me, blocks, intervals, none, scale=None):
    at = index // intervals
    key = me * blocks + at
    if scale != 1:
        key = key * intervals + index % intervals
    return jnp.where(at < blocks, key, none).astype(F32)


def cell_weights(pairs, flags):
    cells = flags.shape[1]
    cell = iota((1, cells), 1)
    diagonal = (cell // BLOCK == cell % BLOCK).astype(F32)
    rows = []
    for t, pair in enumerate(pairs):
        same = (pair[0] == pair[1]).astype(F32)
        rows.append(flags[t : t + 1, :] * (1.0 - same * diagonal))
    return rows


def greet_kernel(
    blocks, intervals, pair_hbm, start_hbm, penalty_hbm, flag_hbm, out_ref, pair_ref, start_ref,
    penalty_ref, flag_ref, sems
):
    copies = [
        pltpu.make_async_copy(source, target, sems.at[n])
        for n, (source, target) in enumerate(
            [
                (start_hbm, start_ref),
                (pair_hbm, pair_ref),
                (flag_hbm, flag_ref),
                (penalty_hbm, penalty_ref),
            ]
        )
    ]
    for copy in copies:
        copy.start()
    for copy in copies[1:]:
        copy.wait()
    owned = blocks * BLOCK
    cells = flag_ref.shape[1]
    me = lax.axis_index("base")
    pairs = scalar_pairs(pair_ref)
    tiles = len(pairs)
    weights = cell_weights(pairs, flag_ref[...].astype(F32))
    lane = iota((cells, LANES), 1)
    cell = iota((cells, LANES), 0)
    at, inside = lane // BLOCK, lane % BLOCK
    member = jnp.where(at < tiles, cell // BLOCK, cell % BLOCK) == inside
    station_w = jnp.zeros((8, LANES), F32)
    for t in range(tiles):
        fold = (member & (at % tiles == t) & (at < 2 * tiles)).astype(BF16)
        station_w = station_w + nn(jnp.broadcast_to(weights[t], (8, cells)).astype(BF16), fold)
    lane = iota((8, LANES), 1)
    row = iota((8, LANES), 0)
    wide = intervals // BLOCK
    slot_at = jnp.where(lane // BLOCK < 2 * tiles, slot_key(lane * wide, pairs, 1, intervals), -2.0)
    owner_at = jnp.where(lane // BLOCK < blocks, (me * blocks + lane // BLOCK).astype(F32), -2.0)
    keys = jnp.where(row == 0, slot_key(lane, pairs, intervals, intervals), 0.0)
    keys = jnp.where(row == 1, owner_key(lane, me, blocks, intervals, -2), keys)
    keys = jnp.where(row == 3, owner_at, keys)
    keys = jnp.where(row == 4, station_w, keys)
    out_ref[GAIN_ROWS:, :] = jnp.where(row == 5, slot_at, keys)
    out_ref[GAIN_ROWS + 2 : GAIN_ROWS + 3, :owned] = penalty_ref[...]
    copies[0].wait()
    place = (iota((BLOCK, owned), 0) == iota((BLOCK, owned), 1) % BLOCK).astype(BF16)
    here = iota((LANES, owned), 0) // intervals == iota((LANES, owned), 1) // BLOCK
    parts = []
    for m in range(8):
        plane = jnp.concatenate([start_ref[m]] * (LANES // intervals), 0)
        parts.append(jnp.where(here, plane, 0.0))
    parts = jnp.concatenate(parts, 0)
    high = parts.astype(BF16)
    low = (parts - high.astype(F32)).astype(BF16)
    turned = nt(place, high) + nt(place, low)
    for m in range(8):
        out_ref[m * BLOCK : (m + 1) * BLOCK, :] = turned[:, m * LANES : (m + 1) * LANES]


def prepare_kernel(
    blocks, intervals, bands, pair_hbm, chan_hbm, flag_hbm, vis_hbm, model_hbm, prod_ref, key_ref,
    at_ref, basis_ref, chans_ref, pair_ref, chan_ref, flag_ref, vis_ref, model_ref, mt_ref, sems
):
    planes, width, cells = vis_ref.shape
    moves = [
        (model_hbm, model_ref),
        (vis_hbm, vis_ref),
        (pair_hbm, pair_ref),
        (chan_hbm, chan_ref),
        (flag_hbm, flag_ref),
    ]
    copies = [
        pltpu.make_async_copy(source, target, sems.at[n])
        for n, (source, target) in enumerate(moves)
    ]
    for copy in copies[:1] + copies[2:]:
        copy.start()
    for copy in copies[2:]:
        copy.wait()
    pairs = scalar_pairs(pair_ref)
    tiles = len(pairs)
    channels = width // tiles
    me = lax.axis_index("base")
    row = iota((2 * LANES, LANES), 0)
    lane = iota((2 * LANES, LANES), 1)
    for ref, scale in ((key_ref, intervals), (at_ref, 1)):
        ref[...] = jnp.where(
            row < LANES,
            slot_key(row, pairs, scale, intervals),
            owner_key(row - LANES, me, blocks, intervals, -1, scale),
        )
    band_at = lax.axis_index("band")
    local = chan_ref[...] - band_at * intervals
    chan = (band_at * channels + iota((1, channels), 1)).astype(F32)
    xpos = -1.0 + (2.0 * chan + 1.0) / (channels * bands)
    member = (iota((2 * LANES, channels), 0) % intervals == local).astype(F32)
    chans = jnp.sum(member, 1, keepdims=True)
    chans_ref[...] = nt(jnp.ones((8, channels), BF16), member.astype(BF16))
    centre = jnp.sum(member * xpos, 1, keepdims=True) / chans
    terms = [jnp.ones((2 * LANES, LANES), F32), jnp.broadcast_to(centre, (2 * LANES, LANES))]
    for order in range(2, NPOLY):
        terms.append(2.0 * terms[1] * terms[-1] - terms[-2])
    basis = jnp.zeros((2 * LANES, LANES), F32)
    for order in range(NPOLY):
        basis = jnp.where(lane % KPAD == order, terms[order], basis)
    basis_ref[...] = jnp.where(row // intervals == lane // KPAD, basis, 0.0)
    lanes = 2 * tiles * intervals
    row = iota((lanes, 2 * width), 0)
    lane = iota((lanes, 2 * width), 1)
    at = jnp.concatenate([local] * (2 * tiles), 1)
    fold = ((row // intervals == lane // channels) & (row % intervals == at)).astype(BF16)
    ident = (iota((cells, cells), 0) == iota((cells, cells), 1)).astype(BF16)
    rows = cell_weights(pairs, flag_ref[...].astype(F32))
    weight = jnp.concatenate([jnp.broadcast_to(w, (channels, cells)) for w in rows], 0)
    half = cells // 2

    def put(at, product):
        beside = jnp.concatenate([product[:half], product[half:]], 1)
        prod_ref[at] = pick(beside, fold).reshape(prod_ref.shape[1:])

    copies[0].wait()
    copies[1].start()
    for m in range(planes):
        masked = (model_ref[m].astype(F32) * weight).astype(BF16)
        mt_ref[m] = nt(ident, masked)
    for x in range(4):
        put(32 + x, mt_ref[x] * mt_ref[x] + mt_ref[4 + x] * mt_ref[4 + x])
    for n, (x, y) in enumerate(CROSS):
        x_re, x_im, y_re, y_im = mt_ref[x], mt_ref[4 + x], mt_ref[y], mt_ref[4 + y]
        put(36 + n, x_re * y_re + x_im * y_im)
        put(42 + n, x_im * y_re - x_re * y_im)
    copies[1].wait()
    for x in range(4):
        v_re, v_im = nt(ident, vis_ref[x]), nt(ident, vis_ref[4 + x])
        for y in range(4):
            m_re, m_im = mt_ref[y], mt_ref[4 + y]
            put(4 * x + y, v_re * m_re + v_im * m_im)
            put(16 + 4 * x + y, v_im * m_re - v_re * m_im)


def tie_kernel(*refs):
    pass


def after(values, others, flops=0):
    place = pl.BlockSpec(memory_space=pl.ANY)
    return pl.pallas_call(
        tie_kernel,
        out_shape=[jax.ShapeDtypeStruct(x.shape, x.dtype) for x in values],
        in_specs=[place] * (len(values) + len(others)),
        out_specs=[place] * len(values),
        input_output_aliases={n: n for n in range(len(values))},
        compiler_params=pltpu.CompilerParams(vmem_limit_bytes=1024 * 1024),
        cost_estimate=pl.CostEstimate(flops=flops, bytes_accessed=0, transcendentals=0),
    )(*values, *others)


def normal_terms(gains, prod_ref, first_s, second_s, a_s, out_ref):
    half = BLOCK // 2
    low = iota((half, LANES), 1) < LANES // 2

    def swap(x):
        return pltpu.roll(x, LANES // 2, 1)

    first, second = [], [[], []]
    for m in range(8):
        part = [gains[m * BLOCK + h * half : m * BLOCK + (h + 1) * half] for h in range(2)]
        first.append(jnp.where(low, part[0], swap(part[1])))
        for h in range(2):
            second[h].append(jnp.where(low, swap(part[h]), part[h]))
    for n, x in enumerate(first + square(first)):
        first_s[n] = x
    for h in range(2):
        for n, x in enumerate(second[h] + square(second[h])):
            second_s[h, n] = x

    def step(i, totals):
        partial = None
        new = []
        one = [first_s[n, pl.ds(i, 1), :] for n in range(12)]
        for h in range(2):
            two = [second_s[h, n] for n in range(12)]

            def load(n):
                return prod_ref[n, i, h * half : (h + 1) * half, :]

            def pairs(r, k, c, n):
                at = (2 * r + k) * 4 + 2 * c + n
                return load(at), load(16 + at)

            def cross(r, k, c, n):
                at = CROSS.index((2 * r + k, 2 * c + n))
                return load(36 + at), load(42 + at)

            own = [[load(32 + 2 * r + k) for k in range(2)] for r in range(2)]
            terms = apply_gains(pairs, two[:8], False) + outer_first(own, cross, two[8:])
            partial = terms if partial is None else [x + y for x, y in zip(partial, terms)]
            terms = apply_gains(pairs, one[:8], True) + outer_second(own, cross, one[8:])
            new += [x + y for x, y in zip(totals[12 * h : 12 * (h + 1)], terms)]
        for k in range(12):
            a_s[k, pl.ds(i, 1), :] = jnp.sum(partial[k], 0, keepdims=True)
        return tuple(new)

    zero = jnp.zeros((half, LANES), F32)
    totals = lax.fori_loop(0, half, step, (zero,) * 24, unroll=4)
    for k in range(12):
        mine = a_s[k]
        for h in range(2):
            other = totals[12 * h + k]
            other = other + swap(other)
            at = k * BLOCK + h * half
            out_ref[at : at + half, :] = jnp.where(low, swap(mine) if h else mine, other)


def key_match(rows, lanes):
    count = lanes.shape[1] // LANES
    return (jnp.concatenate([rows] * count, 1) == lanes).astype(BF16)


def beside(refs, count):
    return jnp.concatenate([p[...] for p in refs[:count]], 1), refs[count:]


def first_kernel(count, *refs):
    every, refs = beside(refs, count)
    key_ref, prod_ref, gains_ref, out_ref = refs[:4]
    scratch = refs[4:]
    select = key_match(key_ref[:LANES, :], every[GAIN_ROWS + 1 : GAIN_ROWS + 2])
    gains = pick(every[:GAIN_ROWS], select)
    gains_ref[...] = gains
    normal_terms(gains, prod_ref, *scratch, out_ref)


def state_kernel(count, blocks, intervals, *refs):
    every, refs = beside(refs, count)
    key_ref, at_ref, gains_ref, chans_ref, basis_ref = refs[:5]
    z_ref, pen_ref, scale_ref, select_ref, turned_ref = refs[5:]
    place = (iota((KPAD, LANES), 0) == iota((KPAD, LANES), 1) % KPAD).astype(BF16)
    for n, piece in enumerate(split(turn(place, basis_ref[LANES:, :]))):
        turned_ref[n * KPAD : (n + 1) * KPAD, :] = piece
    rows = every[GAIN_ROWS:]
    z_ref[:, :LANES] = gains_ref[...]
    z_ref[:, LANES:] = every[:GAIN_ROWS, :LANES]
    select_ref[...] = key_match(key_ref[...], rows[0:1])
    lanes = rows.shape[1]
    diagonal = iota((BLOCK, lanes), 0) == iota((BLOCK, lanes), 1) % BLOCK
    at = at_ref[...]
    pen = pick(jnp.where(diagonal, rows[2:3], 0.0), key_match(at, rows[3:4]))
    unused = iota(pen.shape, 1) >= LANES + blocks * intervals
    pen_ref[...] = jnp.where(unused, 1.0, pen)
    weights = pick(jnp.where(diagonal, rows[4:5], 0.0), key_match(at, rows[5:6]))
    scale_ref[...] = 1.0 / jnp.maximum(weights * chans_ref[0:1, :], 1.0)


def solve(normal, scale, pen, consensus):
    part = [normal[BLOCK * k : BLOCK * (k + 1)] * scale for k in range(12)]
    rhs = [part[m] + pen * consensus[BLOCK * m : BLOCK * (m + 1)] for m in range(8)]
    h_first = part[8] + pen
    h_second = part[9] + pen
    h_real, h_imag = part[10], part[11]
    determ = h_first * h_second - h_real * h_real - h_imag * h_imag
    over = 1.0 / determ
    d_first, d_second = h_first * over, h_second * over
    d_real, d_imag = h_real * over, h_imag * over
    out = [None] * 8
    for r in range(2):
        x_re, y_re = rhs[2 * r], rhs[2 * r + 1]
        x_im, y_im = rhs[4 + 2 * r], rhs[5 + 2 * r]
        out[2 * r] = x_re * d_second - (y_re * d_real + y_im * d_imag)
        out[4 + 2 * r] = x_im * d_second - (y_im * d_real - y_re * d_imag)
        out[2 * r + 1] = y_re * d_first - (x_re * d_real - x_im * d_imag)
        out[5 + 2 * r] = y_im * d_first - (x_im * d_real + x_re * d_imag)
    return jnp.concatenate(out, 0)


def step_kernel(count, *refs):
    every, refs = beside(refs, count)
    select_ref, z_ref, pen_ref, scale_ref, prod_ref, gains_ref, out_ref = refs[:7]
    scratch = refs[7:]
    normal = pick(every, select_ref[...])
    gains = solve(normal, scale_ref[...], pen_ref[...], z_ref[...])
    gains_ref[...] = gains
    normal_terms(gains[:, :LANES], prod_ref, *scratch, out_ref)


def first_total_kernel(gains_ref, basis_ref, out_ref):
    basis = basis_ref[...]
    total = nn(gains_ref[...], basis, precision=HIGH)
    part = basis[: basis.shape[0] // 8]
    gram = lax.dot_general(
        part, part, (((0,), (0,)), ((), ())), preferred_element_type=F32, precision=HIGH
    )
    out_ref[:GAIN_ROWS, :] = total
    out_ref[GAIN_ROWS:, :] = gram[:KPAD]


def total_kernel(gains_ref, dual_ref, basis_ref, out_ref):
    out_ref[...] = nn(gains_ref[...] + dual_ref[...], basis_ref[...], precision=HIGH)


def inverse_of_three(d):
    def minor(r, c):
        (r0, r1), (c0, c1) = [[k for k in range(3) if k != n] for n in (r, c)]
        value = d[r0][c0] * d[r1][c1] - d[r0][c1] * d[r1][c0]
        return value if (r + c) % 2 == 0 else -value

    minors = [[minor(r, c) for c in range(3)] for r in range(3)]
    over = 1.0 / (d[0][0] * minors[0][0] + d[0][1] * minors[0][1] + d[0][2] * minors[0][2])
    return [[minors[c][r] * over for c in range(3)] for r in range(3)]


def invert(gram):
    row, lane = iota(gram.shape, 0), iota(gram.shape, 1)
    inner = (row < NPOLY) & (lane < NPOLY)
    work = jnp.where(inner, gram + jnp.where(row == lane, ridge, 0.0), 0.0)
    lanes = iota((1, gram.shape[1]), 1)
    for p in range(0, NPOLY, 3):
        rows = [work[p + a : p + a + 1] for a in range(3)]
        block = inverse_of_three(
            [
                [jnp.broadcast_to(rows[a][:, p + b : p + b + 1], lanes.shape) for b in range(3)]
                for a in range(3)
            ]
        )
        columns = [work[:, p + b : p + b + 1] for b in range(3)]
        here = (lane >= p) & (lane < p + 3)
        rows = [jnp.where(here[:1], 0.0, x) for x in rows]
        pivots = []
        for a in range(3):
            pivot = block[a][0] * rows[0] + block[a][1] * rows[1] + block[a][2] * rows[2]
            for b in range(3):
                pivot = jnp.where(lanes == p + b, block[a][b], pivot)
            pivots.append(pivot)
        work = jnp.where(here, 0.0, work)
        for b in range(3):
            work = work - columns[b] * pivots[b]
        for a in range(3):
            work = jnp.where(row == p + a, pivots[a], work)
    return work


def settle(total, inverse, basis_ref, gains, z_ref, dual_ref):
    coeff = nn(total, inverse, precision=HIGH)
    consensus = nt(coeff, basis_ref[...], precision=HIGH)
    z_ref[...] = 2.0 * consensus - gains
    dual_ref[...] = gains - consensus


def band_total(refs):
    totals = [ref[...] for ref in refs]
    while len(totals) > 1:
        totals = [totals[n] + totals[n + 1] for n in range(0, len(totals), 2)]
    return totals[0]


def first_consensus_kernel(
    one_ref, two_ref, gains_ref, basis_ref, z_ref, dual_ref, inverse_ref
):
    total = one_ref[...] + two_ref[...]
    small = invert(total[GAIN_ROWS:])
    row, lane = iota((LANES, LANES), 0), iota((LANES, LANES), 1)
    spread = ((row == lane % KPAD) & (row < KPAD)).astype(F32)
    wide = nn(jnp.concatenate([small] * (LANES // KPAD), 0), spread, precision=HIGH)
    inverse = jnp.where(row // KPAD == lane // KPAD, wide, 0.0)
    inverse_ref[...] = inverse
    settle(total[:GAIN_ROWS], inverse, basis_ref, gains_ref[...], z_ref, dual_ref)


def consensus_kernel(
    one_ref, two_ref, gains_ref, old_ref, basis_ref, inverse_ref, z_ref, dual_ref
):
    total = one_ref[...] + two_ref[...]
    gains = gains_ref[...] + old_ref[...]
    settle(total, inverse_ref[...], basis_ref, gains, z_ref, dual_ref)


def last_kernel(count, blocks, intervals, *refs):
    every, refs = beside(refs, count)
    select_ref, z_ref, pen_ref, scale_ref, dual_ref, turned_ref, gains_ref, out_ref = refs
    own = slice(LANES, 2 * LANES)
    normal = pick(every, select_ref[own, :])
    gains = solve(normal, scale_ref[:, own], pen_ref[:, own], z_ref[:, own])
    gains_ref[...] = gains
    owned = blocks * BLOCK
    here = iota((owned, LANES), 0) // BLOCK == iota((owned, LANES), 1) // intervals
    summed = gains + dual_ref[:, own]
    parts = [summed[m * BLOCK : (m + 1) * BLOCK] for m in range(8)]
    parts = [jnp.where(here, jnp.concatenate([x] * blocks, 0), 0.0) for x in parts]
    high, mid, low = split(jnp.concatenate(parts, 0))
    turned = turned_ref[...]
    first, second = nt(turned, high), nt(turned[: 2 * KPAD], mid)
    small = first[2 * KPAD :] + second[KPAD:] + nt(turned[:KPAD], low)
    total = first[:KPAD] + ((first[KPAD : 2 * KPAD] + second[:KPAD]) + small)
    chunks = total.shape[1] // LANES
    for c in range(chunks):
        lanes = slice(c * LANES, (c + 1) * LANES)
        out_ref[8 * c : 8 * c + 8, :] = total[:8, lanes]
        out_ref[8 * chunks + c : 8 * chunks + c + 1, :] = total[8:9, lanes]
    rest = 9 * chunks
    out_ref[rest:, :] = jnp.zeros((out_ref.shape[0] - rest, LANES), F32)


def gains_kernel(blocks, intervals, gains_ref, out_ref):
    owned = blocks * BLOCK
    place = (iota((intervals, LANES), 0) == iota((intervals, LANES), 1) % intervals).astype(BF16)
    here = iota((owned, LANES), 0) // BLOCK == iota((owned, LANES), 1) // intervals
    for m in range(8):
        part = gains_ref[m * BLOCK : (m + 1) * BLOCK, :]
        out_ref[m] = turn(place, jnp.where(here, jnp.concatenate([part] * blocks, 0), 0.0))


def split(values):
    high = values.astype(BF16)
    rest = values - high.astype(F32)
    mid = rest.astype(BF16)
    return high, mid, (rest - mid.astype(F32)).astype(BF16)


def turn(place, values):
    high, mid, low = split(values)
    return (nt(place, high) + nt(place, mid)) + nt(place, low)


def coefficient_kernel(bands, *refs):
    inverse_ref, out_ref = refs[bands:]
    total = band_total(refs[:bands])
    owned = out_ref.shape[2]
    chunks = 8 * owned // LANES
    inverse = inverse_ref[:KPAD, :KPAD]
    eight = jnp.concatenate([total[8 * c : 8 * c + 8] for c in range(chunks)], 1)
    ninth = jnp.concatenate([total[8 * chunks + c : 8 * chunks + c + 1] for c in range(chunks)], 1)
    coeff = nn(inverse[:, :8], eight, precision=HIGH) + inverse[:, 8:9] * ninth
    for m in range(8):
        out_ref[:, m, :] = coeff[:NPOLY, m * owned : (m + 1) * owned]


def call(kernel, operands, shapes, scratch=(), hbm=False, flops=20_000_000):
    vmem = pl.BlockSpec(memory_space=pltpu.VMEM)
    in_specs = [vmem] * len(operands)
    moved = sum(x.size * x.dtype.itemsize for x in (*operands, *shapes))
    if hbm:
        in_specs = [pl.BlockSpec(memory_space=pltpu.HBM)] * len(operands)
        operands = [pltpu.with_memory_space_constraint(x, pltpu.HBM) for x in operands]
    return pl.pallas_call(
        kernel,
        out_shape=shapes,
        in_specs=in_specs,
        out_specs=[vmem] * len(shapes),
        scratch_shapes=list(scratch),
        compiler_params=pltpu.CompilerParams(vmem_limit_bytes=14 * 1024 * 1024),
        cost_estimate=pl.CostEstimate(flops=flops, bytes_accessed=moved, transcendentals=0),
    )(*operands)


def share_base(x, last=(), ties=(2,), ahead=False):
    devices = lax.axis_size("base")
    mine = [x] + [
        lax.ppermute(x, "base", [(d, d ^ (2 * k)) for d in range(devices)])
        for k in range(1, devices // 2)
    ]
    if ahead:
        mine[3:] = after(mine[3:], (), flops=5_000_000_000)
    if last:
        for k, y in zip(ties, after([mine[k] for k in ties], last)):
            mine[k] = y
    other = [lax.ppermute(y, "base", [(d, d ^ 1) for d in range(devices)]) for y in mine]
    return mine + other


def share_band(x):
    devices = lax.axis_size("band")
    return [x] + [
        lax.ppermute(x, "band", [(d, d ^ k) for d in range(devices)]) for k in range(1, devices)
    ]


def sum_band(x):
    devices = lax.axis_size("band")
    step = 1
    while 2 * step < devices:
        x = x + lax.ppermute(x, "band", [(d, d ^ step) for d in range(devices)])
        step = 2 * step
    return x, lax.ppermute(x, "band", [(d, d ^ step) for d in range(devices)])


def on_device(visibilities, model, start_gains, penalty, pairs, flags, chan_band):
    tiles, channels, cells = visibilities.shape[1:]
    intervals = start_gains.shape[1]
    owned = start_gains.shape[2]
    blocks = owned // BLOCK
    count = lax.axis_size("base")
    bands = lax.axis_size("band")
    width = tiles * channels

    def shape(*extent, dtype=F32):
        return jax.ShapeDtypeStruct(extent, dtype)

    wide = shape(GAIN_ROWS, 2 * LANES)
    narrow = shape(GAIN_ROWS, LANES)
    single = shape(BLOCK, 2 * LANES)
    terms = shape(TERM_ROWS, LANES)
    square = shape(2 * LANES, LANES)

    (greeting,) = call(
        functools.partial(greet_kernel, blocks, intervals),
        (pairs, start_gains, penalty.reshape(1, owned), flags),
        [shape(GAIN_ROWS + 8, LANES)],
        [
            pltpu.SMEM(pairs.shape, jnp.int32),
            pltpu.VMEM(start_gains.shape, F32),
            pltpu.VMEM((1, owned), F32),
            pltpu.VMEM(flags.shape, jnp.int32),
            pltpu.SemaphoreType.DMA((4,)),
        ],
        hbm=True,
    )
    products, keys, at, basis, chans = call(
        functools.partial(prepare_kernel, blocks, intervals, bands),
        (
            pairs,
            chan_band.reshape(1, channels),
            flags,
            visibilities.reshape(8, width, cells),
            model.reshape(8, width, cells),
        ),
        [
            shape(PRODUCTS, BLOCK // 2, BLOCK, 2 * tiles * intervals),
            square,
            square,
            square,
            shape(8, 2 * LANES),
        ],
        [
            pltpu.SMEM(pairs.shape, jnp.int32),
            pltpu.VMEM((1, channels), jnp.int32),
            pltpu.VMEM(flags.shape, jnp.int32),
            *[pltpu.VMEM((8, width, cells), BF16)] * 2,
            pltpu.VMEM((8, cells, width), F32),
            pltpu.SemaphoreType.DMA((5,)),
        ],
        hbm=True,
        flops=2_000_000_000,
    )
    greetings = share_base(greeting, last=(chans,), ties=(1, 2))
    scratch = [
        pltpu.VMEM((12, BLOCK // 2, LANES), F32),
        pltpu.VMEM((2, 12, BLOCK // 2, LANES), F32),
        pltpu.VMEM((12, BLOCK // 2, LANES), F32),
    ]

    gains, message = call(
        functools.partial(first_kernel, count),
        (*greetings, keys, products),
        [narrow, terms],
        scratch,
    )
    z, pen, scale, select, turned = call(
        functools.partial(state_kernel, count, blocks, intervals),
        (*greetings, keys, at, gains, chans, basis),
        [
            wide,
            single,
            single,
            shape(2 * LANES, count * LANES, dtype=BF16),
            shape(3 * KPAD, LANES, dtype=BF16),
        ],
    )
    pieces = share_base(message, last=(scale,), ties=(1,))
    gains, message = call(
        functools.partial(step_kernel, count),
        (*pieces, select, z, pen, scale, products),
        [wide, terms],
        scratch,
    )
    (part,) = call(first_total_kernel, (gains, basis), [shape(GAIN_ROWS + KPAD, LANES)])
    z, dual, inverse = call(
        first_consensus_kernel, (*sum_band(part), gains, basis), [wide, wide, narrow]
    )
    pieces = share_base(message, last=(z,), ties=(2,), ahead=True)
    gains, message = call(
        functools.partial(step_kernel, count),
        (*pieces, select, z, pen, scale, products),
        [wide, terms],
        scratch,
    )
    (part,) = call(total_kernel, (gains, dual, basis), [narrow])
    z, dual = call(consensus_kernel, (*sum_band(part), gains, dual, basis, inverse), [wide, wide])
    pieces = share_base(message, last=(z,), ties=(2,), ahead=True)
    chunks = 8 * owned // LANES
    gains, part = call(
        functools.partial(last_kernel, count, blocks, intervals),
        (*pieces, select, z, pen, scale, dual, turned),
        [narrow, shape(8 * chunks + -(-chunks // 8) * 8, LANES)],
    )
    parts = share_band(part)
    (out,) = call(
        functools.partial(gains_kernel, blocks, intervals),
        (gains,),
        [shape(8, intervals, owned)],
    )
    (coefficients,) = call(
        functools.partial(coefficient_kernel, bands),
        (*parts, inverse),
        [shape(NPOLY, 8, owned)],
    )
    return (out, jnp.transpose(coefficients, (1, 0, 2)))


def solution(mesh):
    in_specs = (
        P(None, "base", "band", None),
        P(None, "base", "band", None),
        P(None, "band", "base"),
        P("base"),
        P("base", None),
        P("base", None),
        P("band"),
    )
    out_specs = (P(None, "band", "base"), P(None, None, "base"))
    return jax.shard_map(
        on_device, mesh=mesh, in_specs=in_specs, out_specs=out_specs, check_vma=False
    )
```
